128 devices in a mesh: seq: 8 (over z, x_lo), user: 16 (over y, x_hi, core).
Axes of the slice: x: 4 (x_hi: 2, x_lo: 2; x = x_hi * 2 + x_lo), y: 4, z: 4, core: 2. Of those that a mesh axis runs over, the one named last changes fastest.
Arguments:
- history: bfloat16 [16, 2048, 1024], P('user', 'seq'), may hold values from -6 to 6
- segment_ids: int32 [16, 2048], P('user', 'seq'), may hold values from 0 to 3, as said below
- w_in: bfloat16 [1024, 4096], replicated, may hold values from -0.1875 to 0.1875
- w_out: bfloat16 [1024, 1024], replicated, may hold values from -0.1875 to 0.1875
- cotangent: bfloat16 [16, 2048, 1024], P('user', 'seq'), may hold values from -6 to 6
Outputs:
- layer_out: bfloat16 [16, 2048, 1024], P('user', 'seq')
- grad_history: bfloat16 [16, 2048, 1024], P('user', 'seq')
- grad_w_in: float32 [1024, 4096], P(('seq', 'user'))
- grad_w_out: float32 [1024, 1024], P(('seq', 'user'))
The draws below stay inside these ranges and needn't reach their ends.
Inputs may be any that keep to these rules, and one draw needn't show every extreme that they name: `segment_ids`: in each group the ids never fall along places (time order); each user has 1 to 1536 events and one has exactly 1536.
All inputs are finite; a program needn't handle non-finite values.
Results may differ from the reference program's by a relative error of at most 0.0083.
Values may be sent and summed in bfloat16 or wider, within the bound.
No kernel may reach another device: no remote copies, remote signals or barrier semaphores. Data moves between devices by JAX's collectives and lax.ppermute only.
A program may use at most 192 MiB of HBM per device.

```python
import jax
import jax.numpy as jnp
from jax import lax

D = 1024
H = 8
TOK_DEV = 256
USERS = 4
LEN = 2048
MOST = 1536
GROUPS = 16
TOKENS = 32768
N_SEQ = 8


def group_segments(key):
    rest = LEN - MOST
    cut_key, place_key = jax.random.split(key)
    cuts = jnp.sort(jax.random.choice(cut_key, rest - 1, (USERS - 2,), replace=False) + 1).astype(jnp.int32)
    bounds = jnp.concatenate([jnp.zeros((1,), jnp.int32), cuts, jnp.full((1,), rest, jnp.int32)])
    others = bounds[1:] - bounds[:-1]
    longest_at = jax.random.randint(place_key, (), 0, USERS)
    index = jnp.arange(USERS, dtype=jnp.int32)
    other_index = jnp.clip(index - (index > longest_at).astype(jnp.int32), 0, USERS - 2)
    lengths = jnp.where(index == longest_at, MOST, others[other_index]).astype(jnp.int32)
    ends = jnp.cumsum(lengths)[:-1]
    times = jnp.arange(LEN, dtype=jnp.int32)
    in_time = jnp.sum((times[:, None] >= ends[None, :]).astype(jnp.int32), axis=1)
    stored = jnp.arange(LEN, dtype=jnp.int32)
    shard = stored // TOK_DEV
    within = stored % TOK_DEV
    half = TOK_DEV // 2
    shard_count = LEN // TOK_DEV
    places = jnp.where(within < half, shard * half + within, (2 * shard_count - 1 - shard) * half + within - half)
    return in_time[places].astype(jnp.int32)


def draw_segment_ids(key, part):
    key = jax.random.fold_in(key, 11)
    group_keys = jax.random.split(key, GROUPS)
    return jax.vmap(group_segments)(group_keys)


def level_of(stream_key, dims, cuts, least, largest):
    def one(dim, parts):
        draws = jax.random.uniform(jax.random.fold_in(jax.random.fold_in(stream_key, 6), dim), (parts,), jnp.float32, least / len(cuts), largest / len(cuts))
        return jnp.repeat(jnp.exp(draws), dims[dim] // parts).reshape((-1,) + (1,) * (len(dims) - dim - 1))

    level = one(*cuts[0])
    for cut in cuts[1:]:
        level = level * one(*cut)
    return level


def noise(rng, extent, spread, most, pieces=(), kind=jnp.bfloat16):
    gain = level_of(rng, extent, pieces, -0.22, 0.18) if pieces else 1.0
    values = jax.random.normal(rng, extent, jnp.float32) * spread * gain
    return jnp.minimum(jnp.maximum(values, -most), most).astype(kind)


def setup_inputs(seed: int = 0) -> dict:
    key_list = jax.random.split(jax.random.key(seed), 6)
    history = noise(key_list[0], (GROUPS, LEN, D), 1.0, 6.0, ((0, 16), (1, 8)))
    segment_ids = draw_segment_ids(jax.random.fold_in(key_list[5], 71), 0)
    w_in = noise(key_list[2], (D, 4 * D), D ** -0.5, 0.1875)
    w_out = noise(key_list[3], (D, D), D ** -0.5, 0.1875)
    cotangent = noise(key_list[4], (GROUPS, LEN, D), 1.0, 6.0, ((0, 16), (1, 8)))
    return dict(history=history, segment_ids=segment_ids, w_in=w_in, w_out=w_out, cotangent=cotangent)


epsilon = 1e-05

def time_places(stored, shard_rows, shard_count):
    shard = stored // shard_rows
    within = stored % shard_rows
    half = shard_rows // 2
    return jnp.where(within < half, shard * half + within, (2 * shard_count - 1 - shard) * half + within - half).astype(jnp.int32)

def layer_norm(entries):
    centre = lax.optimization_barrier(jnp.mean(entries, axis=-1, keepdims=True))
    centred = entries - centre
    inverse = lax.rsqrt(lax.optimization_barrier(jnp.mean(centred * centred, axis=-1, keepdims=True)) + epsilon)
    return (centred * inverse, inverse)

def norm_back(normed, inverse, upstream):
    first_term = lax.optimization_barrier(jnp.mean(upstream, axis=-1, keepdims=True))
    second_term = lax.optimization_barrier(jnp.mean(upstream * normed, axis=-1, keepdims=True))
    return inverse * (upstream - first_term - normed * second_term)

def silu_slope(entries):
    sigmoid = jax.nn.sigmoid(entries)
    return sigmoid * (1.0 + entries * (1.0 - sigmoid))

def one_group(history, segments, cotangent, w_in, w_out):
    length = history.shape[0]
    head_size = D // H
    key_scale = head_size ** (-0.5)
    history_f = history.astype(jnp.float32)
    normed, inverse = layer_norm(history_f)
    normed_b = normed.astype(jnp.bfloat16)
    projected = jnp.dot(normed_b, w_in, preferred_element_type=jnp.float32)
    activated = jax.nn.silu(projected).astype(jnp.bfloat16)
    gate_u = activated[:, :D]
    values = activated[:, D:2 * D]
    queries = activated[:, 2 * D:3 * D]
    keys_all = activated[:, 3 * D:]
    value_heads = values.astype(jnp.float32).reshape(length, H, head_size)
    query_heads = queries.astype(jnp.float32).reshape(length, H, head_size)
    key_heads = keys_all.astype(jnp.float32).reshape(length, H, head_size)
    places = time_places(jnp.arange(length, dtype=jnp.int32), TOK_DEV, N_SEQ)
    visible = (segments[:, None] == segments[None, :]) & (places[None, :] <= places[:, None])
    scores = jnp.einsum('qhd,khd->hqk', query_heads, key_heads) * key_scale
    weights = jnp.where(visible, jax.nn.silu(scores), 0.0).astype(jnp.bfloat16)
    weights_f = weights.astype(jnp.float32)
    attended = jnp.einsum('hqk,khd->qhd', weights_f, value_heads).reshape(length, D)
    mixed, mix_inverse = layer_norm(attended)
    gated = (mixed * gate_u.astype(jnp.float32)).astype(jnp.bfloat16)
    layer_out = (history_f + jnp.dot(gated, w_out, preferred_element_type=jnp.float32)).astype(jnp.bfloat16)
    grad_gated = jnp.dot(cotangent, w_out.T, preferred_element_type=jnp.float32)
    grad_u = grad_gated * mixed
    grad_att = norm_back(mixed, mix_inverse, grad_gated * gate_u.astype(jnp.float32)).astype(jnp.bfloat16)
    grad_heads = grad_att.astype(jnp.float32).reshape(length, H, head_size)
    slopes_raw = jnp.einsum('qhd,khd->hqk', grad_heads, value_heads)
    slopes = jnp.where(visible, slopes_raw * silu_slope(scores), 0.0).astype(jnp.bfloat16)
    slopes_f = slopes.astype(jnp.float32)
    grad_values = jnp.einsum('hqk,qhd->khd', weights_f, grad_heads).reshape(length, D)
    grad_queries = key_scale * jnp.einsum('hqk,khd->qhd', slopes_f, key_heads).reshape(length, D)
    grad_keys = key_scale * jnp.einsum('hqk,qhd->khd', slopes_f, query_heads).reshape(length, D)
    grad_proj = (jnp.concatenate([grad_u, grad_values, grad_queries, grad_keys], axis=1) * silu_slope(projected)).astype(jnp.bfloat16)
    part_in = jnp.dot(normed_b.T, grad_proj, preferred_element_type=jnp.float32)
    part_out = jnp.dot(gated.T, cotangent, preferred_element_type=jnp.float32)
    grad_normed = jnp.dot(grad_proj, w_in.T, preferred_element_type=jnp.float32)
    grad_history = (cotangent.astype(jnp.float32) + norm_back(normed, inverse, grad_normed)).astype(jnp.bfloat16)
    return (layer_out, grad_history, part_in, part_out)

def reference(history, segment_ids, w_in, w_out, cotangent):

    def group_step(running, group_data):
        history_row, segment_row, cotangent_row = group_data
        layer_out, grad_history, part_in, part_out = one_group(history_row, segment_row, cotangent_row, w_in, w_out)
        return ((running[0] + part_in, running[1] + part_out), (layer_out, grad_history))
    zeros_in = jnp.zeros((D, 4 * D), jnp.float32)
    zeros_out = jnp.zeros((D, D), jnp.float32)
    sums, stacked = lax.scan(group_step, (zeros_in, zeros_out), (history, segment_ids, cotangent))
    factor = TOKENS ** (-0.5)
    return (stacked[0], stacked[1], sums[0] * factor, sums[1] * factor)
```

```python
import jax
import jax.numpy as jnp
from jax import lax
from jax.sharding import PartitionSpec as P

F32 = jnp.float32
BF16 = jnp.bfloat16
EPS = 1e-05
H = 8
HD = 128
NZ, NX = 4, 2
NY, NXH, NC = 4, 2, 2


def seq_perm(dz, dx):
    return [
        (((z + dz) % NZ) * NX + (x ^ dx), z * NX + x) for z in range(NZ) for x in range(NX)
    ]


def user_perm(dy, dh, dc):
    return [
        ((((y + dy) % NY) * NXH + (h ^ dh)) * NC + (c ^ dc), (y * NXH + h) * NC + c)
        for y in range(NY)
        for h in range(NXH)
        for c in range(NC)
    ]


def from_seq(a, dz, dx):
    return lax.ppermute(a, "seq", seq_perm(dz, dx))


def from_user(a, dy, dh, dc):
    return lax.ppermute(a, "user", user_perm(dy, dh, dc))


def from_both(a, dh, dx):
    pairs = []
    for s in range(NZ * NX):
        for u in range(NY * NXH * NC):
            pairs.append(((s ^ dx) * NY * NXH * NC + (u ^ (dh * NC)), s * NY * NXH * NC + u))
    return lax.ppermute(a, ("seq", "user"), pairs)


def gather_seq(block, x_rows=(96, 176)):
    got = {(0, 0): block}
    got[1, 0] = from_seq(block, 1, 0)
    got[3, 0] = from_seq(block, 3, 0)
    got[0, 1] = from_seq(block, 0, 1)
    got[2, 0] = from_seq(got[1, 0], 1, 0)
    got[3, 1] = from_seq(got[0, 1], 3, 0)
    got[1, 1] = from_seq(got[1, 0], 0, 1)
    a, b = x_rows
    got[2, 1] = jnp.concatenate(
        [
            from_seq(got[2, 0][:a], 0, 1),
            from_seq(got[1, 1][a:b], 1, 0),
            from_seq(got[3, 1][b:], 3, 0),
        ],
        axis=0,
    )
    return got


def assemble(got, z, x):
    rows, width = got[0, 0].shape
    whole = jnp.zeros((NZ * NX * rows, width), got[0, 0].dtype)
    for (dz, dx), block in got.items():
        at = (((z + dz) % NZ) * NX + (x ^ dx)) * rows
        whole = lax.dynamic_update_slice(whole, block, (at, 0))
    return whole


def layer_norm(entries):
    centre = jnp.mean(entries, axis=-1, keepdims=True)
    centred = entries - centre
    inverse = lax.rsqrt(jnp.mean(centred * centred, axis=-1, keepdims=True) + EPS)
    return centred * inverse, inverse


def norm_back(normed, inverse, upstream):
    first_term = jnp.mean(upstream, axis=-1, keepdims=True)
    second_term = jnp.mean(upstream * normed, axis=-1, keepdims=True)
    return inverse * (upstream - first_term - normed * second_term)


def silu_slope(entries):
    sigmoid = jax.nn.sigmoid(entries)
    return sigmoid * (1.0 + entries * (1.0 - sigmoid))


def dot(a, b):
    return jnp.dot(a, b, preferred_element_type=F32)


def dot_nt(a, b):
    return lax.dot_general(a, b, (((1,), (1,)), ((), ())), preferred_element_type=F32)


def dot_tn(a, b):
    return lax.dot_general(a, b, (((0,), (0,)), ((), ())), preferred_element_type=F32)


def local(history, segment_ids, w_in, w_out, cotangent):
    hist = history[0]
    cot = cotangent[0]
    rows, width = hist.shape
    length = rows * NZ * NX
    s = lax.axis_index("seq")
    u = lax.axis_index("user")
    z, x = s // NX, s % NX
    y, xh, core = u // (NXH * NC), (u // NC) % NXH, u % NC
    scale = HD ** (-0.5)

    hist_got = gather_seq(hist)
    grad_gated_own = dot_nt(cot, w_out).astype(BF16)
    ids = segment_ids[0].astype(BF16).reshape(2, HD)
    ids = jnp.pad(ids, ((0, 14), (0, 0)))
    to_heads = jnp.concatenate(
        [
            grad_gated_own.reshape(rows, H, HD).transpose(1, 0, 2),
            jnp.broadcast_to(ids[None], (H, 16, HD)),
        ],
        axis=1,
    )
    at_head = lax.all_to_all(to_heads, "seq", 0, 0, tiled=True)
    grad_gated = at_head[:, :rows].reshape(length, HD).astype(F32)
    segments = at_head[:, rows : rows + 2].reshape(length).astype(jnp.int32)
    cot_got = gather_seq(cot)

    hist_all = assemble(hist_got, z, x)
    normed_all, _ = layer_norm(hist_all.astype(F32))
    normed_b = normed_all.astype(BF16)
    w_head = lax.dynamic_slice(w_in.reshape(width, 4, H, HD), (0, 0, s, 0), (width, 4, 1, HD))
    w_head = w_head.reshape(width, 4 * HD)
    projected = dot(normed_b, w_head)
    activated = jax.nn.silu(projected).astype(BF16)
    gate_u, values, queries, keys = (activated[:, i * HD : (i + 1) * HD] for i in range(4))

    stored = jnp.arange(length, dtype=jnp.int32)
    half = rows // 2
    shard, within = stored // rows, stored % rows
    places = jnp.where(
        within < half, shard * half + within, (2 * NZ * NX - 1 - shard) * half + within - half
    )
    visible = (segments[:, None] == segments[None, :]) & (places[None, :] <= places[:, None])
    scores = dot_nt(queries, keys) * scale
    weights = jnp.where(visible, jax.nn.silu(scores), 0.0).astype(BF16)
    attended = dot(weights, values)

    gate_f = gate_u.astype(F32)
    grad_mixed = grad_gated * gate_f
    mean_h = jnp.mean(attended, axis=1)
    centred_h = attended - mean_h[:, None]
    stats = jnp.stack(
        [
            mean_h,
            jnp.sum(centred_h * centred_h, axis=1),
            jnp.sum(grad_mixed, axis=1),
            jnp.sum(grad_mixed * centred_h, axis=1),
        ]
    )
    pair = jnp.stack([stats, from_seq(stats, 0, 1)])
    stats = jnp.concatenate([pair] + [from_seq(pair, dz, 0) for dz in (1, 3, 2)])
    mean_row = jnp.mean(stats[:, 0], axis=0)
    apart = stats[:, 0] - mean_row
    variance = (jnp.sum(stats[:, 1], axis=0) + HD * jnp.sum(apart * apart, axis=0)) / width
    inverse = lax.rsqrt(variance + EPS)
    first = jnp.sum(stats[:, 2], axis=0) / width
    second = inverse * jnp.sum(stats[:, 3] + apart * stats[:, 2], axis=0) / width
    mixed = (attended - mean_row[:, None]) * inverse[:, None]
    gated = (mixed * gate_f).astype(BF16)
    grad_u = grad_gated * mixed
    grad_att = (
        inverse[:, None] * (grad_mixed - first[:, None] - mixed * second[:, None])
    ).astype(BF16)

    slopes = jnp.where(visible, dot_nt(grad_att, values) * silu_slope(scores), 0.0).astype(BF16)
    grad_values = dot_tn(weights, grad_att)
    grad_queries = dot(slopes, keys) * scale
    grad_keys = dot_tn(slopes, queries) * scale
    grad_proj = (
        jnp.concatenate([grad_u, grad_values, grad_queries, grad_keys], axis=1)
        * silu_slope(projected)
    ).astype(BF16)

    back = jnp.concatenate([grad_proj, gated], axis=1).reshape(H, rows, 5 * HD)
    back = lax.all_to_all(back, "seq", 0, 0, tiled=True)

    part_in = dot_tn(normed_b, grad_proj)
    cot_all = assemble(cot_got, z, x)
    part_out = dot_tn(gated, cot_all)
    users = NY * NXH * NC
    n_in = width // (users * H)
    terms_in = part_in.reshape(H, users, n_in, 4 * HD).transpose(1, 0, 2, 3)
    terms_in = terms_in.reshape(users, H * n_in, 4 * HD)
    terms_out = part_out.reshape(users, -1, 4 * HD)
    terms = jnp.concatenate([terms_in, terms_out], axis=1)
    n_rows = terms.shape[1]
    terms = terms.reshape(NY * NXH, NC, n_rows, 4 * HD)

    def pick(a, at, axis):
        return lax.dynamic_index_in_dim(a, at, axis, keepdims=False)

    terms = pick(terms, core, 1) + from_user(pick(terms, 1 - core, 1), 0, 0, 1)
    terms = terms.reshape(NY, NXH, n_rows, 4 * HD)
    total = pick(terms, y, 0)
    for d in (1, 3, 2):
        sent = pick(terms, (y - d) % NY, 0).astype(BF16)
        total = total + from_user(sent, d, 0, 0).astype(F32)
    rows_in = total[:, : H * n_in].reshape(NXH, NZ, NX, n_in, 4 * HD)
    rows_out = total[:, H * n_in :]

    def slab(h, l):
        return pick(pick(rows_in, h, 0), l, 1).reshape(NZ * n_in, 4 * HD)

    same = jnp.concatenate([slab(1 - xh, x), pick(rows_out, 1 - xh, 0)])
    same = from_both(same, 1, 0)
    own_in = slab(xh, x) + same[: NZ * n_in]
    own_out = pick(rows_out, xh, 0) + same[NZ * n_in :]
    other_in = from_both(slab(xh, 1 - x), 0, 1) + from_both(slab(1 - xh, 1 - x), 1, 1)
    columns = jnp.where(
        x == 0, jnp.stack([own_in, other_in]), jnp.stack([other_in, own_in])
    ).reshape(NX, NZ, n_in, 4 * HD)
    whole = jnp.zeros((NZ, NX, n_in, 4 * HD), F32)
    whole = lax.dynamic_update_slice(whole, pick(columns, z, 1)[None], (z, 0, 0, 0))
    for d in (1, 3, 2):
        got = from_seq(pick(columns, (z - d) % NZ, 1), d, 0)
        whole = lax.dynamic_update_slice(whole, got[None], ((z + d) % NZ, 0, 0, 0))
    factor = (length * users) ** (-0.5)
    grad_w_in = whole.reshape(H, n_in, 4, HD).transpose(1, 2, 0, 3).reshape(n_in, 4 * width)
    grad_w_out = own_out.reshape(-1, width)

    hist_f = hist.astype(F32)
    normed, inverse = layer_norm(hist_f)
    proj_tok = back[:, :, : 4 * HD].reshape(H, rows, 4, HD).transpose(1, 2, 0, 3)
    grad_normed = dot_nt(proj_tok.reshape(rows, 4 * width), w_in)
    gated_tok = back[:, :, 4 * HD :].transpose(1, 0, 2).reshape(rows, width)
    layer_out = (hist_f + dot(gated_tok, w_out)).astype(BF16)
    grad_history = (cot.astype(F32) + norm_back(normed, inverse, grad_normed)).astype(BF16)
    return layer_out[None], grad_history[None], grad_w_in * factor, grad_w_out * factor


def solution(mesh):
    in_specs = (P("user", "seq", None), P("user", "seq"), P(), P(), P("user", "seq", None))
    out_specs = (
        P("user", "seq", None),
        P("user", "seq", None),
        P(("seq", "user"), None),
        P(("seq", "user"), None),
    )
    return jax.shard_map(local, mesh=mesh, in_specs=in_specs, out_specs=out_specs, check_vma=False)
```

```python
import jax
import jax.numpy as jnp
from jax import lax
from jax.experimental import pallas as pl
from jax.experimental.pallas import tpu as pltpu
from jax.sharding import PartitionSpec as P

F32 = jnp.float32
BF16 = jnp.bfloat16
EPS = 1e-05
H = 8
HD = 128
NZ, NX = 4, 2
NY, NXH, NC = 4, 2, 2
ORDER = ((0, 0), (1, 0), (3, 0), (0, 1), (2, 0), (3, 1), (1, 1), (2, 1))


def seq_perm(dz, dx):
    return [
        (((z + dz) % NZ) * NX + (x ^ dx), z * NX + x) for z in range(NZ) for x in range(NX)
    ]


def user_perm(dy, dh, dc):
    return [
        ((((y + dy) % NY) * NXH + (h ^ dh)) * NC + (c ^ dc), (y * NXH + h) * NC + c)
        for y in range(NY)
        for h in range(NXH)
        for c in range(NC)
    ]


def from_seq(a, dz, dx):
    return lax.ppermute(a, "seq", seq_perm(dz, dx))


def from_user(a, dy, dh, dc):
    return lax.ppermute(a, "user", user_perm(dy, dh, dc))


def from_both(a, dh, dx):
    pairs = []
    for s in range(NZ * NX):
        for u in range(NY * NXH * NC):
            pairs.append(((s ^ dx) * NY * NXH * NC + (u ^ (dh * NC)), s * NY * NXH * NC + u))
    return lax.ppermute(a, ("seq", "user"), pairs)


def gather_seq(block, x_rows=(96, 176)):
    got = {(0, 0): block}
    got[1, 0] = from_seq(block, 1, 0)
    got[3, 0] = from_seq(block, 3, 0)
    got[0, 1] = from_seq(block, 0, 1)
    got[2, 0] = from_seq(got[1, 0], 1, 0)
    got[3, 1] = from_seq(got[0, 1], 3, 0)
    got[1, 1] = from_seq(got[1, 0], 0, 1)
    a, b = x_rows
    got[2, 1] = jnp.concatenate(
        [
            from_seq(got[2, 0][:a], 0, 1),
            from_seq(got[1, 1][a:b], 1, 0),
            from_seq(got[3, 1][b:], 3, 0),
        ],
        axis=0,
    )
    return got


def layer_norm(entries):
    centre = jnp.mean(entries, axis=-1, keepdims=True)
    centred = entries - centre
    inverse = lax.rsqrt(jnp.mean(centred * centred, axis=-1, keepdims=True) + EPS)
    return centred * inverse, inverse


def norm_back(normed, inverse, upstream):
    first_term = jnp.mean(upstream, axis=-1, keepdims=True)
    second_term = jnp.mean(upstream * normed, axis=-1, keepdims=True)
    return inverse * (upstream - first_term - normed * second_term)


def dot(a, b):
    return jnp.dot(a, b, preferred_element_type=F32)


def dot_nt(a, b):
    return lax.dot_general(a, b, (((1,), (1,)), ((), ())), preferred_element_type=F32)


def dot_tn(a, b):
    return lax.dot_general(a, b, (((0,), (0,)), ((), ())), preferred_element_type=F32)


def ln_proj_kernel(at_ref, hist_ref, w_ref, *refs):
    normed_ref, act_ref, slope_ref = refs[-3:]
    hist = hist_ref[...].astype(F32)
    normed, _ = layer_norm(hist)
    normed_b = normed.astype(BF16)
    normed_ref[...] = normed_b
    projected = dot(normed_b, w_ref[...])
    half = 0.5 * projected
    tanh = jnp.tanh(half)
    silu = half + half * tanh
    act_ref[...] = silu.astype(BF16)
    slope_ref[...] = 0.5 + 0.5 * tanh + silu * (0.5 - 0.5 * tanh)


def ln_proj(at, block, w_head, outs):
    rows, width = block.shape
    cols = w_head.shape[1]
    half = rows // 2
    length = rows * NZ * NX

    def stored(i, at_ref):
        return (2 * at_ref[0] + i, 0)

    def in_time(i, at_ref):
        return (jnp.where(i == 0, at_ref[0], 2 * NZ * NX - 1 - at_ref[0]), 0)

    out_specs = (
        pl.BlockSpec((half, width), stored),
        pl.BlockSpec((half, cols), in_time),
        pl.BlockSpec((half, cols), in_time),
    )
    in_specs = [
        pl.BlockSpec((half, width), lambda i, at_ref: (i, 0)),
        pl.BlockSpec((width, cols), lambda i, at_ref: (0, 0)),
    ]
    aliases = {}
    if outs:
        in_specs += [pl.BlockSpec(memory_space=pl.ANY)] * 3
        aliases = {3: 0, 4: 1, 5: 2}
    return pl.pallas_call(
        ln_proj_kernel,
        grid_spec=pltpu.PrefetchScalarGridSpec(
            num_scalar_prefetch=1, grid=(2,), in_specs=in_specs, out_specs=out_specs
        ),
        out_shape=(
            jax.ShapeDtypeStruct((length, width), BF16),
            jax.ShapeDtypeStruct((length, cols), BF16),
            jax.ShapeDtypeStruct((length, cols), F32),
        ),
        input_output_aliases=aliases,
        compiler_params=pltpu.CompilerParams(vmem_limit_bytes=16 << 20),
        cost_estimate=pl.CostEstimate(
            flops=2 * rows * width * cols, bytes_accessed=3 << 20, transcendentals=rows * cols
        ),
        name="ln_proj",
    )(at, block, w_head, *outs)


TILE = 256
SCALE = HD ** (-0.5)


def tile_place(block):
    last = 2 * NZ * NX - 1
    return (block, 0) if block < NZ * NX else (last - block, HD)


def forward_kernel(first_ref, act_ref, head_ref, start_ref, att_ref, gate_ref, gg_ref, stats_ref, vt_ref):
    length = act_ref.shape[0]
    blocks = length // TILE
    for j in range(blocks):
        at = slice(j * TILE, (j + 1) * TILE)
        vt_ref[:, at] = act_ref[at, HD : 2 * HD].T
    key_row = lax.broadcasted_iota(jnp.int32, (TILE, TILE), 0)
    query_col = lax.broadcasted_iota(jnp.int32, (1, TILE), 1)
    for i in range(blocks):
        at = slice(i * TILE, (i + 1) * TILE)
        queries = act_ref[at, 2 * HD : 3 * HD]
        start = start_ref[:, at]

        def step(j, total):
            base = pl.multiple_of(j * TILE, TILE)
            half = dot_nt(act_ref[pl.ds(base, TILE), 3 * HD :], queries) * (0.5 * SCALE)
            weights = half + half * jnp.tanh(half)
            seen = (key_row <= query_col + (i * TILE - base)) & (key_row >= start - base)
            weights = jnp.where(seen, weights, 0.0).astype(BF16)
            return total + dot(vt_ref[:, pl.ds(base, TILE)], weights)

        total = lax.fori_loop(first_ref[i], i + 1, step, jnp.zeros((HD, TILE), F32))
        att_ref[:, at] = total
        gate = act_ref[at, :HD].T
        parts = []
        for block in (2 * i, 2 * i + 1):
            shard, row = tile_place(block)
            parts.append(head_ref[shard, row : row + HD, :].T)
        gg = jnp.concatenate(parts, axis=1)
        gate_ref[:, at] = gate
        gg_ref[:, at] = gg
        grad_mixed = gg.astype(F32) * gate.astype(F32)
        mean = jnp.sum(total, axis=0, keepdims=True) * (1.0 / HD)
        centred = total - mean
        stats_ref[0:1, at] = mean
        stats_ref[1:2, at] = jnp.sum(centred * centred, axis=0, keepdims=True)
        stats_ref[2:3, at] = jnp.sum(grad_mixed, axis=0, keepdims=True)
        stats_ref[3:4, at] = jnp.sum(grad_mixed * centred, axis=0, keepdims=True)


def vmem():
    return pl.BlockSpec(memory_space=pltpu.VMEM)


def smem():
    return pl.BlockSpec(memory_space=pltpu.SMEM)


def forward(first, act, at_head, start):
    length = act.shape[0]
    return pl.pallas_call(
        forward_kernel,
        in_specs=[smem(), vmem(), vmem(), vmem()],
        out_specs=[vmem()] * 4,
        out_shape=(
            jax.ShapeDtypeStruct((HD, length), F32),
            jax.ShapeDtypeStruct((HD, length), BF16),
            jax.ShapeDtypeStruct((HD, length), BF16),
            jax.ShapeDtypeStruct((4, length), F32),
        ),
        scratch_shapes=[pltpu.VMEM((HD, length), BF16)],
        compiler_params=pltpu.CompilerParams(vmem_limit_bytes=24 << 20),
        cost_estimate=pl.CostEstimate(
            flops=2 * HD * length * length, bytes_accessed=6 << 20, transcendentals=length * length // 2
        ),
        name="attention_forward",
    )(first, act, at_head, start)


def mix_kernel(own_ref, one_ref, three_ref, two_ref, att_ref, gate_ref, gg_ref, slope_ref, early_ref, go_ref, got_ref):
    length = att_ref.shape[1]
    width = H * HD
    heads = [ref[k] for ref in (own_ref, one_ref, three_ref, two_ref) for k in range(NX)]
    mean_all = sum(a[0:1] for a in heads) * (1.0 / H)
    apart = [a[0:1] - mean_all for a in heads]
    spread = sum(a[1:2] for a in heads) + HD * sum(d * d for d in apart)
    inverse_all = lax.rsqrt(spread * (1.0 / width) + EPS)
    first_all = sum(a[2:3] for a in heads) * (1.0 / width)
    second_all = inverse_all * sum(a[3:4] + d * a[2:3] for a, d in zip(heads, apart)) * (1.0 / width)
    for i in range(length // TILE):
        at = slice(i * TILE, (i + 1) * TILE)
        gate = gate_ref[:, at].astype(F32)
        gg = gg_ref[:, at].astype(F32)
        inverse = inverse_all[:, at]
        mixed = (att_ref[:, at] - mean_all[:, at]) * inverse
        grad_att = inverse * (gg * gate - first_all[:, at] - mixed * second_all[:, at])
        got_ref[:, at] = grad_att.astype(BF16)
        go_ref[at, :] = grad_att.T.astype(BF16)
        gated = (mixed * gate).T.astype(BF16)
        grad_u = (gg * mixed).T * slope_ref[at, :HD]
        for k in range(2):
            shard, row = tile_place(2 * i + k)
            early_ref[shard, row : row + HD, :HD] = gated[k * HD : (k + 1) * HD]
            early_ref[shard, row : row + HD, HD:] = grad_u[k * HD : (k + 1) * HD].astype(BF16)


def mix(own, one, three, two, att, gate, gg, slope):
    length = att.shape[1]
    shards = NZ * NX
    whole = lambda shape: pl.BlockSpec(shape, lambda i: (0,) * len(shape))
    return pl.pallas_call(
        mix_kernel,
        grid=(1,),
        in_specs=[whole(own.shape)] * 4
        + [whole(att.shape)] * 3
        + [pl.BlockSpec((length, HD), lambda i: (0, 0))],
        out_specs=[whole((shards, length // shards, 2 * HD)), whole((length, HD)), whole((HD, length))],
        out_shape=(
            jax.ShapeDtypeStruct((shards, length // shards, 2 * HD), BF16),
            jax.ShapeDtypeStruct((length, HD), BF16),
            jax.ShapeDtypeStruct((HD, length), BF16),
        ),
        compiler_params=pltpu.CompilerParams(vmem_limit_bytes=24 << 20),
        cost_estimate=pl.CostEstimate(flops=20 * HD * length, bytes_accessed=6 << 20, transcendentals=0),
        name="mix",
    )(own, one, three, two, att, gate, gg, slope)


def backward_kernel(first_ref, act_ref, go_ref, got_ref, start_ref, slope_ref, late_ref, kt_ref, dk_ref, dv_ref):
    length = act_ref.shape[0]
    blocks = length // TILE
    for j in range(blocks):
        at = slice(j * TILE, (j + 1) * TILE)
        kt_ref[:, at] = act_ref[at, 3 * HD :].T
    key_row = lax.broadcasted_iota(jnp.int32, (TILE, TILE), 0)
    query_col = lax.broadcasted_iota(jnp.int32, (1, TILE), 1)
    dk_ref[...] = jnp.zeros_like(dk_ref)
    dv_ref[...] = jnp.zeros_like(dv_ref)

    def put(i, k, column, value):
        shard, row = tile_place(2 * i + k)
        late_ref[shard, row : row + HD, column * HD : (column + 1) * HD] = value

    for i in range(blocks):
        at = slice(i * TILE, (i + 1) * TILE)
        queries = act_ref[at, 2 * HD : 3 * HD]
        grad_out = go_ref[at, :]
        grad_out_t = got_ref[:, at]
        start = start_ref[:, at]

        def step(j, total):
            base = pl.multiple_of(j * TILE, TILE)
            here = pl.ds(base, TILE)
            half = dot_nt(act_ref[here, 3 * HD :], queries) * (0.5 * SCALE)
            tanh = jnp.tanh(half)
            weights = half + half * tanh
            sig = 0.5 + 0.5 * tanh
            slope = sig + weights * (1.0 - sig)
            seen = (key_row <= query_col + (i * TILE - base)) & (key_row >= start - base)
            ahead = dot(act_ref[here, HD : 2 * HD], grad_out_t)
            weights = jnp.where(seen, weights, 0.0).astype(BF16)
            slopes = jnp.where(seen, ahead * slope, 0.0).astype(BF16)
            dv_ref[here, :] += dot(weights, grad_out)
            dk_ref[here, :] += dot(slopes, queries)
            return total + dot(kt_ref[:, here], slopes)

        total = lax.fori_loop(first_ref[i], i + 1, step, jnp.zeros((HD, TILE), F32))
        grad_q = total.T * slope_ref[at, 2 * HD : 3 * HD] * SCALE
        for k in range(2):
            put(i, k, 1, grad_q[k * HD : (k + 1) * HD].astype(BF16))
    for i in range(blocks):
        for k in range(2):
            at = slice(i * TILE + k * HD, i * TILE + (k + 1) * HD)
            put(i, k, 0, (dv_ref[at, :] * slope_ref[at, HD : 2 * HD]).astype(BF16))
            put(i, k, 2, (dk_ref[at, :] * SCALE * slope_ref[at, 3 * HD :]).astype(BF16))


def backward(first, act, grad_out, grad_out_t, start, slope):
    length = act.shape[0]
    shards = NZ * NX
    return pl.pallas_call(
        backward_kernel,
        in_specs=[smem()] + [vmem()] * 5,
        out_specs=vmem(),
        out_shape=jax.ShapeDtypeStruct((shards, length // shards, 3 * HD), BF16),
        scratch_shapes=[
            pltpu.VMEM((HD, length), BF16),
            pltpu.VMEM((length, HD), F32),
            pltpu.VMEM((length, HD), F32),
        ],
        compiler_params=pltpu.CompilerParams(vmem_limit_bytes=32 << 20),
        cost_estimate=pl.CostEstimate(
            flops=5 * HD * length * length, bytes_accessed=10 << 20, transcendentals=length * length // 2
        ),
        name="attention_backward",
    )(first, act, grad_out, grad_out_t, start, slope)


def part_out_kernel(at_ref, early_ref, *refs):
    out_ref = refs[-1]
    total = None
    for r, cot_ref in enumerate(refs[:-1]):
        term = dot_tn(early_ref[at_ref[r], :, :HD], cot_ref[...])
        total = term if total is None else total + term
    out_ref[...] = total


def part_out_of(at, early, blocks):
    width = blocks[0].shape[1]
    return pl.pallas_call(
        part_out_kernel,
        in_specs=[smem()] + [vmem()] * (1 + len(blocks)),
        out_specs=vmem(),
        out_shape=jax.ShapeDtypeStruct((HD, width), F32),
        compiler_params=pltpu.CompilerParams(vmem_limit_bytes=24 << 20),
        cost_estimate=pl.CostEstimate(
            flops=2 * HD * width * 2048, bytes_accessed=6 << 20, transcendentals=0
        ),
        name="part_out",
    )(at, early, *blocks)


def local(history, segment_ids, w_in, w_out, cotangent):
    hist = history[0]
    cot = cotangent[0]
    rows, width = hist.shape
    length = rows * NZ * NX
    s = lax.axis_index("seq")
    u = lax.axis_index("user")
    z, x = s // NX, s % NX
    y, xh, core = u // (NXH * NC), (u // NC) % NXH, u % NC

    hist_got = gather_seq(hist)
    w_head = jnp.concatenate(
        [lax.dynamic_slice(w_in, (0, i * width + s * HD), (width, HD)) for i in range(4)], axis=1
    )

    def place_of(key):
        return ((z + key[0]) % NZ) * NX + (x ^ key[1])

    outs = ()
    for key in ORDER:
        outs = ln_proj(place_of(key).reshape(1), hist_got[key], w_head, outs)
    normed_b, act, slope = outs

    grad_gated_own = dot_nt(cot, w_out).astype(BF16)
    ids = segment_ids[0].astype(BF16).reshape(2, HD)
    ids = jnp.pad(ids, ((0, 14), (0, 0)))
    to_heads = jnp.concatenate(
        [
            grad_gated_own.reshape(rows, H, HD).transpose(1, 0, 2),
            jnp.broadcast_to(ids[None], (H, 16, HD)),
        ],
        axis=1,
    )
    at_head = lax.all_to_all(to_heads, "seq", 0, 0, tiled=True)
    ids = at_head[:, rows : rows + 2].astype(jnp.int32)
    ids = jnp.concatenate([ids[:, 0], ids[::-1, 1]], axis=0).reshape(1, length)
    start = sum(jnp.where(ids > v, jnp.sum((ids == v).astype(jnp.int32)), 0) for v in range(3))
    first = start[0, ::TILE] // TILE

    cot_late, _ = lax.optimization_barrier((cot, hist_got[1, 1]))
    cot_got = gather_seq(cot_late)

    att, gate_t, gg_t, stats = forward(first, act, at_head, start)
    pair = jnp.stack([stats, from_seq(stats, 0, 1)])
    others = [from_seq(pair, dz, 0) for dz in (1, 3, 2)]
    early, grad_out, grad_out_t = mix(pair, *others, att, gate_t, gg_t, slope)
    early_back = lax.all_to_all(early, "seq", 0, 0, tiled=True)
    late = backward(first, act, grad_out, grad_out_t, start, slope)
    late_back = lax.all_to_all(late, "seq", 0, 0, tiled=True)

    grad_proj = jnp.concatenate(
        [early[:, :, HD:].reshape(length, HD), late.reshape(length, 3 * HD)], axis=1
    )
    part_in = dot_tn(normed_b, grad_proj)
    places = jnp.stack([place_of(key) for key in ORDER])
    part_out = part_out_of(places, early, [cot_got[key] for key in ORDER])
    users = NY * NXH * NC
    n_in = width // (users * H)
    terms_in = part_in.reshape(H, users, n_in, 4 * HD).transpose(1, 0, 2, 3)
    terms_in = terms_in.reshape(users, H * n_in, 4 * HD)
    terms_out = part_out.reshape(users, -1, 4 * HD)
    terms = jnp.concatenate([terms_in, terms_out], axis=1)
    n_rows = terms.shape[1]
    terms = terms.reshape(NY * NXH, NC, n_rows, 4 * HD)

    def pick(a, at, axis):
        return lax.dynamic_index_in_dim(a, at, axis, keepdims=False)

    terms = pick(terms, core, 1) + from_user(pick(terms, 1 - core, 1), 0, 0, 1)
    terms = terms.reshape(NY, NXH, n_rows, 4 * HD)
    total = pick(terms, y, 0)
    for d in (1, 3, 2):
        sent = pick(terms, (y - d) % NY, 0).astype(BF16)
        total = total + from_user(sent, d, 0, 0).astype(F32)
    rows_in = total[:, : H * n_in].reshape(NXH, NZ, NX, n_in, 4 * HD)
    rows_out = total[:, H * n_in :]

    def slab(h, l):
        return pick(pick(rows_in, h, 0), l, 1).reshape(NZ * n_in, 4 * HD)

    same = jnp.concatenate([slab(1 - xh, x), pick(rows_out, 1 - xh, 0)])
    same = from_both(same, 1, 0)
    own_in = slab(xh, x) + same[: NZ * n_in]
    own_out = pick(rows_out, xh, 0) + same[NZ * n_in :]
    other_in = from_both(slab(xh, 1 - x), 0, 1) + from_both(slab(1 - xh, 1 - x), 1, 1)
    columns = jnp.where(
        x == 0, jnp.stack([own_in, other_in]), jnp.stack([other_in, own_in])
    ).reshape(NX, NZ, n_in, 4 * HD)
    whole = jnp.zeros((NZ, NX, n_in, 4 * HD), F32)
    whole = lax.dynamic_update_slice(whole, pick(columns, z, 1)[None], (z, 0, 0, 0))
    for d in (1, 3, 2):
        got = from_seq(pick(columns, (z - d) % NZ, 1), d, 0)
        whole = lax.dynamic_update_slice(whole, got[None], ((z + d) % NZ, 0, 0, 0))
    factor = (length * users) ** (-0.5)
    grad_w_in = whole.reshape(H, n_in, 4, HD).transpose(1, 2, 0, 3).reshape(n_in, 4 * width)
    grad_w_out = own_out.reshape(-1, width)

    hist_f = hist.astype(F32)
    normed, inverse = layer_norm(hist_f)
    proj_tok = jnp.concatenate([early_back[:, :, HD:], late_back], axis=2)
    proj_tok = proj_tok.reshape(H, rows, 4, HD).transpose(1, 2, 0, 3)
    grad_normed = dot_nt(proj_tok.reshape(rows, 4 * width), w_in)
    gated_tok = early_back[:, :, :HD].transpose(1, 0, 2).reshape(rows, width)
    layer_out = (hist_f + dot(gated_tok, w_out)).astype(BF16)
    grad_history = (cot.astype(F32) + norm_back(normed, inverse, grad_normed)).astype(BF16)
    return layer_out[None], grad_history[None], grad_w_in * factor, grad_w_out * factor


def solution(mesh):
    in_specs = (P("user", "seq", None), P("user", "seq"), P(), P(), P("user", "seq", None))
    out_specs = (
        P("user", "seq", None),
        P("user", "seq", None),
        P(("seq", "user"), None),
        P(("seq", "user"), None),
    )
    return jax.shard_map(local, mesh=mesh, in_specs=in_specs, out_specs=out_specs, check_vma=False)
```

```python
import functools

import jax
import jax.numpy as jnp
from jax import lax
from jax.experimental import pallas as pl
from jax.experimental.pallas import tpu as pltpu
from jax.sharding import PartitionSpec as P

F32 = jnp.float32
BF16 = jnp.bfloat16
EPS = 1e-05
H = 8
HD = 128
NZ, NX = 4, 2
NY, NXH, NC = 4, 2, 2
ORDER = ((0, 0), (1, 0), (3, 0), (0, 1), (2, 0), (3, 1), (1, 1), (2, 1))


def seq_perm(dz, dx):
    return [
        (((z + dz) % NZ) * NX + (x ^ dx), z * NX + x) for z in range(NZ) for x in range(NX)
    ]


def user_perm(dy, dh, dc):
    return [
        ((((y + dy) % NY) * NXH + (h ^ dh)) * NC + (c ^ dc), (y * NXH + h) * NC + c)
        for y in range(NY)
        for h in range(NXH)
        for c in range(NC)
    ]


def from_seq(a, dz, dx):
    return lax.ppermute(a, "seq", seq_perm(dz, dx))


def from_user(a, dy, dh, dc):
    return lax.ppermute(a, "user", user_perm(dy, dh, dc))


def from_both(a, dh, dx):
    pairs = []
    for s in range(NZ * NX):
        for u in range(NY * NXH * NC):
            pairs.append(((s ^ dx) * NY * NXH * NC + (u ^ (dh * NC)), s * NY * NXH * NC + u))
    return lax.ppermute(a, ("seq", "user"), pairs)


def step_one(block):
    return {
        (1, 0): from_seq(block, 1, 0),
        (3, 0): from_seq(block, 3, 0),
        (0, 1): from_seq(block, 0, 1),
    }


def step_two(got):
    return {
        (2, 0): from_seq(got[1, 0], 1, 0),
        (3, 1): from_seq(got[0, 1], 3, 0),
        (1, 1): from_seq(got[1, 0], 0, 1),
    }


def step_three(got, a=96, b=176):
    return {
        (2, 1): jnp.concatenate(
            [
                from_seq(got[2, 0][:a], 0, 1),
                from_seq(got[1, 1][a:b], 1, 0),
                from_seq(got[3, 1][b:], 3, 0),
            ],
            axis=0,
        )
    }


def layer_norm(entries):
    centre = jnp.mean(entries, axis=-1, keepdims=True)
    centred = entries - centre
    inverse = lax.rsqrt(jnp.mean(centred * centred, axis=-1, keepdims=True) + EPS)
    return centred * inverse, inverse


def norm_back(normed, inverse, upstream):
    first_term = jnp.mean(upstream, axis=-1, keepdims=True)
    second_term = jnp.mean(upstream * normed, axis=-1, keepdims=True)
    return inverse * (upstream - first_term - normed * second_term)


def dot(a, b):
    return jnp.dot(a, b, preferred_element_type=F32)


def dot_nt(a, b):
    return lax.dot_general(a, b, (((1,), (1,)), ((), ())), preferred_element_type=F32)


def dot_tn(a, b):
    return lax.dot_general(a, b, (((0,), (0,)), ((), ())), preferred_element_type=F32)


def params():
    return pltpu.CompilerParams(vmem_limit_bytes=56 << 20)


def ln_proj_kernel(at_ref, hist_ref, w_ref, *refs):
    normed_ref, act_ref, slope_ref = refs[-3:]
    hist = hist_ref[...].astype(F32)
    normed, _ = layer_norm(hist)
    normed_b = normed.astype(BF16)
    normed_ref[...] = normed_b.T
    projected = dot(normed_b, w_ref[...])
    half = 0.5 * projected
    tanh = jnp.tanh(half)
    silu = half + half * tanh
    act_ref[...] = silu.astype(BF16)
    slope_ref[...] = 0.5 + 0.5 * tanh + silu * (0.5 - 0.5 * tanh)


def ln_proj(at, block, w_head, outs):
    rows, width = block.shape
    cols = w_head.shape[1]
    half = rows // 2
    length = rows * NZ * NX

    def stored(i, at_ref):
        return (0, 2 * at_ref[0] + i)

    def in_time(i, at_ref):
        return (jnp.where(i == 0, at_ref[0], 2 * NZ * NX - 1 - at_ref[0]), 0)

    out_specs = (
        pl.BlockSpec((width, half), stored),
        pl.BlockSpec((half, cols), in_time),
        pl.BlockSpec((half, cols), in_time),
    )
    in_specs = [
        pl.BlockSpec((half, width), lambda i, at_ref: (i, 0)),
        pl.BlockSpec((width, cols), lambda i, at_ref: (0, 0)),
    ]
    aliases = {}
    if outs:
        in_specs += [pl.BlockSpec(memory_space=pl.ANY)] * 3
        aliases = {3: 0, 4: 1, 5: 2}
    return pl.pallas_call(
        ln_proj_kernel,
        grid_spec=pltpu.PrefetchScalarGridSpec(
            num_scalar_prefetch=1, grid=(2,), in_specs=in_specs, out_specs=out_specs
        ),
        out_shape=(
            jax.ShapeDtypeStruct((width, length), BF16),
            jax.ShapeDtypeStruct((length, cols), BF16),
            jax.ShapeDtypeStruct((length, cols), F32),
        ),
        input_output_aliases=aliases,
        compiler_params=params(),
        cost_estimate=pl.CostEstimate(
            flops=2 * rows * width * cols, bytes_accessed=3 << 20, transcendentals=rows * cols
        ),
        name="ln_proj",
    )(at, block, w_head, *outs)


TQ = 1024
TK = 512
TM = 256
SCALE = HD ** (-0.5)


def tile_place(block):
    last = 2 * NZ * NX - 1
    return (block, 0) if block < NZ * NX else (last - block, HD)


def forward_kernel(first_ref, act_ref, head_ref, start_ref, att_ref, gate_ref, gg_ref, stats_ref, vt_ref):
    length = act_ref.shape[0]
    for j in range(length // TK):
        at = slice(j * TK, (j + 1) * TK)
        vt_ref[:, at] = act_ref[at, HD : 2 * HD].T
    key_row = lax.broadcasted_iota(jnp.int32, (TK, TQ), 0)
    query_col = lax.broadcasted_iota(jnp.int32, (1, TQ), 1)
    for i in range(length // TQ):
        at = slice(i * TQ, (i + 1) * TQ)
        queries = act_ref[at, 2 * HD : 3 * HD]
        start = start_ref[:, at]

        def step(j, total):
            base = pl.multiple_of(j * TK, TK)
            half = dot_nt(act_ref[pl.ds(base, TK), 3 * HD :], queries) * (0.5 * SCALE)
            weights = half + half * jnp.tanh(half)
            seen = (key_row <= query_col + (i * TQ - base)) & (key_row >= start - base)
            weights = jnp.where(seen, weights, 0.0).astype(BF16)
            return total + dot(vt_ref[:, pl.ds(base, TK)], weights)

        end = ((i + 1) * TQ + TK - 1) // TK
        total = lax.fori_loop(first_ref[i], end, step, jnp.zeros((HD, TQ), F32))
        att_ref[:, at] = total
        gate = act_ref[at, :HD].T
        parts = []
        for block in range(i * TQ // HD, (i + 1) * TQ // HD):
            shard, row = tile_place(block)
            parts.append(head_ref[shard, row : row + HD, :].T)
        gg = jnp.concatenate(parts, axis=1)
        gate_ref[:, at] = gate
        gg_ref[:, at] = gg
        grad_mixed = gg.astype(F32) * gate.astype(F32)
        mean = jnp.sum(total, axis=0, keepdims=True) * (1.0 / HD)
        centred = total - mean
        stats_ref[0:1, at] = mean
        stats_ref[1:2, at] = jnp.sum(centred * centred, axis=0, keepdims=True)
        stats_ref[2:3, at] = jnp.sum(grad_mixed, axis=0, keepdims=True)
        stats_ref[3:4, at] = jnp.sum(grad_mixed * centred, axis=0, keepdims=True)


def vmem():
    return pl.BlockSpec(memory_space=pltpu.VMEM)


def smem():
    return pl.BlockSpec(memory_space=pltpu.SMEM)


def forward(first, act, at_head, start):
    length = act.shape[0]
    return pl.pallas_call(
        forward_kernel,
        in_specs=[smem(), vmem(), vmem(), vmem()],
        out_specs=[vmem()] * 4,
        out_shape=(
            jax.ShapeDtypeStruct((HD, length), F32),
            jax.ShapeDtypeStruct((HD, length), BF16),
            jax.ShapeDtypeStruct((HD, length), BF16),
            jax.ShapeDtypeStruct((4, length), F32),
        ),
        scratch_shapes=[pltpu.VMEM((HD, length), BF16)],
        compiler_params=params(),
        cost_estimate=pl.CostEstimate(
            flops=2 * HD * length * length, bytes_accessed=6 << 20, transcendentals=length * length // 2
        ),
        name="attention_forward",
    )(first, act, at_head, start)


def mix_kernel(own_ref, one_ref, three_ref, two_ref, att_ref, gate_ref, gg_ref, slope_ref, early_ref, go_ref, got_ref, gated_ref):
    length = att_ref.shape[1]
    width = H * HD
    heads = [ref[k] for ref in (own_ref, one_ref, three_ref, two_ref) for k in range(NX)]
    mean_all = sum(a[0:1] for a in heads) * (1.0 / H)
    apart = [a[0:1] - mean_all for a in heads]
    spread = sum(a[1:2] for a in heads) + HD * sum(d * d for d in apart)
    inverse_all = lax.rsqrt(spread * (1.0 / width) + EPS)
    first_all = sum(a[2:3] for a in heads) * (1.0 / width)
    second_all = inverse_all * sum(a[3:4] + d * a[2:3] for a, d in zip(heads, apart)) * (1.0 / width)
    for i in range(length // TM):
        at = slice(i * TM, (i + 1) * TM)
        gate = gate_ref[:, at].astype(F32)
        gg = gg_ref[:, at].astype(F32)
        inverse = inverse_all[:, at]
        mixed = (att_ref[:, at] - mean_all[:, at]) * inverse
        grad_att = inverse * (gg * gate - first_all[:, at] - mixed * second_all[:, at])
        got_ref[:, at] = grad_att.astype(BF16)
        go_ref[at, :] = grad_att.T.astype(BF16)
        gated_t = (mixed * gate).astype(BF16)
        gated = gated_t.T
        grad_u = (gg * mixed).T * slope_ref[at, :HD]
        for k in range(TM // HD):
            shard, row = tile_place(i * TM // HD + k)
            stored = slice(2 * HD * shard + row, 2 * HD * shard + row + HD)
            gated_ref[:, stored] = gated_t[:, k * HD : (k + 1) * HD]
            early_ref[shard, row : row + HD, :HD] = gated[k * HD : (k + 1) * HD]
            early_ref[shard, row : row + HD, HD:] = grad_u[k * HD : (k + 1) * HD].astype(BF16)


def mix(own, one, three, two, att, gate, gg, slope):
    length = att.shape[1]
    shards = NZ * NX
    whole = lambda shape: pl.BlockSpec(shape, lambda i: (0,) * len(shape))
    return pl.pallas_call(
        mix_kernel,
        grid=(1,),
        in_specs=[whole(own.shape)] * 4
        + [whole(att.shape)] * 3
        + [pl.BlockSpec((length, HD), lambda i: (0, 0))],
        out_specs=[whole((shards, length // shards, 2 * HD)), whole((length, HD))]
        + [whole((HD, length))] * 2,
        out_shape=(
            jax.ShapeDtypeStruct((shards, length // shards, 2 * HD), BF16),
            jax.ShapeDtypeStruct((length, HD), BF16),
            jax.ShapeDtypeStruct((HD, length), BF16),
            jax.ShapeDtypeStruct((HD, length), BF16),
        ),
        compiler_params=params(),
        cost_estimate=pl.CostEstimate(flops=20 * HD * length, bytes_accessed=6 << 20, transcendentals=0),
        name="mix",
    )(own, one, three, two, att, gate, gg, slope)


def backward_kernel(first_ref, act_ref, go_ref, got_ref, start_ref, slope_ref, late_ref, kt_ref, dk_ref, dv_ref):
    length = act_ref.shape[0]
    for j in range(length // TK):
        at = slice(j * TK, (j + 1) * TK)
        kt_ref[:, at] = act_ref[at, 3 * HD :].T
    key_row = lax.broadcasted_iota(jnp.int32, (TK, TQ), 0)
    query_col = lax.broadcasted_iota(jnp.int32, (1, TQ), 1)
    dk_ref[...] = jnp.zeros_like(dk_ref)
    dv_ref[...] = jnp.zeros_like(dv_ref)

    def put(block, column, value):
        shard, row = tile_place(block)
        late_ref[shard, row : row + HD, column * HD : (column + 1) * HD] = value.astype(BF16)

    for i in range(length // TQ):
        at = slice(i * TQ, (i + 1) * TQ)
        queries = act_ref[at, 2 * HD : 3 * HD]
        grad_out = go_ref[at, :]
        grad_out_t = got_ref[:, at]
        start = start_ref[:, at]

        def step(j, total):
            base = pl.multiple_of(j * TK, TK)
            here = pl.ds(base, TK)
            half = dot_nt(act_ref[here, 3 * HD :], queries) * (0.5 * SCALE)
            tanh = jnp.tanh(half)
            weights = half + half * tanh
            sig = 0.5 + 0.5 * tanh
            slope = sig + weights * (1.0 - sig)
            seen = (key_row <= query_col + (i * TQ - base)) & (key_row >= start - base)
            ahead = dot(act_ref[here, HD : 2 * HD], grad_out_t)
            weights = jnp.where(seen, weights, 0.0).astype(BF16)
            slopes = jnp.where(seen, ahead * slope, 0.0).astype(BF16)
            dv_ref[here, :] += dot(weights, grad_out)
            dk_ref[here, :] += dot(slopes, queries)
            return total + dot(kt_ref[:, here], slopes)

        end = ((i + 1) * TQ + TK - 1) // TK
        total = lax.fori_loop(first_ref[i], end, step, jnp.zeros((HD, TQ), F32))
        grad_q = total.T * slope_ref[at, 2 * HD : 3 * HD] * SCALE
        for k in range(TQ // HD):
            put(i * TQ // HD + k, 1, grad_q[k * HD : (k + 1) * HD])
    for block in range(length // HD):
        at = slice(block * HD, (block + 1) * HD)
        put(block, 0, dv_ref[at, :] * slope_ref[at, HD : 2 * HD])
        put(block, 2, dk_ref[at, :] * SCALE * slope_ref[at, 3 * HD :])


def backward(first, act, grad_out, grad_out_t, start, slope):
    length = act.shape[0]
    shards = NZ * NX
    return pl.pallas_call(
        backward_kernel,
        in_specs=[smem()] + [vmem()] * 5,
        out_specs=vmem(),
        out_shape=jax.ShapeDtypeStruct((shards, length // shards, 3 * HD), BF16),
        scratch_shapes=[
            pltpu.VMEM((HD, length), BF16),
            pltpu.VMEM((length, HD), F32),
            pltpu.VMEM((length, HD), F32),
        ],
        compiler_params=params(),
        cost_estimate=pl.CostEstimate(
            flops=5 * HD * length * length, bytes_accessed=10 << 20, transcendentals=length * length // 2
        ),
        name="attention_backward",
    )(first, act, grad_out, grad_out_t, start, slope)


def terms_in_kernel(core_ref, normed_ref, gate_ref, late_ref, keep_ref, send_ref, res_ref):
    shards, rows, _ = gate_ref.shape
    normed_t = normed_ref[...]
    res_ref[:, :HD] = dot(normed_t, gate_ref[...].reshape(shards * rows, HD))
    res_ref[:, HD:] = dot(normed_t, late_ref[...].reshape(shards * rows, 3 * HD))
    core = core_ref[0]
    for k in range(res_ref.shape[0] // HD):
        for pair in range(NY * NXH):
            mine = pl.multiple_of(k * HD + (pair * NC + core) * 8, 8)
            other = pl.multiple_of(k * HD + (pair * NC + 1 - core) * 8, 8)
            keep_ref[pair, k * 8 : (k + 1) * 8, :] = res_ref[pl.ds(mine, 8), :]
            send_ref[pair, k * 8 : (k + 1) * 8, :] = res_ref[pl.ds(other, 8), :]


def terms_in(core, normed_t, early, late):
    width, length = normed_t.shape
    shards, rows, _ = early.shape
    shape = jax.ShapeDtypeStruct((NY * NXH, 80, 4 * HD), F32)
    out_spec = pl.BlockSpec((NY * NXH, 16, 4 * HD), lambda g: (0, g, 0))
    return pl.pallas_call(
        terms_in_kernel,
        grid=(4,),
        in_specs=[
            smem(),
            pl.BlockSpec((width // 4, length), lambda g: (g, 0)),
            pl.BlockSpec((shards, rows, HD), lambda g: (0, 0, 1)),
            pl.BlockSpec((shards, rows, 3 * HD), lambda g: (0, 0, 0)),
        ],
        out_specs=[out_spec] * 2,
        out_shape=[shape] * 2,
        scratch_shapes=[pltpu.VMEM((width // 4, 4 * HD), F32)],
        compiler_params=params(),
        cost_estimate=pl.CostEstimate(
            flops=2 * width * length * 4 * HD, bytes_accessed=9 << 20, transcendentals=0
        ),
        name="terms_in",
    )(core, normed_t, early, late)


def terms_out_kernel(core_ref, at_ref, gated_ref, *refs):
    cots = refs[: NZ * NX]
    keep_ref, send_ref, res_ref = refs[-3:]
    rows = cots[0].shape[0]
    total = None
    for r, cot_ref in enumerate(cots):
        here = pl.ds(pl.multiple_of(at_ref[r] * rows, rows), rows)
        term = dot(gated_ref[:, here], cot_ref[...])
        total = term if total is None else total + term
    res_ref[...] = total
    core = core_ref[0]
    for pair in range(NY * NXH):
        for out_ref, who in ((keep_ref, core), (send_ref, 1 - core)):
            block = res_ref[pl.ds(pl.multiple_of((pair * NC + who) * 8, 8), 8), :]
            out_ref[pair, :8, :] = block[:, : 4 * HD]
            out_ref[pair, 8:, :] = block[:, 4 * HD :]


def terms_out(core, at, gated_t, cots, keep, send):
    width = cots[0].shape[1]
    whole = lambda a: pl.BlockSpec(a.shape, lambda g: (0,) * a.ndim)
    out_spec = pl.BlockSpec((NY * NXH, 16, 4 * HD), lambda g: (0, 4, 0))
    return pl.pallas_call(
        terms_out_kernel,
        grid=(1,),
        in_specs=[smem(), smem(), whole(gated_t)]
        + [whole(c) for c in cots]
        + [pl.BlockSpec(memory_space=pl.ANY)] * 2,
        out_specs=[out_spec] * 2,
        out_shape=[jax.ShapeDtypeStruct(keep.shape, F32)] * 2,
        scratch_shapes=[pltpu.VMEM((HD, width), F32)],
        input_output_aliases={3 + len(cots): 0, 4 + len(cots): 1},
        compiler_params=params(),
        cost_estimate=pl.CostEstimate(
            flops=2 * HD * width * gated_t.shape[1], bytes_accessed=6 << 20, transcendentals=0
        ),
        name="terms_out",
    )(core, at, gated_t, *cots, keep, send)


def small(kernel, name, scalars, arrays, outs, scratch=()):
    size = sum(a.size * a.dtype.itemsize for a in arrays)
    return pl.pallas_call(
        kernel,
        in_specs=[smem()] + [vmem()] * len(arrays),
        out_specs=[vmem()] * len(outs),
        out_shape=[jax.ShapeDtypeStruct(shape, dtype) for shape, dtype in outs],
        scratch_shapes=list(scratch),
        compiler_params=params(),
        cost_estimate=pl.CostEstimate(flops=size, bytes_accessed=2 * size, transcendentals=0),
        name=name,
    )(scalars, *arrays)


def core_sum_kernel(pos_ref, keep_ref, got_ref, own_ref, one_ref, three_ref, two_ref):
    y = pos_ref[0]
    for d, out_ref in ((0, own_ref), (1, one_ref), (3, three_ref), (2, two_ref)):
        here = pl.ds(((y - d + NY) % NY) * NXH, NXH)
        out_ref[...] = (keep_ref[here] + got_ref[here]).astype(out_ref.dtype)


def y_sum_kernel(pos_ref, own_ref, a_ref, b_ref, c_ref, keep_ref, same_ref, one_ref, two_ref, sum_ref):
    xh, x = pos_ref[1], pos_ref[2]
    sum_ref[...] = own_ref[...] + (
        a_ref[...].astype(F32) + b_ref[...].astype(F32) + c_ref[...].astype(F32)
    )

    def slab(out_ref, h, l):
        for k in range(NZ):
            out_ref[k * 8 : (k + 1) * 8, :] = sum_ref[
                h, pl.ds(pl.multiple_of((k * NX + l) * 8, 8), 8), :
            ]

    slab(keep_ref, xh, x)
    keep_ref[32:, :] = sum_ref[xh, 64:, :]
    slab(same_ref, 1 - xh, x)
    same_ref[32:, :] = sum_ref[1 - xh, 64:, :]
    slab(one_ref, xh, 1 - x)
    slab(two_ref, 1 - xh, 1 - x)


def x_sum_kernel(pos_ref, keep_ref, same_ref, a_ref, b_ref, own_ref, one_ref, three_ref, two_ref, out_ref, sum_ref):
    z, x = pos_ref[3], pos_ref[2]
    mine = keep_ref[...] + same_ref[...]
    sum_ref[x] = mine[:32]
    sum_ref[1 - x] = a_ref[...] + b_ref[...]
    out_ref[...] = mine[32:]
    for d, to_ref in ((0, own_ref), (1, one_ref), (3, three_ref), (2, two_ref)):
        here = pl.ds(pl.multiple_of(((z - d + NZ) % NZ) * 8, 8), 8)
        for l in range(NX):
            to_ref[l * 8 : (l + 1) * 8, :] = sum_ref[l, here, :]


def z_place_kernel(factor, pos_ref, own_ref, one_ref, three_ref, two_ref, out_ref, w_in_ref, w_out_ref):
    z = pos_ref[3]
    for d, ref in ((0, own_ref), (1, one_ref), (3, three_ref), (2, two_ref)):
        for l in range(NX):
            for k in range(4):
                at = pl.multiple_of((k * H + ((z + d) % NZ) * NX + l) * HD, HD)
                w_in_ref[:, pl.ds(at, HD)] = (
                    ref[l * 8 : (l + 1) * 8, k * HD : (k + 1) * HD] * factor
                )
    w_out_ref[:, : 4 * HD] = out_ref[:8] * factor
    w_out_ref[:, 4 * HD :] = out_ref[8:] * factor


def shard_kernel(gated_ref, gate_ref, late_ref, w_in_ref, w_out_ref, hist_ref, cot_ref, layer_ref, grad_ref, acc_ref):
    step = pl.program_id(0)

    def columns(ref):
        return jnp.concatenate([ref[h] for h in range(H)], axis=1)

    @pl.when(step == 0)
    def _():
        hist = hist_ref[...].astype(F32)
        layer_ref[...] = (hist + dot(columns(gated_ref), w_out_ref[...])).astype(BF16)
        acc_ref[...] = dot_nt(columns(gate_ref), w_in_ref[...])

    @pl.when(step > 0)
    def _():
        acc_ref[...] += dot_nt(columns(late_ref), w_in_ref[...])

    @pl.when(step == 3)
    def _():
        normed, inverse = layer_norm(hist_ref[...].astype(F32))
        back = norm_back(normed, inverse, acc_ref[...])
        grad_ref[...] = (cot_ref[...].astype(F32) + back).astype(BF16)


def shard_outputs(early, late, w_in, w_out, hist, cot):
    rows, width = hist.shape
    whole = lambda a: pl.BlockSpec(a.shape, lambda k: (0,) * a.ndim)
    return pl.pallas_call(
        shard_kernel,
        grid=(4,),
        in_specs=[
            pl.BlockSpec((H, rows, HD), lambda k: (0, 0, 0)),
            pl.BlockSpec((H, rows, HD), lambda k: (0, 0, 1)),
            pl.BlockSpec((H, rows, HD), lambda k: (0, 0, jnp.maximum(k - 1, 0))),
            pl.BlockSpec((width, width), lambda k: (0, k)),
            whole(w_out),
            whole(hist),
            whole(cot),
        ],
        out_specs=[whole(hist)] * 2,
        out_shape=[jax.ShapeDtypeStruct(hist.shape, BF16)] * 2,
        scratch_shapes=[pltpu.VMEM((rows, width), F32)],
        compiler_params=params(),
        cost_estimate=pl.CostEstimate(
            flops=10 * rows * width * width, bytes_accessed=14 << 20, transcendentals=0
        ),
        name="shard_outputs",
    )(early, early, late, w_in, w_out, hist, cot)


def local(history, segment_ids, w_in, w_out, cotangent):
    hist = history[0]
    cot = cotangent[0]
    rows, width = hist.shape
    length = rows * NZ * NX
    s = lax.axis_index("seq")
    u = lax.axis_index("user")
    z, x = s // NX, s % NX
    y, xh, core = u // (NXH * NC), (u // NC) % NXH, u % NC

    users = NY * NXH * NC
    tie = lax.optimization_barrier
    w_head = jnp.concatenate(
        [lax.dynamic_slice(w_in, (0, i * width + s * HD), (width, HD)) for i in range(4)], axis=1
    )

    def place_of(key):
        return ((z + key[0]) % NZ) * NX + (x ^ key[1])

    def project(got, outs):
        for key, block in got.items():
            outs = ln_proj(place_of(key).reshape(1), block, w_head, outs)
        return outs

    got = step_one(hist)
    outs = project({(0, 0): hist}, ())
    grad_gated_own = dot_nt(cot, w_out).astype(BF16)
    ids = segment_ids[0].astype(BF16).reshape(2, HD)
    ids = jnp.pad(ids, ((0, 14), (0, 0)))
    to_heads = jnp.concatenate(
        [
            grad_gated_own.reshape(rows, H, HD).transpose(1, 0, 2),
            jnp.broadcast_to(ids[None], (H, 16, HD)),
        ],
        axis=1,
    )
    at_head = lax.all_to_all(to_heads, "seq", 0, 0, tiled=True)
    got, outs = tie((got, outs))
    more = step_two(got)
    outs = project(got, outs)
    more, outs, at_head = tie((more, outs, at_head))
    got.update(more)
    last = step_three(got)
    outs = project(more, outs)
    ids = at_head[:, rows : rows + 2].astype(jnp.int32)
    ids = jnp.concatenate([ids[:, 0], ids[::-1, 1]], axis=0).reshape(1, length)
    start = sum(jnp.where(ids > v, jnp.sum((ids == v).astype(jnp.int32)), 0) for v in range(3))
    first = start[0, ::TQ] // TK
    last, outs, start, first, cot_next = tie((last, outs, start, first, cot))
    cots = {(0, 0): cot}
    fresh = step_one(cot_next)
    normed_t, act, slope = project(last, outs)
    att, gate_t, gg_t, stats = forward(first, act, at_head, start)
    stats, fresh = tie((stats, fresh))
    cots.update(fresh)
    pair = jnp.stack([stats, from_seq(stats, 0, 1)])
    others = [from_seq(pair, dz, 0) for dz in (1, 3, 2)]
    early, grad_out, grad_out_t, gated_t = mix(pair, *others, att, gate_t, gg_t, slope)
    early, grad_out, grad_out_t, cots = tie((early, grad_out, grad_out_t, cots))
    early_back = lax.all_to_all(early, "seq", 0, 0, tiled=True)
    fresh = step_two(cots)
    late = backward(first, act, grad_out, grad_out_t, start, slope)
    late, fresh = tie((late, fresh))
    cots.update(fresh)
    cots.update(step_three(cots))
    late_back = lax.all_to_all(late, "seq", 0, 0, tiled=True)

    at_core = core.reshape(1)
    keep, send = terms_in(at_core, normed_t, early, late)
    places = jnp.stack([place_of(key) for key in ORDER])
    keep, send = terms_out(at_core, places, gated_t, [cots[key] for key in ORDER], keep, send)
    at = jnp.stack([y, xh, x, z])
    n = 4 * HD
    got = from_user(send, 0, 0, 1)
    own, *sends = small(
        core_sum_kernel,
        "core_sum",
        at,
        [keep, got],
        [((NXH, 80, n), F32)] + [((NXH, 80, n), BF16)] * 3,
    )
    sends = [from_user(a, d, 0, 0) for a, d in zip(sends, (1, 3, 2))]
    keep, same, one, two = small(
        y_sum_kernel,
        "y_sum",
        at,
        [own, *sends],
        [((48, n), F32)] * 2 + [((32, n), F32)] * 2,
        [pltpu.VMEM((NXH, 80, n), F32)],
    )
    same = from_both(same, 1, 0)
    one = from_both(one, 0, 1)
    two = from_both(two, 1, 1)
    own, *sends, own_out = small(
        x_sum_kernel,
        "x_sum",
        at,
        [keep, same, one, two],
        [((16, n), F32)] * 5,
        [pltpu.VMEM((NX, 32, n), F32)],
    )
    sends = [from_seq(a, d, 0) for a, d in zip(sends, (1, 3, 2))]
    factor = (length * users) ** (-0.5)
    grad_w_in, grad_w_out = small(
        functools.partial(z_place_kernel, factor),
        "z_place",
        at,
        [own, *sends, own_out],
        [((8, 4 * width), F32), ((8, width), F32)],
    )

    layer_out, grad_history = shard_outputs(early_back, late_back, w_in, w_out, hist, cot)
    return layer_out[None], grad_history[None], grad_w_in, grad_w_out


def solution(mesh):
    in_specs = (P("user", "seq", None), P("user", "seq"), P(), P(), P("user", "seq", None))
    out_specs = (
        P("user", "seq", None),
        P("user", "seq", None),
        P(("seq", "user"), None),
        P(("seq", "user"), None),
    )
    return jax.shard_map(local, mesh=mesh, in_specs=in_specs, out_specs=out_specs, check_vma=False)
```

```python
import functools

import jax
import jax.numpy as jnp
from jax import lax
from jax.experimental import pallas as pl
from jax.experimental.pallas import tpu as pltpu
from jax.sharding import PartitionSpec as P

F32 = jnp.float32
BF16 = jnp.bfloat16
EPS = 1e-05
H = 8
HD = 128
NZ, NX = 4, 2
NY, NXH, NC = 4, 2, 2
ORDER = ((0, 0), (1, 0), (3, 0), (0, 1), (2, 0), (3, 1), (1, 1), (2, 1))


def seq_perm(dz, dx):
    return [
        (((z + dz) % NZ) * NX + (x ^ dx), z * NX + x) for z in range(NZ) for x in range(NX)
    ]


def user_perm(dy, dh, dc):
    return [
        ((((y + dy) % NY) * NXH + (h ^ dh)) * NC + (c ^ dc), (y * NXH + h) * NC + c)
        for y in range(NY)
        for h in range(NXH)
        for c in range(NC)
    ]


def from_seq(a, dz, dx):
    return lax.ppermute(a, "seq", seq_perm(dz, dx))


def from_user(a, dy, dh, dc):
    return lax.ppermute(a, "user", user_perm(dy, dh, dc))


def from_both(a, dh, dx):
    pairs = []
    for s in range(NZ * NX):
        for u in range(NY * NXH * NC):
            pairs.append(((s ^ dx) * NY * NXH * NC + (u ^ (dh * NC)), s * NY * NXH * NC + u))
    return lax.ppermute(a, ("seq", "user"), pairs)


def step_one(block):
    return {
        (1, 0): from_seq(block, 1, 0),
        (3, 0): from_seq(block, 3, 0),
        (0, 1): from_seq(block, 0, 1),
    }


def step_two(got):
    return {
        (2, 0): from_seq(got[1, 0], 1, 0),
        (3, 1): from_seq(got[0, 1], 3, 0),
        (1, 1): from_seq(got[1, 0], 0, 1),
    }


def step_three(got, a=96, b=176):
    return {
        (2, 1): jnp.concatenate(
            [
                from_seq(got[2, 0][:a], 0, 1),
                from_seq(got[1, 1][a:b], 1, 0),
                from_seq(got[3, 1][b:], 3, 0),
            ],
            axis=0,
        )
    }


def layer_norm(entries):
    centre = jnp.mean(entries, axis=-1, keepdims=True)
    centred = entries - centre
    inverse = lax.rsqrt(jnp.mean(centred * centred, axis=-1, keepdims=True) + EPS)
    return centred * inverse, inverse


def norm_back(normed, inverse, upstream):
    first_term = jnp.mean(upstream, axis=-1, keepdims=True)
    second_term = jnp.mean(upstream * normed, axis=-1, keepdims=True)
    return inverse * (upstream - first_term - normed * second_term)


def dot(a, b):
    return jnp.dot(a, b, preferred_element_type=F32)


def dot_nt(a, b):
    return lax.dot_general(a, b, (((1,), (1,)), ((), ())), preferred_element_type=F32)


def dot_tn(a, b):
    return lax.dot_general(a, b, (((0,), (0,)), ((), ())), preferred_element_type=F32)


LIMIT = 56


def params(limit):
    return pltpu.CompilerParams(vmem_limit_bytes=limit << 20)


def ln_proj_kernel(count, at_ref, *refs):
    w_ref = refs[count]
    normed_ref, act_ref, slope_ref = refs[-3:]
    half = act_ref.shape[2]
    for k in range(count):

        @pl.when(pl.program_id(0) == k)
        def _():
            normed, _ = layer_norm(refs[k][...].astype(F32))
            normed_b = normed.astype(BF16)
            normed_ref[...] = normed_b.T
            projected = dot(normed_b, w_ref[...])
            tanh = jnp.tanh(0.5 * projected)
            sig = 0.5 + 0.5 * tanh
            silu = projected * sig
            act = silu.astype(BF16)
            slope = sig + silu * (1.0 - sig)
            for i in range(2):
                act_ref[i, 0] = act[i * half : (i + 1) * half]
                slope_ref[i, 0] = slope[i * half : (i + 1) * half]


def ln_proj(at, blocks, w_head, outs):
    rows, width = blocks[0].shape
    cols = w_head.shape[1]
    half, shards = rows // 2, NZ * NX
    by_half = pl.BlockSpec((2, 1, half, cols), lambda i, at_ref: (0, at_ref[i], 0, 0))
    in_specs = [pl.BlockSpec((rows, width), lambda i, at_ref: (0, 0))] * len(blocks)
    in_specs.append(pl.BlockSpec((width, cols), lambda i, at_ref: (0, 0)))
    aliases = {}
    if outs:
        in_specs += [pl.BlockSpec(memory_space=pl.ANY)] * 3
        aliases = {len(in_specs) + k - 2: k for k in range(3)}
    return pl.pallas_call(
        functools.partial(ln_proj_kernel, len(blocks)),
        grid_spec=pltpu.PrefetchScalarGridSpec(
            num_scalar_prefetch=1,
            grid=(len(blocks),),
            in_specs=in_specs,
            out_specs=(
                pl.BlockSpec((width, rows), lambda i, at_ref: (0, at_ref[i])),
                by_half,
                by_half,
            ),
        ),
        out_shape=(
            jax.ShapeDtypeStruct((width, rows * shards), BF16),
            jax.ShapeDtypeStruct((2, shards, half, cols), BF16),
            jax.ShapeDtypeStruct((2, shards, half, cols), F32),
        ),
        input_output_aliases=aliases,
        compiler_params=params(LIMIT),
        cost_estimate=pl.CostEstimate(
            flops=2 * rows * width * cols * len(blocks),
            bytes_accessed=3 * len(blocks) << 20,
            transcendentals=rows * cols * len(blocks),
        ),
        name="ln_proj",
    )(at, *blocks, w_head, *outs)


FQ, FK = 512, 512
BQ, BK = 256, 256
TM = 256
SCALE = HD ** (-0.5)


def tile_place(block):
    last = 2 * NZ * NX - 1
    return (block, 0) if block < NZ * NX else (last - block, HD)


def time_rows(ref, first, count, column, columns=1):
    parts = []
    for block in range(first // HD, (first + count) // HD):
        shard, row = tile_place(block)
        parts.append(ref[row // HD, shard, :, column * HD : (column + columns) * HD])
    return parts[0] if len(parts) == 1 else jnp.concatenate(parts, axis=0)


def tiles(length, rows, cols):
    key_row = lax.broadcasted_iota(jnp.int32, (cols, rows), 0)
    query_col = lax.broadcasted_iota(jnp.int32, (1, rows), 1)

    def seen(i, j, start):
        mask = key_row >= start - j
        if j + cols > i:
            mask = mask & (key_row <= query_col + (i - j))
        return mask

    return [(i, range(0, i + rows, cols)) for i in range(0, length, rows)], seen


def forward_kernel(act_ref, head_ref, start_ref, att_ref, gate_ref, gg_ref, stats_ref):
    length = att_ref.shape[1]
    values_t = [time_rows(act_ref, j, FK, 1).T for j in range(0, length, FK)]
    keys = [time_rows(act_ref, j, FK, 3) for j in range(0, length, FK)]
    queries_in, seen = tiles(length, FQ, FK)
    for i, keys_in in queries_in:
        at = slice(i, i + FQ)
        queries = time_rows(act_ref, i, FQ, 2)
        start = start_ref[:, at]
        total = None
        for j in keys_in:
            half = dot_nt(keys[j // FK], queries) * (0.5 * SCALE)
            weights = half + half * jnp.tanh(half)
            weights = jnp.where(seen(i, j, start), weights, 0.0).astype(BF16)
            term = dot(values_t[j // FK], weights)
            total = term if total is None else total + term
        att_ref[:, at] = total
        gate = time_rows(act_ref, i, FQ, 0).T
        parts = []
        for block in range(i // HD, (i + FQ) // HD):
            shard, row = tile_place(block)
            parts.append(head_ref[shard, row : row + HD, :])
        gg = jnp.concatenate(parts, axis=0).T
        gate_ref[:, at] = gate
        gg_ref[:, at] = gg
        grad_mixed = gg.astype(F32) * gate.astype(F32)
        mean = jnp.sum(total, axis=0, keepdims=True) * (1.0 / HD)
        centred = total - mean
        stats_ref[0:1, at] = mean
        stats_ref[1:2, at] = jnp.sum(centred * centred, axis=0, keepdims=True)
        stats_ref[2:3, at] = jnp.sum(grad_mixed, axis=0, keepdims=True)
        stats_ref[3:4, at] = jnp.sum(grad_mixed * centred, axis=0, keepdims=True)


def vmem():
    return pl.BlockSpec(memory_space=pltpu.VMEM)


def smem():
    return pl.BlockSpec(memory_space=pltpu.SMEM)


def forward(act, at_head, start):
    length = start.shape[1]
    return pl.pallas_call(
        forward_kernel,
        in_specs=[vmem()] * 3,
        out_specs=[vmem()] * 4,
        out_shape=(
            jax.ShapeDtypeStruct((HD, length), F32),
            jax.ShapeDtypeStruct((HD, length), BF16),
            jax.ShapeDtypeStruct((HD, length), BF16),
            jax.ShapeDtypeStruct((4, length), F32),
        ),
        compiler_params=params(LIMIT),
        cost_estimate=pl.CostEstimate(
            flops=8 * HD * length * length, bytes_accessed=6 << 20, transcendentals=length * length // 2
        ),
        name="attention_forward",
    )(act, at_head, start)


def mix_kernel(own_ref, one_ref, three_ref, two_ref, att_ref, gate_ref, gg_ref, slope_ref, early_ref, go_ref, got_ref, gated_ref):
    length = att_ref.shape[1]
    width = H * HD
    heads = [ref[k] for ref in (own_ref, one_ref, three_ref, two_ref) for k in range(NX)]
    mean_all = sum(a[0:1] for a in heads) * (1.0 / H)
    apart = [a[0:1] - mean_all for a in heads]
    spread = sum(a[1:2] for a in heads) + HD * sum(d * d for d in apart)
    inverse_all = lax.rsqrt(spread * (1.0 / width) + EPS)
    first_all = sum(a[2:3] for a in heads) * (1.0 / width)
    second_all = inverse_all * sum(a[3:4] + d * a[2:3] for a, d in zip(heads, apart)) * (1.0 / width)
    for i in range(length // TM):
        at = slice(i * TM, (i + 1) * TM)
        gate = gate_ref[:, at].astype(F32)
        gg = gg_ref[:, at].astype(F32)
        inverse = inverse_all[:, at]
        mixed = (att_ref[:, at] - mean_all[:, at]) * inverse
        grad_att = inverse * (gg * gate - first_all[:, at] - mixed * second_all[:, at])
        got_ref[:, at] = grad_att.astype(BF16)
        go_ref[at, :] = grad_att.T.astype(BF16)
        gated_t = (mixed * gate).astype(BF16)
        gated = gated_t.T
        grad_u = (gg * mixed).T * time_rows(slope_ref, i * TM, TM, 0)
        for k in range(TM // HD):
            shard, row = tile_place(i * TM // HD + k)
            stored = slice(2 * HD * shard + row, 2 * HD * shard + row + HD)
            gated_ref[:, stored] = gated_t[:, k * HD : (k + 1) * HD]
            early_ref[shard, row : row + HD, :HD] = gated[k * HD : (k + 1) * HD]
            early_ref[shard, row : row + HD, HD:] = grad_u[k * HD : (k + 1) * HD].astype(BF16)


def mix(own, one, three, two, att, gate, gg, slope):
    length = att.shape[1]
    shards = NZ * NX
    whole = lambda shape: pl.BlockSpec(shape, lambda i: (0,) * len(shape))
    return pl.pallas_call(
        mix_kernel,
        grid=(1,),
        in_specs=[whole(own.shape)] * 4
        + [whole(att.shape)] * 3
        + [pl.BlockSpec(slope.shape[:3] + (HD,), lambda i: (0, 0, 0, 0))],
        out_specs=[whole((shards, length // shards, 2 * HD)), whole((length, HD))]
        + [whole((HD, length))] * 2,
        out_shape=(
            jax.ShapeDtypeStruct((shards, length // shards, 2 * HD), BF16),
            jax.ShapeDtypeStruct((length, HD), BF16),
            jax.ShapeDtypeStruct((HD, length), BF16),
            jax.ShapeDtypeStruct((HD, length), BF16),
        ),
        compiler_params=params(LIMIT),
        cost_estimate=pl.CostEstimate(flops=20 * HD * length, bytes_accessed=6 << 20, transcendentals=0),
        name="mix",
    )(own, one, three, two, att, gate, gg, slope)


def backward_kernel(act_ref, go_ref, got_ref, start_ref, slope_ref, late_ref, dk_ref, dv_ref):
    length = go_ref.shape[0]
    keys = [time_rows(act_ref, j, BK, 3) for j in range(0, length, BK)]
    keys_t = [k.T for k in keys]
    values = [time_rows(act_ref, j, BK, 1) for j in range(0, length, BK)]
    queries_in, seen = tiles(length, BQ, BK)

    def put(first, column, value):
        value = (value * time_rows(slope_ref, first, value.shape[0], column + 1)).astype(BF16)
        for k in range(value.shape[0] // HD):
            shard, row = tile_place(first // HD + k)
            late_ref[shard, row : row + HD, column * HD : (column + 1) * HD] = value[
                k * HD : (k + 1) * HD
            ]

    started = set()
    for i, keys_in in queries_in:
        at = slice(i, i + BQ)
        queries = time_rows(act_ref, i, BQ, 2)
        grad_out = go_ref[at, :]
        grad_out_t = got_ref[:, at]
        start = start_ref[:, at]
        total = None
        for j in keys_in:
            here = slice(j, j + BK)
            half = dot_nt(keys[j // BK], queries) * (0.5 * SCALE)
            tanh = jnp.tanh(half)
            weights = half + half * tanh
            sig = 0.5 + 0.5 * tanh
            slope = sig + weights * (1.0 - sig)
            mask = seen(i, j, start)
            ahead = dot(values[j // BK], grad_out_t)
            weights = jnp.where(mask, weights, 0.0).astype(BF16)
            slopes = jnp.where(mask, ahead * slope, 0.0).astype(BF16)
            dv = dot(weights, grad_out)
            dk = dot(slopes, queries)
            if j in started:
                dv_ref[here, :] += dv
                dk_ref[here, :] += dk
            else:
                dv_ref[here, :] = dv
                dk_ref[here, :] = dk
                started.add(j)
            term = dot(keys_t[j // BK], slopes)
            total = term if total is None else total + term
        put(i, 1, total.T * SCALE)
    for j in range(0, length, BK):
        put(j, 0, dv_ref[j : j + BK, :])
        put(j, 2, dk_ref[j : j + BK, :] * SCALE)


def backward(act, grad_out, grad_out_t, start, slope):
    length = start.shape[1]
    shards = NZ * NX
    return pl.pallas_call(
        backward_kernel,
        in_specs=[vmem()] * 5,
        out_specs=vmem(),
        out_shape=jax.ShapeDtypeStruct((shards, length // shards, 3 * HD), BF16),
        scratch_shapes=[pltpu.VMEM((length, HD), F32)] * 2,
        compiler_params=params(LIMIT),
        cost_estimate=pl.CostEstimate(
            flops=15 * HD * length * length, bytes_accessed=10 << 20, transcendentals=length * length // 2
        ),
        name="attention_backward",
    )(act, grad_out, grad_out_t, start, slope)


def terms_in_kernel(core_ref, normed_ref, gate_ref, late_ref, keep_ref, send_ref, res_ref, grad_ref):
    shards, rows, _ = gate_ref.shape

    @pl.when(pl.program_id(0) == 0)
    def _():
        grad_ref[:, :HD] = gate_ref[...].reshape(shards * rows, HD)
        grad_ref[:, HD:] = late_ref[...].reshape(shards * rows, 3 * HD)

    res_ref[...] = dot(normed_ref[...], grad_ref[...])
    core = core_ref[0]
    for k in range(res_ref.shape[0] // HD):
        for pair in range(NY * NXH):
            mine = pl.multiple_of(k * HD + (pair * NC + core) * 8, 8)
            other = pl.multiple_of(k * HD + (pair * NC + 1 - core) * 8, 8)
            keep_ref[pair, k * 8 : (k + 1) * 8, :] = res_ref[pl.ds(mine, 8), :]
            send_ref[pair, k * 8 : (k + 1) * 8, :] = res_ref[pl.ds(other, 8), :]


def terms_in(core, normed_t, early, late):
    width, length = normed_t.shape
    shards, rows, _ = early.shape
    shape = jax.ShapeDtypeStruct((NY * NXH, 80, 4 * HD), F32)
    out_spec = pl.BlockSpec((NY * NXH, 16, 4 * HD), lambda g: (0, g, 0))
    return pl.pallas_call(
        terms_in_kernel,
        grid=(4,),
        in_specs=[
            smem(),
            pl.BlockSpec((width // 4, length), lambda g: (g, 0)),
            pl.BlockSpec((shards, rows, HD), lambda g: (0, 0, 1)),
            pl.BlockSpec((shards, rows, 3 * HD), lambda g: (0, 0, 0)),
        ],
        out_specs=[out_spec] * 2,
        out_shape=[shape] * 2,
        scratch_shapes=[pltpu.VMEM((width // 4, 4 * HD), F32), pltpu.VMEM((length, 4 * HD), BF16)],
        compiler_params=params(LIMIT),
        cost_estimate=pl.CostEstimate(
            flops=2 * width * length * 4 * HD, bytes_accessed=9 << 20, transcendentals=0
        ),
        name="terms_in",
    )(core, normed_t, early, late)


def terms_out_kernel(core_ref, at_ref, gated_ref, *refs):
    cots = refs[: NZ * NX]
    keep_ref, send_ref, res_ref = refs[-3:]
    rows = cots[0].shape[0]
    total = None
    for r, cot_ref in enumerate(cots):
        here = pl.ds(pl.multiple_of(at_ref[r] * rows, rows), rows)
        term = dot(gated_ref[:, here], cot_ref[...])
        total = term if total is None else total + term
    res_ref[...] = total
    core = core_ref[0]
    for pair in range(NY * NXH):
        for out_ref, who in ((keep_ref, core), (send_ref, 1 - core)):
            block = res_ref[pl.ds(pl.multiple_of((pair * NC + who) * 8, 8), 8), :]
            out_ref[pair, :8, :] = block[:, : 4 * HD]
            out_ref[pair, 8:, :] = block[:, 4 * HD :]


def terms_out(core, at, gated_t, cots, keep, send):
    width = cots[0].shape[1]
    whole = lambda a: pl.BlockSpec(a.shape, lambda g: (0,) * a.ndim)
    out_spec = pl.BlockSpec((NY * NXH, 16, 4 * HD), lambda g: (0, 4, 0))
    return pl.pallas_call(
        terms_out_kernel,
        grid=(1,),
        in_specs=[smem(), smem(), whole(gated_t)]
        + [whole(c) for c in cots]
        + [pl.BlockSpec(memory_space=pl.ANY)] * 2,
        out_specs=[out_spec] * 2,
        out_shape=[jax.ShapeDtypeStruct(keep.shape, F32)] * 2,
        scratch_shapes=[pltpu.VMEM((HD, width), F32)],
        input_output_aliases={3 + len(cots): 0, 4 + len(cots): 1},
        compiler_params=params(LIMIT),
        cost_estimate=pl.CostEstimate(
            flops=2 * HD * width * gated_t.shape[1], bytes_accessed=6 << 20, transcendentals=0
        ),
        name="terms_out",
    )(core, at, gated_t, *cots, keep, send)


def small(kernel, name, scalars, arrays, outs, scratch=(), limit=12):
    size = sum(a.size * a.dtype.itemsize for a in arrays)
    return pl.pallas_call(
        kernel,
        in_specs=[smem()] + [vmem()] * len(arrays),
        out_specs=[vmem()] * len(outs),
        out_shape=[jax.ShapeDtypeStruct(shape, dtype) for shape, dtype in outs],
        scratch_shapes=list(scratch),
        compiler_params=params(limit),
        cost_estimate=pl.CostEstimate(flops=size, bytes_accessed=2 * size, transcendentals=0),
        name=name,
    )(scalars, *arrays)


def core_sum_kernel(pos_ref, keep_ref, got_ref, own_ref, one_ref, three_ref, two_ref):
    y = pos_ref[0]
    for d, out_ref in ((0, own_ref), (1, one_ref), (3, three_ref), (2, two_ref)):
        here = pl.ds(((y - d + NY) % NY) * NXH, NXH)
        out_ref[...] = (keep_ref[here] + got_ref[here]).astype(out_ref.dtype)


def y_sum_kernel(pos_ref, own_ref, a_ref, b_ref, c_ref, keep_ref, same_ref, one_ref, two_ref, sum_ref):
    xh, x = pos_ref[1], pos_ref[2]
    sum_ref[...] = own_ref[...] + (
        a_ref[...].astype(F32) + b_ref[...].astype(F32) + c_ref[...].astype(F32)
    )

    def slab(out_ref, h, l):
        for k in range(NZ):
            out_ref[k * 8 : (k + 1) * 8, :] = sum_ref[
                h, pl.ds(pl.multiple_of((k * NX + l) * 8, 8), 8), :
            ]

    slab(keep_ref, xh, x)
    keep_ref[32:, :] = sum_ref[xh, 64:, :]
    slab(same_ref, 1 - xh, x)
    same_ref[32:, :] = sum_ref[1 - xh, 64:, :]
    slab(one_ref, xh, 1 - x)
    slab(two_ref, 1 - xh, 1 - x)


def x_sum_kernel(pos_ref, keep_ref, same_ref, a_ref, b_ref, own_ref, one_ref, three_ref, two_ref, out_ref, sum_ref):
    z, x = pos_ref[3], pos_ref[2]
    mine = keep_ref[...] + same_ref[...]
    sum_ref[x] = mine[:32]
    sum_ref[1 - x] = a_ref[...] + b_ref[...]
    out_ref[...] = mine[32:]
    for d, to_ref in ((0, own_ref), (1, one_ref), (3, three_ref), (2, two_ref)):
        here = pl.ds(pl.multiple_of(((z - d + NZ) % NZ) * 8, 8), 8)
        for l in range(NX):
            to_ref[l * 8 : (l + 1) * 8, :] = sum_ref[l, here, :]


def z_place_kernel(factor, pos_ref, own_ref, one_ref, three_ref, two_ref, out_ref, w_in_ref, w_out_ref):
    z = pos_ref[3]
    for d, ref in ((0, own_ref), (1, one_ref), (3, three_ref), (2, two_ref)):
        for l in range(NX):
            for k in range(4):
                at = pl.multiple_of((k * H + ((z + d) % NZ) * NX + l) * HD, HD)
                w_in_ref[:, pl.ds(at, HD)] = (
                    ref[l * 8 : (l + 1) * 8, k * HD : (k + 1) * HD] * factor
                )
    w_out_ref[:, : 4 * HD] = out_ref[:8] * factor
    w_out_ref[:, 4 * HD :] = out_ref[8:] * factor


def shard_kernel(gated_ref, gate_ref, late_ref, w_in_ref, w_out_ref, hist_ref, cot_ref, layer_ref, grad_ref, acc_ref):
    step = pl.program_id(0)

    def columns(ref):
        return jnp.concatenate([ref[h] for h in range(H)], axis=1)

    @pl.when(step == 0)
    def _():
        hist = hist_ref[...].astype(F32)
        layer_ref[...] = (hist + dot(columns(gated_ref), w_out_ref[...])).astype(BF16)
        acc_ref[...] = dot_nt(columns(gate_ref), w_in_ref[...])

    @pl.when(step > 0)
    def _():
        acc_ref[...] += dot_nt(columns(late_ref), w_in_ref[...])

    @pl.when(step == 3)
    def _():
        normed, inverse = layer_norm(hist_ref[...].astype(F32))
        back = norm_back(normed, inverse, acc_ref[...])
        grad_ref[...] = (cot_ref[...].astype(F32) + back).astype(BF16)


def shard_outputs(early, late, w_in, w_out, hist, cot):
    rows, width = hist.shape
    whole = lambda a: pl.BlockSpec(a.shape, lambda k: (0,) * a.ndim)
    return pl.pallas_call(
        shard_kernel,
        grid=(4,),
        in_specs=[
            pl.BlockSpec((H, rows, HD), lambda k: (0, 0, 0)),
            pl.BlockSpec((H, rows, HD), lambda k: (0, 0, 1)),
            pl.BlockSpec((H, rows, HD), lambda k: (0, 0, jnp.maximum(k - 1, 0))),
            pl.BlockSpec((width, width), lambda k: (0, k)),
            whole(w_out),
            whole(hist),
            whole(cot),
        ],
        out_specs=[whole(hist)] * 2,
        out_shape=[jax.ShapeDtypeStruct(hist.shape, BF16)] * 2,
        scratch_shapes=[pltpu.VMEM((rows, width), F32)],
        compiler_params=params(LIMIT),
        cost_estimate=pl.CostEstimate(
            flops=10 * rows * width * width, bytes_accessed=14 << 20, transcendentals=0
        ),
        name="shard_outputs",
    )(early, early, late, w_in, w_out, hist, cot)


def local(history, segment_ids, w_in, w_out, cotangent):
    hist = history[0]
    cot = cotangent[0]
    rows, width = hist.shape
    length = rows * NZ * NX
    s = lax.axis_index("seq")
    u = lax.axis_index("user")
    z, x = s // NX, s % NX
    y, xh, core = u // (NXH * NC), (u // NC) % NXH, u % NC

    users = NY * NXH * NC
    tie = lax.optimization_barrier
    w_head = jnp.concatenate(
        [lax.dynamic_slice(w_in, (0, i * width + s * HD), (width, HD)) for i in range(4)], axis=1
    )

    def place_of(key):
        return ((z + key[0]) % NZ) * NX + (x ^ key[1])

    def project(got, outs):
        at = jnp.stack([place_of(key) for key in got])
        return ln_proj(at, list(got.values()), w_head, outs)

    got = step_one(hist)
    outs = project({(0, 0): hist}, ())
    grad_gated_own = dot_nt(cot, w_out).astype(BF16)
    ids = segment_ids[0].astype(BF16).reshape(2, HD)
    ids = jnp.pad(ids, ((0, 14), (0, 0)))
    to_heads = jnp.concatenate(
        [
            grad_gated_own.reshape(rows, H, HD).transpose(1, 0, 2),
            jnp.broadcast_to(ids[None], (H, 16, HD)),
        ],
        axis=1,
    )
    at_head = lax.all_to_all(to_heads, "seq", 0, 0, tiled=True)
    got, outs = tie((got, outs))
    more = step_two(got)
    outs = project(got, outs)
    more, outs = tie((more, outs))
    got.update(more)
    last = step_three(got)
    outs = project(more, outs)
    ids = at_head[:, rows : rows + 2].astype(jnp.int32)
    ids = jnp.concatenate([ids[:, 0], ids[::-1, 1]], axis=0).reshape(1, length)
    start = sum(jnp.where(ids > v, jnp.sum((ids == v).astype(jnp.int32)), 0) for v in range(3))
    last, outs, start, at_head, cot_next = tie((last, outs, start, at_head, cot))
    cots = step_one(cot_next)
    normed_t, act, slope = project(last, outs)
    att, gate_t, gg_t, stats = forward(act, at_head, start)
    stats, cots = tie((stats, cots))
    cots[0, 0] = cot
    pair = jnp.stack([stats, from_seq(stats, 0, 1)])
    others = [from_seq(pair, dz, 0) for dz in (1, 3, 2)]
    early, grad_out, grad_out_t, gated_t = mix(pair, *others, att, gate_t, gg_t, slope)
    early, grad_out, grad_out_t, cots = tie((early, grad_out, grad_out_t, cots))
    early_back = lax.all_to_all(early, "seq", 0, 0, tiled=True)
    fresh = step_two(cots)
    late = backward(act, grad_out, grad_out_t, start, slope)
    late, fresh = tie((late, fresh))
    cots.update(fresh)
    cots.update(step_three(cots))
    late_back = lax.all_to_all(late, "seq", 0, 0, tiled=True)

    at_core = core.reshape(1)
    keep, send = terms_in(at_core, normed_t, early, late)
    places = jnp.stack([place_of(key) for key in ORDER])
    keep, send = terms_out(at_core, places, gated_t, [cots[key] for key in ORDER], keep, send)
    at = jnp.stack([y, xh, x, z])
    n = 4 * HD
    got = from_user(send, 0, 0, 1)
    own, *sends = small(
        core_sum_kernel,
        "core_sum",
        at,
        [keep, got],
        [((NXH, 80, n), F32)] + [((NXH, 80, n), BF16)] * 3,
        limit=LIMIT,
    )
    early_back, late_back, own, sends = tie((early_back, late_back, own, sends))
    sends = [from_user(a, d, 0, 0) for a, d in zip(sends, (1, 3, 2))]
    layer_out, grad_history = shard_outputs(early_back, late_back, w_in, w_out, hist, cot)
    sends, layer_out, grad_history = tie((sends, layer_out, grad_history))
    keep, same, one, two = small(
        y_sum_kernel,
        "y_sum",
        at,
        [own, *sends],
        [((48, n), F32)] * 2 + [((32, n), F32)] * 2,
        [pltpu.VMEM((NXH, 80, n), F32)],
    )
    same = from_both(same, 1, 0)
    one = from_both(one, 0, 1)
    two = from_both(two, 1, 1)
    own, *sends, own_out = small(
        x_sum_kernel,
        "x_sum",
        at,
        [keep, same, one, two],
        [((16, n), F32)] * 5,
        [pltpu.VMEM((NX, 32, n), F32)],
    )
    sends = [from_seq(a, d, 0) for a, d in zip(sends, (1, 3, 2))]
    factor = (length * users) ** (-0.5)
    grad_w_in, grad_w_out = small(
        functools.partial(z_place_kernel, factor),
        "z_place",
        at,
        [own, *sends, own_out],
        [((8, 4 * width), F32), ((8, width), F32)],
    )
    return layer_out[None], grad_history[None], grad_w_in, grad_w_out


def solution(mesh):
    in_specs = (P("user", "seq", None), P("user", "seq"), P(), P(), P("user", "seq", None))
    out_specs = (
        P("user", "seq", None),
        P("user", "seq", None),
        P(("seq", "user"), None),
        P(("seq", "user"), None),
    )
    return jax.shard_map(local, mesh=mesh, in_specs=in_specs, out_specs=out_specs, check_vma=False)
```

```python
import functools

import jax
import jax.numpy as jnp
from jax import lax
from jax.experimental import pallas as pl
from jax.experimental.pallas import tpu as pltpu
from jax.sharding import PartitionSpec as P

F32 = jnp.float32
BF16 = jnp.bfloat16
EPS = 1e-05
H = 8
HD = 128
NZ, NX = 4, 2
NY, NXH, NC = 4, 2, 2


def seq_perm(dz, dx):
    return [
        (((z + dz) % NZ) * NX + (x ^ dx), z * NX + x) for z in range(NZ) for x in range(NX)
    ]


def user_perm(dy, dh, dc):
    return [
        ((((y + dy) % NY) * NXH + (h ^ dh)) * NC + (c ^ dc), (y * NXH + h) * NC + c)
        for y in range(NY)
        for h in range(NXH)
        for c in range(NC)
    ]


def from_seq(a, dz, dx):
    return lax.ppermute(a, "seq", seq_perm(dz, dx))


def from_user(a, dy, dh, dc):
    return lax.ppermute(a, "user", user_perm(dy, dh, dc))


def from_both(a, dh, dx):
    pairs = []
    for s in range(NZ * NX):
        for u in range(NY * NXH * NC):
            pairs.append(((s ^ dx) * NY * NXH * NC + (u ^ (dh * NC)), s * NY * NXH * NC + u))
    return lax.ppermute(a, ("seq", "user"), pairs)


def step_one(block):
    return {
        (1, 0): from_seq(block, 1, 0),
        (3, 0): from_seq(block, 3, 0),
        (0, 1): from_seq(block, 0, 1),
    }


def step_two(got):
    return {
        (2, 0): from_seq(got[1, 0], 1, 0),
        (3, 1): from_seq(got[0, 1], 3, 0),
        (1, 1): from_seq(got[1, 0], 0, 1),
    }


def step_three(got, a=96, b=176):
    return {
        (2, 1): jnp.concatenate(
            [
                from_seq(got[2, 0][:a], 0, 1),
                from_seq(got[1, 1][a:b], 1, 0),
                from_seq(got[3, 1][b:], 3, 0),
            ],
            axis=0,
        )
    }


def layer_norm(entries):
    centre = jnp.mean(entries, axis=-1, keepdims=True)
    centred = entries - centre
    inverse = lax.rsqrt(jnp.mean(centred * centred, axis=-1, keepdims=True) + EPS)
    return centred * inverse, inverse


def norm_back(normed, inverse, upstream):
    first_term = jnp.mean(upstream, axis=-1, keepdims=True)
    second_term = jnp.mean(upstream * normed, axis=-1, keepdims=True)
    return inverse * (upstream - first_term - normed * second_term)


def dot(a, b):
    return jnp.dot(a, b, preferred_element_type=F32)


def dot_nt(a, b):
    return lax.dot_general(a, b, (((1,), (1,)), ((), ())), preferred_element_type=F32)


def dot_tn(a, b):
    return lax.dot_general(a, b, (((0,), (0,)), ((), ())), preferred_element_type=F32)


LIMIT = 56


def params(limit):
    return pltpu.CompilerParams(vmem_limit_bytes=limit << 20)


def ln_proj_kernel(count, at_ref, *refs):
    w_ref = refs[count]
    normed_ref, act_ref, slope_ref = refs[-3:]
    half = act_ref.shape[2]
    for k in range(count):

        @pl.when(pl.program_id(0) == k)
        def _():
            normed, _ = layer_norm(refs[k][...].astype(F32))
            normed_b = normed.astype(BF16)
            normed_ref[...] = normed_b.T
            projected = dot(normed_b, w_ref[...])
            tanh = jnp.tanh(0.5 * projected)
            sig = 0.5 + 0.5 * tanh
            silu = projected * sig
            act = silu.astype(BF16)
            slope = sig + silu * (1.0 - sig)
            for i in range(2):
                act_ref[i, 0] = act[i * half : (i + 1) * half]
                slope_ref[i, 0] = slope[i * half : (i + 1) * half]


def ln_proj(at, blocks, w_head, outs):
    rows, width = blocks[0].shape
    cols = w_head.shape[1]
    half, shards = rows // 2, NZ * NX
    by_half = pl.BlockSpec((2, 1, half, cols), lambda i, at_ref: (0, at_ref[i], 0, 0))
    in_specs = [pl.BlockSpec((rows, width), lambda i, at_ref: (0, 0))] * len(blocks)
    in_specs.append(pl.BlockSpec((width, cols), lambda i, at_ref: (0, 0)))
    aliases = {}
    if outs:
        in_specs += [pl.BlockSpec(memory_space=pl.ANY)] * 3
        aliases = {len(in_specs) + k - 2: k for k in range(3)}
    return pl.pallas_call(
        functools.partial(ln_proj_kernel, len(blocks)),
        grid_spec=pltpu.PrefetchScalarGridSpec(
            num_scalar_prefetch=1,
            grid=(len(blocks),),
            in_specs=in_specs,
            out_specs=(
                pl.BlockSpec((width, rows), lambda i, at_ref: (0, at_ref[i])),
                by_half,
                by_half,
            ),
        ),
        out_shape=(
            jax.ShapeDtypeStruct((width, rows * shards), BF16),
            jax.ShapeDtypeStruct((2, shards, half, cols), BF16),
            jax.ShapeDtypeStruct((2, shards, half, cols), F32),
        ),
        input_output_aliases=aliases,
        compiler_params=params(LIMIT),
        cost_estimate=pl.CostEstimate(
            flops=2 * rows * width * cols * len(blocks),
            bytes_accessed=3 * len(blocks) << 20,
            transcendentals=rows * cols * len(blocks),
        ),
        name="ln_proj",
    )(at, *blocks, w_head, *outs)


FQ, FK = 512, 512
BQ, BK = 256, 256
SCALE = HD ** (-0.5)


def tile_place(block):
    last = 2 * NZ * NX - 1
    return (block, 0) if block < NZ * NX else (last - block, HD)


def time_rows(ref, first, count, column, columns=1):
    parts = []
    for block in range(first // HD, (first + count) // HD):
        shard, row = tile_place(block)
        parts.append(ref[row // HD, shard, :, column * HD : (column + columns) * HD])
    return parts[0] if len(parts) == 1 else jnp.concatenate(parts, axis=0)


def tiles(length, rows, cols):
    key_row = lax.broadcasted_iota(jnp.int32, (cols, rows), 0)
    query_col = lax.broadcasted_iota(jnp.int32, (1, rows), 1)

    def seen(i, j, start):
        mask = key_row >= start - j
        if j + cols > i:
            mask = mask & (key_row <= query_col + (i - j))
        return mask

    return [(i, range(0, i + rows, cols)) for i in range(0, length, rows)], seen


def forward_kernel(act_ref, head_ref, start_ref, att_ref, gate_ref, gg_ref, stats_ref):
    length = att_ref.shape[1]
    values_t = [time_rows(act_ref, j, FK, 1).T for j in range(0, length, FK)]
    keys = [time_rows(act_ref, j, FK, 3) for j in range(0, length, FK)]
    queries_in, seen = tiles(length, FQ, FK)
    for i, keys_in in queries_in:
        at = slice(i, i + FQ)
        queries = time_rows(act_ref, i, FQ, 2)
        start = start_ref[:, at]
        total = None
        for j in keys_in:
            half = dot_nt(keys[j // FK], queries) * (0.5 * SCALE)
            weights = half + half * jnp.tanh(half)
            weights = jnp.where(seen(i, j, start), weights, 0.0).astype(BF16)
            term = dot(values_t[j // FK], weights)
            total = term if total is None else total + term
        att_ref[:, at] = total
        gate = time_rows(act_ref, i, FQ, 0).T
        parts = []
        for block in range(i // HD, (i + FQ) // HD):
            shard, row = tile_place(block)
            parts.append(head_ref[shard, row : row + HD, :])
        gg = jnp.concatenate(parts, axis=0).T
        gate_ref[:, at] = gate
        gg_ref[:, at] = gg
        grad_mixed = gg.astype(F32) * gate.astype(F32)
        mean = jnp.sum(total, axis=0, keepdims=True) * (1.0 / HD)
        centred = total - mean
        stats_ref[0:1, at] = mean
        stats_ref[1:2, at] = jnp.sum(centred * centred, axis=0, keepdims=True)
        stats_ref[2:3, at] = jnp.sum(grad_mixed, axis=0, keepdims=True)
        stats_ref[3:4, at] = jnp.sum(grad_mixed * centred, axis=0, keepdims=True)


def vmem():
    return pl.BlockSpec(memory_space=pltpu.VMEM)


def smem():
    return pl.BlockSpec(memory_space=pltpu.SMEM)


def forward(act, at_head, start):
    length = start.shape[1]
    return pl.pallas_call(
        forward_kernel,
        in_specs=[vmem()] * 3,
        out_specs=[vmem()] * 4,
        out_shape=(
            jax.ShapeDtypeStruct((HD, length), F32),
            jax.ShapeDtypeStruct((HD, length), BF16),
            jax.ShapeDtypeStruct((HD, length), BF16),
            jax.ShapeDtypeStruct((4, length), F32),
        ),
        compiler_params=params(LIMIT),
        cost_estimate=pl.CostEstimate(
            flops=8 * HD * length * length, bytes_accessed=6 << 20, transcendentals=length * length // 2
        ),
        name="attention_forward",
    )(act, at_head, start)


def mix_kernel(own_ref, one_ref, three_ref, two_ref, att_ref, gate_ref, gg_ref, slope_ref, early_ref, go_ref, got_ref):
    width = H * HD
    heads = [ref[k] for ref in (own_ref, one_ref, three_ref, two_ref) for k in range(NX)]
    mean_all = sum(a[0:1] for a in heads) * (1.0 / H)
    apart = [a[0:1] - mean_all for a in heads]
    spread = sum(a[1:2] for a in heads) + HD * sum(d * d for d in apart)
    inverse = lax.rsqrt(spread * (1.0 / width) + EPS)
    first = sum(a[2:3] for a in heads) * (1.0 / width)
    second = inverse * sum(a[3:4] + d * a[2:3] for a, d in zip(heads, apart)) * (1.0 / width)
    gate = gate_ref[...].astype(F32)
    gg = gg_ref[...].astype(F32)
    mixed = (att_ref[...] - mean_all) * inverse
    grad_att = inverse * (gg * gate - first - mixed * second)
    got_ref[...] = grad_att.astype(BF16)
    go_ref[...] = grad_att.T.astype(BF16)
    gated = (mixed * gate).astype(BF16).T
    grad_u = (gg * mixed).T
    late = pl.program_id(0) >= NZ * NX // 2

    def put(order):
        for k in range(2):
            at = slice(k * HD, (k + 1) * HD)
            early_ref[order[k], 0, :, :HD] = gated[at]
            early_ref[order[k], 0, :, HD:] = (grad_u[at] * slope_ref[0, order[k]]).astype(BF16)

    pl.when(jnp.logical_not(late))(lambda: put((0, 1)))
    pl.when(late)(lambda: put((1, 0)))


def mix(own, one, three, two, att, gate, gg, slope):
    length = att.shape[1]
    shards = NZ * NX
    tile = 2 * HD
    turn = shards // 2

    def pair(i):
        return jnp.where(i < turn, i, 2 * turn - 1 - i)

    by_tile = pl.BlockSpec((HD, tile), lambda i: (0, i))
    return pl.pallas_call(
        mix_kernel,
        grid=(length // tile,),
        in_specs=[pl.BlockSpec((NX, 4, tile), lambda i: (0, 0, i))] * 4
        + [by_tile] * 3
        + [pl.BlockSpec((1, 2, HD, HD), lambda i: (i // turn, pair(i), 0, 0))],
        out_specs=[
            pl.BlockSpec((2, 1, HD, tile), lambda i: (pair(i), i // turn, 0, 0)),
            pl.BlockSpec((tile, HD), lambda i: (i, 0)),
            by_tile,
        ],
        out_shape=(
            jax.ShapeDtypeStruct((shards, 2, HD, tile), BF16),
            jax.ShapeDtypeStruct((length, HD), BF16),
            jax.ShapeDtypeStruct((HD, length), BF16),
        ),
        compiler_params=params(LIMIT),
        cost_estimate=pl.CostEstimate(flops=20 * HD * length, bytes_accessed=6 << 20, transcendentals=0),
        name="mix",
    )(own, one, three, two, att, gate, gg, slope)


def backward_kernel(act_ref, go_ref, got_ref, start_ref, early_ref, slope_hbm, back_ref, dk_ref, dv_ref, slope_ref, sem):
    length = go_ref.shape[0]
    copy = pltpu.make_async_copy(slope_hbm, slope_ref, sem)
    copy.start()
    for shard in range(NZ * NX):
        for k in range(2):
            rows = slice(k * HD, (k + 1) * HD)
            back_ref[shard, rows, :HD] = early_ref[shard, k, :, HD:]
            back_ref[shard, rows, 4 * HD :] = early_ref[shard, k, :, :HD]
    keys = [time_rows(act_ref, j, BK, 3) for j in range(0, length, BK)]
    keys_t = [k.T for k in keys]
    values = [time_rows(act_ref, j, BK, 1) for j in range(0, length, BK)]
    queries_in, seen = tiles(length, BQ, BK)

    def put(first, column, value):
        value = (value * time_rows(slope_ref, first, value.shape[0], column)).astype(BF16)
        for k in range(value.shape[0] // HD):
            shard, row = tile_place(first // HD + k)
            back_ref[shard, row : row + HD, column * HD : (column + 1) * HD] = value[
                k * HD : (k + 1) * HD
            ]

    started = set()
    for i, keys_in in queries_in:
        at = slice(i, i + BQ)
        queries = time_rows(act_ref, i, BQ, 2)
        grad_out = go_ref[at, :]
        grad_out_t = got_ref[:, at]
        start = start_ref[:, at]
        total = None
        for j in keys_in:
            here = slice(j, j + BK)
            half = dot_nt(keys[j // BK], queries) * (0.5 * SCALE)
            tanh = jnp.tanh(half)
            weights = half + half * tanh
            sig = 0.5 + 0.5 * tanh
            slope = sig + weights * (1.0 - sig)
            mask = seen(i, j, start)
            ahead = dot(values[j // BK], grad_out_t)
            weights = jnp.where(mask, weights, 0.0).astype(BF16)
            slopes = jnp.where(mask, ahead * slope, 0.0).astype(BF16)
            dv = dot(weights, grad_out)
            dk = dot(slopes, queries)
            if j in started:
                dv_ref[here, :] += dv
                dk_ref[here, :] += dk
            else:
                dv_ref[here, :] = dv
                dk_ref[here, :] = dk
                started.add(j)
            term = dot(keys_t[j // BK], slopes)
            total = term if total is None else total + term
        if i == 0:
            copy.wait()
        put(i, 2, total.T * SCALE)
    for j in range(0, length, BK):
        put(j, 1, dv_ref[j : j + BK, :])
        put(j, 3, dk_ref[j : j + BK, :] * SCALE)


def backward(act, grad_out, grad_out_t, start, early, slope):
    length = start.shape[1]
    shards = NZ * NX
    return pl.pallas_call(
        backward_kernel,
        in_specs=[vmem()] * 5 + [pl.BlockSpec(memory_space=pl.ANY)],
        out_specs=vmem(),
        out_shape=jax.ShapeDtypeStruct((shards, length // shards, 5 * HD), BF16),
        scratch_shapes=[pltpu.VMEM((length, HD), F32)] * 2
        + [pltpu.VMEM(slope.shape, F32), pltpu.SemaphoreType.DMA],
        compiler_params=params(LIMIT),
        cost_estimate=pl.CostEstimate(
            flops=15 * HD * length * length, bytes_accessed=10 << 20, transcendentals=length * length // 2
        ),
        name="attention_backward",
    )(act, grad_out, grad_out_t, start, early, slope)


def terms_in_kernel(core_ref, normed_ref, grad_ref, keep_ref, send_ref, res_ref):
    shards, rows, cols = grad_ref.shape
    res_ref[...] = dot(normed_ref[...], grad_ref[...].reshape(shards * rows, cols))
    core = core_ref[0]
    for k in range(res_ref.shape[0] // HD):
        for pair in range(NY * NXH):
            mine = pl.multiple_of(k * HD + (pair * NC + core) * 8, 8)
            other = pl.multiple_of(k * HD + (pair * NC + 1 - core) * 8, 8)
            keep_ref[pair, k * 8 : (k + 1) * 8, :] = res_ref[pl.ds(mine, 8), :]
            send_ref[pair, k * 8 : (k + 1) * 8, :] = res_ref[pl.ds(other, 8), :]


def terms_in(core, normed_t, back):
    width, length = normed_t.shape
    shards, rows, _ = back.shape
    shape = jax.ShapeDtypeStruct((NY * NXH, 80, 4 * HD), F32)
    out_spec = pl.BlockSpec((NY * NXH, 16, 4 * HD), lambda g: (0, g, 0))
    return pl.pallas_call(
        terms_in_kernel,
        grid=(4,),
        in_specs=[
            smem(),
            pl.BlockSpec((width // 4, length), lambda g: (g, 0)),
            pl.BlockSpec((shards, rows, 4 * HD), lambda g: (0, 0, 0)),
        ],
        out_specs=[out_spec] * 2,
        out_shape=[shape] * 2,
        scratch_shapes=[pltpu.VMEM((width // 4, 4 * HD), F32)],
        compiler_params=params(LIMIT),
        cost_estimate=pl.CostEstimate(
            flops=2 * width * length * 4 * HD, bytes_accessed=9 << 20, transcendentals=0
        ),
        name="terms_in",
    )(core, normed_t, back)


def terms_out_kernel(core_ref, gated_ref, cot_ref, _, __, keep_ref, send_ref, res_ref, gated_t_ref):
    shards, rows, _ = gated_ref.shape

    @pl.when(pl.program_id(0) == 0)
    def _():
        for shard in range(shards):
            gated_t_ref[:, shard * rows : (shard + 1) * rows] = gated_ref[shard].T

    res_ref[...] = dot(gated_t_ref[...], cot_ref[...])
    core = core_ref[0]
    for pair in range(NY * NXH):
        for out_ref, who in ((keep_ref, core), (send_ref, 1 - core)):
            out_ref[pair] = res_ref[pl.ds(pl.multiple_of((pair * NC + who) * 8, 8), 8), :]


def terms_out(core, back, cot_all, keep, send):
    shards, rows, _ = back.shape
    length, width = cot_all.shape
    out_spec = pl.BlockSpec((NY * NXH, 8, 4 * HD), lambda g: (0, 8 + g, 0))
    return pl.pallas_call(
        terms_out_kernel,
        grid=(2,),
        in_specs=[
            smem(),
            pl.BlockSpec((shards, rows, HD), lambda g: (0, 0, 4)),
            pl.BlockSpec((length, width // 2), lambda g: (0, g)),
        ]
        + [pl.BlockSpec(memory_space=pl.ANY)] * 2,
        out_specs=[out_spec] * 2,
        out_shape=[jax.ShapeDtypeStruct(keep.shape, F32)] * 2,
        scratch_shapes=[pltpu.VMEM((HD, width // 2), F32), pltpu.VMEM((HD, length), BF16)],
        input_output_aliases={3: 0, 4: 1},
        compiler_params=params(LIMIT),
        cost_estimate=pl.CostEstimate(
            flops=2 * HD * width * length, bytes_accessed=6 << 20, transcendentals=0
        ),
        name="terms_out",
    )(core, back, cot_all, keep, send)


def small(kernel, name, scalars, arrays, outs, scratch=(), limit=12):
    size = sum(a.size * a.dtype.itemsize for a in arrays)
    return pl.pallas_call(
        kernel,
        in_specs=[smem()] + [vmem()] * len(arrays),
        out_specs=[vmem()] * len(outs),
        out_shape=[jax.ShapeDtypeStruct(shape, dtype) for shape, dtype in outs],
        scratch_shapes=list(scratch),
        compiler_params=params(limit),
        cost_estimate=pl.CostEstimate(flops=size, bytes_accessed=2 * size, transcendentals=0),
        name=name,
    )(scalars, *arrays)


def core_sum_kernel(pos_ref, keep_ref, got_ref, own_ref, one_ref, three_ref, two_ref):
    y = pos_ref[0]
    for d, out_ref in ((0, own_ref), (1, one_ref), (3, three_ref), (2, two_ref)):
        here = pl.ds(((y - d + NY) % NY) * NXH, NXH)
        out_ref[...] = (keep_ref[here] + got_ref[here]).astype(out_ref.dtype)


def y_sum_kernel(pos_ref, own_ref, a_ref, b_ref, c_ref, keep_ref, same_ref, one_ref, two_ref, sum_ref):
    xh, x = pos_ref[1], pos_ref[2]
    sum_ref[...] = own_ref[...] + (
        a_ref[...].astype(F32) + b_ref[...].astype(F32) + c_ref[...].astype(F32)
    )

    def slab(out_ref, h, l):
        for k in range(NZ):
            out_ref[k * 8 : (k + 1) * 8, :] = sum_ref[
                h, pl.ds(pl.multiple_of((k * NX + l) * 8, 8), 8), :
            ]

    slab(keep_ref, xh, x)
    keep_ref[32:, :] = sum_ref[xh, 64:, :]
    slab(same_ref, 1 - xh, x)
    same_ref[32:, :] = sum_ref[1 - xh, 64:, :]
    slab(one_ref, xh, 1 - x)
    slab(two_ref, 1 - xh, 1 - x)


def x_sum_kernel(pos_ref, keep_ref, same_ref, a_ref, b_ref, own_ref, one_ref, three_ref, two_ref, out_ref, sum_ref):
    z, x = pos_ref[3], pos_ref[2]
    mine = keep_ref[...] + same_ref[...]
    sum_ref[x] = mine[:32]
    sum_ref[1 - x] = a_ref[...] + b_ref[...]
    out_ref[...] = mine[32:]
    for d, to_ref in ((0, own_ref), (1, one_ref), (3, three_ref), (2, two_ref)):
        here = pl.ds(pl.multiple_of(((z - d + NZ) % NZ) * 8, 8), 8)
        for l in range(NX):
            to_ref[l * 8 : (l + 1) * 8, :] = sum_ref[l, here, :]


def z_place_kernel(factor, pos_ref, own_ref, one_ref, three_ref, two_ref, out_ref, w_in_ref, w_out_ref):
    z = pos_ref[3]
    for d, ref in ((0, own_ref), (1, one_ref), (3, three_ref), (2, two_ref)):
        for l in range(NX):
            for k in range(4):
                at = pl.multiple_of((k * H + ((z + d) % NZ) * NX + l) * HD, HD)
                w_in_ref[:, pl.ds(at, HD)] = (
                    ref[l * 8 : (l + 1) * 8, k * HD : (k + 1) * HD] * factor
                )
    w_out_ref[:, : 4 * HD] = out_ref[:8] * factor
    w_out_ref[:, 4 * HD :] = out_ref[8:] * factor


def shard_kernel(gated_ref, grad_ref, w_in_ref, w_out_ref, hist_ref, cot_ref, layer_ref, grad_hist_ref, acc_ref):
    step = pl.program_id(0)

    def columns(ref):
        return jnp.concatenate([ref[h] for h in range(H)], axis=1)

    term = dot_nt(columns(grad_ref), w_in_ref[...])

    @pl.when(step == 0)
    def _():
        hist = hist_ref[...].astype(F32)
        layer_ref[...] = (hist + dot(columns(gated_ref), w_out_ref[...])).astype(BF16)
        acc_ref[...] = term

    @pl.when(step > 0)
    def _():
        acc_ref[...] += term

    @pl.when(step == 3)
    def _():
        normed, inverse = layer_norm(hist_ref[...].astype(F32))
        grad = norm_back(normed, inverse, acc_ref[...])
        grad_hist_ref[...] = (cot_ref[...].astype(F32) + grad).astype(BF16)


def shard_outputs(back, w_in, w_out, hist, cot):
    rows, width = hist.shape
    whole = lambda a: pl.BlockSpec(a.shape, lambda k: (0,) * a.ndim)
    return pl.pallas_call(
        shard_kernel,
        grid=(4,),
        in_specs=[
            pl.BlockSpec((H, rows, HD), lambda k: (0, 0, 4)),
            pl.BlockSpec((H, rows, HD), lambda k: (0, 0, k)),
            pl.BlockSpec((width, width), lambda k: (0, k)),
            whole(w_out),
            whole(hist),
            whole(cot),
        ],
        out_specs=[whole(hist)] * 2,
        out_shape=[jax.ShapeDtypeStruct(hist.shape, BF16)] * 2,
        scratch_shapes=[pltpu.VMEM((rows, width), F32)],
        compiler_params=params(LIMIT),
        cost_estimate=pl.CostEstimate(
            flops=10 * rows * width * width, bytes_accessed=14 << 20, transcendentals=0
        ),
        name="shard_outputs",
    )(back, back, w_in, w_out, hist, cot)


def local(history, segment_ids, w_in, w_out, cotangent):
    hist = history[0]
    cot = cotangent[0]
    rows, width = hist.shape
    length = rows * NZ * NX
    s = lax.axis_index("seq")
    u = lax.axis_index("user")
    z, x = s // NX, s % NX
    y, xh, core = u // (NXH * NC), (u // NC) % NXH, u % NC

    users = NY * NXH * NC
    tie = lax.optimization_barrier
    w_head = jnp.concatenate(
        [lax.dynamic_slice(w_in, (0, i * width + s * HD), (width, HD)) for i in range(4)], axis=1
    )

    def place_of(key):
        return ((z + key[0]) % NZ) * NX + (x ^ key[1])

    def project(got, outs):
        at = jnp.stack([place_of(key) for key in got])
        return ln_proj(at, list(got.values()), w_head, outs)

    got = step_one(hist)
    outs = project({(0, 0): hist}, ())
    grad_gated_own = dot_nt(cot, w_out).astype(BF16).reshape(rows, H, HD).transpose(1, 0, 2)
    got, outs, grad_gated_own, cot_next = tie((got, outs, grad_gated_own, cot))
    cot_all = lax.all_gather(cot_next, "seq", axis=0, tiled=True)
    ids = segment_ids[0].astype(BF16).reshape(2, HD)
    ids = jnp.pad(ids, ((0, 14), (0, 0)))
    to_heads = jnp.concatenate(
        [
            grad_gated_own,
            jnp.broadcast_to(ids[None], (H, 16, HD)),
        ],
        axis=1,
    )
    at_head = lax.all_to_all(to_heads, "seq", 0, 0, tiled=True)
    more = step_two(got)
    outs = project(got, outs)
    more, outs = tie((more, outs))
    got.update(more)
    last = step_three(got)
    outs = project(more, outs)
    ids = at_head[:, rows : rows + 2].astype(jnp.int32)
    ids = jnp.concatenate([ids[:, 0], ids[::-1, 1]], axis=0).reshape(1, length)
    start = sum(jnp.where(ids > v, jnp.sum((ids == v).astype(jnp.int32)), 0) for v in range(3))
    last, outs, start, at_head = tie((last, outs, start, at_head))
    normed_t, act, slope = project(last, outs)
    att, gate_t, gg_t, stats = forward(act, at_head, start)
    pair = jnp.stack([stats, from_seq(stats, 0, 1)])
    others = [from_seq(pair, dz, 0) for dz in (1, 3, 2)]
    early, grad_out, grad_out_t = mix(pair, *others, att, gate_t, gg_t, slope)
    back = backward(act, grad_out, grad_out_t, start, early, slope)
    back_tok = lax.all_to_all(back, "seq", 0, 0, tiled=True)

    at_core = core.reshape(1)
    keep, send = terms_in(at_core, normed_t, back)
    keep, send = terms_out(at_core, back, cot_all, keep, send)
    at = jnp.stack([y, xh, x, z])
    n = 4 * HD
    got = from_user(send, 0, 0, 1)
    own, *sends = small(
        core_sum_kernel,
        "core_sum",
        at,
        [keep, got],
        [((NXH, 80, n), F32)] + [((NXH, 80, n), BF16)] * 3,
        limit=LIMIT,
    )
    back_tok, own, sends = tie((back_tok, own, sends))
    sends = [from_user(a, d, 0, 0) for a, d in zip(sends, (1, 3, 2))]
    layer_out, grad_history = shard_outputs(back_tok, w_in, w_out, hist, cot)
    sends, layer_out, grad_history = tie((sends, layer_out, grad_history))
    keep, same, one, two = small(
        y_sum_kernel,
        "y_sum",
        at,
        [own, *sends],
        [((48, n), F32)] * 2 + [((32, n), F32)] * 2,
        [pltpu.VMEM((NXH, 80, n), F32)],
    )
    same = from_both(same, 1, 0)
    one = from_both(one, 0, 1)
    two = from_both(two, 1, 1)
    own, *sends, own_out = small(
        x_sum_kernel,
        "x_sum",
        at,
        [keep, same, one, two],
        [((16, n), F32)] * 5,
        [pltpu.VMEM((NX, 32, n), F32)],
    )
    sends = [from_seq(a, d, 0) for a, d in zip(sends, (1, 3, 2))]
    factor = (length * users) ** (-0.5)
    grad_w_in, grad_w_out = small(
        functools.partial(z_place_kernel, factor),
        "z_place",
        at,
        [own, *sends, own_out],
        [((8, 4 * width), F32), ((8, width), F32)],
    )
    return layer_out[None], grad_history[None], grad_w_in, grad_w_out


def solution(mesh):
    in_specs = (P("user", "seq", None), P("user", "seq"), P(), P(), P("user", "seq", None))
    out_specs = (
        P("user", "seq", None),
        P("user", "seq", None),
        P(("seq", "user"), None),
        P(("seq", "user"), None),
    )
    return jax.shard_map(local, mesh=mesh, in_specs=in_specs, out_specs=out_specs, check_vma=False)
```

```python
import functools

import jax
import jax.numpy as jnp
from jax import lax
from jax.experimental import pallas as pl
from jax.experimental.pallas import tpu as pltpu
from jax.sharding import PartitionSpec as P

F32 = jnp.float32
BF16 = jnp.bfloat16
EPS = 1e-05
H = 8
HD = 128
NZ, NX = 4, 2
NY, NXH, NC = 4, 2, 2


def seq_perm(dz, dx):
    return [
        (((z + dz) % NZ) * NX + (x ^ dx), z * NX + x) for z in range(NZ) for x in range(NX)
    ]


def user_perm(dy, dh, dc):
    return [
        ((((y + dy) % NY) * NXH + (h ^ dh)) * NC + (c ^ dc), (y * NXH + h) * NC + c)
        for y in range(NY)
        for h in range(NXH)
        for c in range(NC)
    ]


def from_seq(a, dz, dx):
    return lax.ppermute(a, "seq", seq_perm(dz, dx))


def from_user(a, dy, dh, dc):
    return lax.ppermute(a, "user", user_perm(dy, dh, dc))


def from_both(a, dh, dx):
    pairs = []
    for s in range(NZ * NX):
        for u in range(NY * NXH * NC):
            pairs.append(((s ^ dx) * NY * NXH * NC + (u ^ (dh * NC)), s * NY * NXH * NC + u))
    return lax.ppermute(a, ("seq", "user"), pairs)


def step_one(block):
    return {
        (1, 0): from_seq(block, 1, 0),
        (3, 0): from_seq(block, 3, 0),
        (0, 1): from_seq(block, 0, 1),
    }


def step_two(got):
    return {
        (2, 0): from_seq(got[1, 0], 1, 0),
        (3, 1): from_seq(got[0, 1], 3, 0),
        (1, 1): from_seq(got[1, 0], 0, 1),
    }


def step_three(got, a=96, b=176):
    return {
        (2, 1): jnp.concatenate(
            [
                from_seq(got[2, 0][:a], 0, 1),
                from_seq(got[1, 1][a:b], 1, 0),
                from_seq(got[3, 1][b:], 3, 0),
            ],
            axis=0,
        )
    }


def layer_norm(entries):
    centre = jnp.mean(entries, axis=-1, keepdims=True)
    centred = entries - centre
    inverse = lax.rsqrt(jnp.mean(centred * centred, axis=-1, keepdims=True) + EPS)
    return centred * inverse, inverse


def norm_back(normed, inverse, upstream):
    first_term = jnp.mean(upstream, axis=-1, keepdims=True)
    second_term = jnp.mean(upstream * normed, axis=-1, keepdims=True)
    return inverse * (upstream - first_term - normed * second_term)


def dot(a, b):
    return jnp.dot(a, b, preferred_element_type=F32)


def dot_nt(a, b):
    return lax.dot_general(a, b, (((1,), (1,)), ((), ())), preferred_element_type=F32)


def dot_tn(a, b):
    return lax.dot_general(a, b, (((0,), (0,)), ((), ())), preferred_element_type=F32)


LIMIT = 56


def params(limit):
    return pltpu.CompilerParams(vmem_limit_bytes=limit << 20)


def ln_proj_kernel(count, at_ref, *refs):
    w_ref = refs[count]
    normed_ref, act_ref, slope_ref = refs[-3:]
    half = act_ref.shape[2]
    for k in range(count):

        @pl.when(pl.program_id(0) == k)
        def _():
            normed, _ = layer_norm(refs[k][...].astype(F32))
            normed_b = normed.astype(BF16)
            normed_ref[...] = normed_b.T
            projected = dot(normed_b, w_ref[...])
            tanh = jnp.tanh(0.5 * projected)
            sig = 0.5 + 0.5 * tanh
            silu = projected * sig
            act = silu.astype(BF16)
            slope = sig + silu * (1.0 - sig)
            for i in range(2):
                act_ref[i, 0] = act[i * half : (i + 1) * half]
                slope_ref[i, 0] = slope[i * half : (i + 1) * half]


def ln_proj(at, blocks, w_head, outs):
    rows, width = blocks[0].shape
    cols = w_head.shape[1]
    half, shards = rows // 2, NZ * NX
    by_half = pl.BlockSpec((2, 1, half, cols), lambda i, at_ref: (0, at_ref[i], 0, 0))
    in_specs = [pl.BlockSpec((rows, width), lambda i, at_ref: (0, 0))] * len(blocks)
    in_specs.append(pl.BlockSpec((width, cols), lambda i, at_ref: (0, 0)))
    aliases = {}
    if outs:
        in_specs += [pl.BlockSpec(memory_space=pl.ANY)] * 3
        aliases = {len(in_specs) + k - 2: k for k in range(3)}
    return pl.pallas_call(
        functools.partial(ln_proj_kernel, len(blocks)),
        grid_spec=pltpu.PrefetchScalarGridSpec(
            num_scalar_prefetch=1,
            grid=(len(blocks),),
            in_specs=in_specs,
            out_specs=(
                pl.BlockSpec((width, rows), lambda i, at_ref: (0, at_ref[i])),
                by_half,
                by_half,
            ),
        ),
        out_shape=(
            jax.ShapeDtypeStruct((width, rows * shards), BF16),
            jax.ShapeDtypeStruct((2, shards, half, cols), BF16),
            jax.ShapeDtypeStruct((2, shards, half, cols), F32),
        ),
        input_output_aliases=aliases,
        compiler_params=params(LIMIT),
        cost_estimate=pl.CostEstimate(
            flops=2 * rows * width * cols * len(blocks),
            bytes_accessed=3 * len(blocks) << 20,
            transcendentals=rows * cols * len(blocks),
        ),
        name="ln_proj",
    )(at, *blocks, w_head, *outs)


FQ, FK = 512, 512
BQ, BK = 256, 256
SCALE = HD ** (-0.5)


def tile_place(block):
    last = 2 * NZ * NX - 1
    return (block, 0) if block < NZ * NX else (last - block, HD)


def time_rows(ref, first, count, column, columns=1):
    parts = []
    for block in range(first // HD, (first + count) // HD):
        shard, row = tile_place(block)
        parts.append(ref[row // HD, shard, :, column * HD : (column + columns) * HD])
    return parts[0] if len(parts) == 1 else jnp.concatenate(parts, axis=0)


def tiles(length, rows, cols):
    key_row = lax.broadcasted_iota(jnp.int32, (cols, rows), 0)
    query_col = lax.broadcasted_iota(jnp.int32, (1, rows), 1)

    def seen(i, j, start):
        mask = key_row >= start - j
        if j + cols > i:
            mask = mask & (key_row <= query_col + (i - j))
        return mask

    return [(i, range(0, i + rows, cols)) for i in range(0, length, rows)], seen


def forward_kernel(act_ref, head_ref, start_ref, att_ref, gate_ref, gg_ref, stats_ref):
    length = att_ref.shape[1]
    values_t = [time_rows(act_ref, j, FK, 1).T for j in range(0, length, FK)]
    keys = [time_rows(act_ref, j, FK, 3) for j in range(0, length, FK)]
    queries_in, seen = tiles(length, FQ, FK)
    for i, keys_in in queries_in:
        at = slice(i, i + FQ)
        queries = time_rows(act_ref, i, FQ, 2)
        start = start_ref[:, at]
        total = None
        for j in keys_in:
            half = dot_nt(keys[j // FK], queries) * (0.5 * SCALE)
            weights = half + half * jnp.tanh(half)
            weights = jnp.where(seen(i, j, start), weights, 0.0).astype(BF16)
            term = dot(values_t[j // FK], weights)
            total = term if total is None else total + term
        att_ref[:, at] = total
        gate = time_rows(act_ref, i, FQ, 0).T
        parts = []
        for block in range(i // HD, (i + FQ) // HD):
            shard, row = tile_place(block)
            parts.append(head_ref[shard, row : row + HD, :])
        gg = jnp.concatenate(parts, axis=0).T
        gate_ref[:, at] = gate
        gg_ref[:, at] = gg
        grad_mixed = gg.astype(F32) * gate.astype(F32)
        mean = jnp.sum(total, axis=0, keepdims=True) * (1.0 / HD)
        centred = total - mean
        stats_ref[0:1, at] = mean
        stats_ref[1:2, at] = jnp.sum(centred * centred, axis=0, keepdims=True)
        stats_ref[2:3, at] = jnp.sum(grad_mixed, axis=0, keepdims=True)
        stats_ref[3:4, at] = jnp.sum(grad_mixed * centred, axis=0, keepdims=True)


def vmem():
    return pl.BlockSpec(memory_space=pltpu.VMEM)


def smem():
    return pl.BlockSpec(memory_space=pltpu.SMEM)


def forward(act, at_head, start):
    length = start.shape[1]
    return pl.pallas_call(
        forward_kernel,
        in_specs=[vmem()] * 3,
        out_specs=[vmem()] * 4,
        out_shape=(
            jax.ShapeDtypeStruct((HD, length), F32),
            jax.ShapeDtypeStruct((HD, length), BF16),
            jax.ShapeDtypeStruct((HD, length), BF16),
            jax.ShapeDtypeStruct((4, length), F32),
        ),
        compiler_params=params(LIMIT),
        cost_estimate=pl.CostEstimate(
            flops=8 * HD * length * length, bytes_accessed=6 << 20, transcendentals=length * length // 2
        ),
        name="attention_forward",
    )(act, at_head, start)


def mix_kernel(own_ref, one_ref, three_ref, two_ref, att_ref, gate_ref, gg_ref, slope_ref, early_ref, go_ref, got_ref):
    length = att_ref.shape[1]
    width = H * HD
    tile = 2 * HD
    heads = [ref[k] for ref in (own_ref, one_ref, three_ref, two_ref) for k in range(NX)]
    mean_all = sum(a[0:1] for a in heads) * (1.0 / H)
    apart = [a[0:1] - mean_all for a in heads]
    spread = sum(a[1:2] for a in heads) + HD * sum(d * d for d in apart)
    inverse_all = lax.rsqrt(spread * (1.0 / width) + EPS)
    first_all = sum(a[2:3] for a in heads) * (1.0 / width)
    second_all = inverse_all * sum(a[3:4] + d * a[2:3] for a, d in zip(heads, apart)) * (1.0 / width)
    for i in range(0, length, tile):
        at = slice(i, i + tile)
        gate = gate_ref[:, at].astype(F32)
        gg = gg_ref[:, at].astype(F32)
        inverse = inverse_all[:, at]
        mixed = (att_ref[:, at] - mean_all[:, at]) * inverse
        grad_att = inverse * (gg * gate - first_all[:, at] - mixed * second_all[:, at])
        got_ref[:, at] = grad_att.astype(BF16)
        go_ref[at, :] = grad_att.T.astype(BF16)
        gated = (mixed * gate).astype(BF16).T
        grad_u = ((gg * mixed).T * time_rows(slope_ref, i, tile, 0)).astype(BF16)
        for k in range(2):
            shard, row = tile_place(i // HD + k)
            early_ref[shard, row : row + HD, :HD] = gated[k * HD : (k + 1) * HD]
            early_ref[shard, row : row + HD, HD:] = grad_u[k * HD : (k + 1) * HD]


def mix(own, one, three, two, att, gate, gg, slope):
    length = att.shape[1]
    shards = NZ * NX
    whole = lambda shape: pl.BlockSpec(shape, lambda i: (0,) * len(shape))
    return pl.pallas_call(
        mix_kernel,
        grid=(1,),
        in_specs=[whole(own.shape)] * 4
        + [whole(att.shape)] * 3
        + [pl.BlockSpec(slope.shape[:3] + (HD,), lambda i: (0, 0, 0, 0))],
        out_specs=[whole((shards, length // shards, 2 * HD)), whole((length, HD)), whole((HD, length))],
        out_shape=(
            jax.ShapeDtypeStruct((shards, length // shards, 2 * HD), BF16),
            jax.ShapeDtypeStruct((length, HD), BF16),
            jax.ShapeDtypeStruct((HD, length), BF16),
        ),
        compiler_params=params(LIMIT),
        cost_estimate=pl.CostEstimate(flops=20 * HD * length, bytes_accessed=6 << 20, transcendentals=0),
        name="mix",
    )(own, one, three, two, att, gate, gg, slope)


def backward_kernel(act_ref, go_ref, got_ref, start_ref, early_ref, slope_hbm, back_ref, dk_ref, dv_ref, slope_ref, sem):
    length = go_ref.shape[0]
    copy = pltpu.make_async_copy(slope_hbm, slope_ref, sem)
    copy.start()
    back_ref[:, :, :HD] = early_ref[:, :, HD:]
    back_ref[:, :, 4 * HD :] = early_ref[:, :, :HD]
    keys = [time_rows(act_ref, j, BK, 3) for j in range(0, length, BK)]
    keys_t = [k.T for k in keys]
    values = [time_rows(act_ref, j, BK, 1) for j in range(0, length, BK)]
    queries_in, seen = tiles(length, BQ, BK)

    def put(first, column, value):
        value = (value * time_rows(slope_ref, first, value.shape[0], column)).astype(BF16)
        for k in range(value.shape[0] // HD):
            shard, row = tile_place(first // HD + k)
            back_ref[shard, row : row + HD, column * HD : (column + 1) * HD] = value[
                k * HD : (k + 1) * HD
            ]

    started = set()
    for i, keys_in in queries_in:
        at = slice(i, i + BQ)
        queries = time_rows(act_ref, i, BQ, 2)
        grad_out = go_ref[at, :]
        grad_out_t = got_ref[:, at]
        start = start_ref[:, at]
        total = None
        for j in keys_in:
            here = slice(j, j + BK)
            half = dot_nt(keys[j // BK], queries) * (0.5 * SCALE)
            tanh = jnp.tanh(half)
            weights = half + half * tanh
            sig = 0.5 + 0.5 * tanh
            slope = sig + weights * (1.0 - sig)
            mask = seen(i, j, start)
            ahead = dot(values[j // BK], grad_out_t)
            weights = jnp.where(mask, weights, 0.0).astype(BF16)
            slopes = jnp.where(mask, ahead * slope, 0.0).astype(BF16)
            dv = dot(weights, grad_out)
            dk = dot(slopes, queries)
            if j in started:
                dv_ref[here, :] += dv
                dk_ref[here, :] += dk
            else:
                dv_ref[here, :] = dv
                dk_ref[here, :] = dk
                started.add(j)
            term = dot(keys_t[j // BK], slopes)
            total = term if total is None else total + term
        if i == 0:
            copy.wait()
        put(i, 2, total.T * SCALE)
    for j in range(0, length, BK):
        put(j, 1, dv_ref[j : j + BK, :])
        put(j, 3, dk_ref[j : j + BK, :] * SCALE)


def backward(act, grad_out, grad_out_t, start, early, slope):
    length = start.shape[1]
    shards = NZ * NX
    return pl.pallas_call(
        backward_kernel,
        in_specs=[vmem()] * 5 + [pl.BlockSpec(memory_space=pl.ANY)],
        out_specs=vmem(),
        out_shape=jax.ShapeDtypeStruct((shards, length // shards, 5 * HD), BF16),
        scratch_shapes=[pltpu.VMEM((length, HD), F32)] * 2
        + [pltpu.VMEM(slope.shape, F32), pltpu.SemaphoreType.DMA],
        compiler_params=params(LIMIT),
        cost_estimate=pl.CostEstimate(
            flops=15 * HD * length * length, bytes_accessed=10 << 20, transcendentals=length * length // 2
        ),
        name="attention_backward",
    )(act, grad_out, grad_out_t, start, early, slope)


def terms_in_kernel(core_ref, normed_ref, grad_ref, keep_ref, send_ref, res_ref):
    shards, rows, cols = grad_ref.shape
    res_ref[...] = dot(normed_ref[...], grad_ref[...].reshape(shards * rows, cols))
    core = core_ref[0]
    for k in range(res_ref.shape[0] // HD):
        for pair in range(NY * NXH):
            mine = pl.multiple_of(k * HD + (pair * NC + core) * 8, 8)
            other = pl.multiple_of(k * HD + (pair * NC + 1 - core) * 8, 8)
            keep_ref[pair, k * 8 : (k + 1) * 8, :] = res_ref[pl.ds(mine, 8), :]
            send_ref[pair, k * 8 : (k + 1) * 8, :] = res_ref[pl.ds(other, 8), :]


def terms_in(core, normed_t, back):
    width, length = normed_t.shape
    shards, rows, _ = back.shape
    shape = jax.ShapeDtypeStruct((NY * NXH, 80, 4 * HD), F32)
    out_spec = pl.BlockSpec((NY * NXH, 16, 4 * HD), lambda g: (0, g, 0))
    return pl.pallas_call(
        terms_in_kernel,
        grid=(4,),
        in_specs=[
            smem(),
            pl.BlockSpec((width // 4, length), lambda g: (g, 0)),
            pl.BlockSpec((shards, rows, 4 * HD), lambda g: (0, 0, 0)),
        ],
        out_specs=[out_spec] * 2,
        out_shape=[shape] * 2,
        scratch_shapes=[pltpu.VMEM((width // 4, 4 * HD), F32)],
        compiler_params=params(LIMIT),
        cost_estimate=pl.CostEstimate(
            flops=2 * width * length * 4 * HD, bytes_accessed=9 << 20, transcendentals=0
        ),
        name="terms_in",
    )(core, normed_t, back)


def terms_out_kernel(core_ref, gated_ref, cot_ref, _, __, keep_ref, send_ref, res_ref, gated_t_ref):
    shards, rows, _ = gated_ref.shape

    @pl.when(pl.program_id(0) == 0)
    def _():
        for shard in range(shards):
            gated_t_ref[:, shard * rows : (shard + 1) * rows] = gated_ref[shard].T

    res_ref[...] = dot(gated_t_ref[...], cot_ref[...])
    core = core_ref[0]
    for pair in range(NY * NXH):
        for out_ref, who in ((keep_ref, core), (send_ref, 1 - core)):
            out_ref[pair] = res_ref[pl.ds(pl.multiple_of((pair * NC + who) * 8, 8), 8), :]


def terms_out(core, back, cot_all, keep, send):
    shards, rows, _ = back.shape
    length, width = cot_all.shape
    out_spec = pl.BlockSpec((NY * NXH, 8, 4 * HD), lambda g: (0, 8 + g, 0))
    return pl.pallas_call(
        terms_out_kernel,
        grid=(2,),
        in_specs=[
            smem(),
            pl.BlockSpec((shards, rows, HD), lambda g: (0, 0, 4)),
            pl.BlockSpec((length, width // 2), lambda g: (0, g)),
        ]
        + [pl.BlockSpec(memory_space=pl.ANY)] * 2,
        out_specs=[out_spec] * 2,
        out_shape=[jax.ShapeDtypeStruct(keep.shape, F32)] * 2,
        scratch_shapes=[pltpu.VMEM((HD, width // 2), F32), pltpu.VMEM((HD, length), BF16)],
        input_output_aliases={3: 0, 4: 1},
        compiler_params=params(LIMIT),
        cost_estimate=pl.CostEstimate(
            flops=2 * HD * width * length, bytes_accessed=6 << 20, transcendentals=0
        ),
        name="terms_out",
    )(core, back, cot_all, keep, send)


def small(kernel, name, scalars, arrays, outs, scratch=(), limit=12):
    size = sum(a.size * a.dtype.itemsize for a in arrays)
    return pl.pallas_call(
        kernel,
        in_specs=[smem()] + [vmem()] * len(arrays),
        out_specs=[vmem()] * len(outs),
        out_shape=[jax.ShapeDtypeStruct(shape, dtype) for shape, dtype in outs],
        scratch_shapes=list(scratch),
        compiler_params=params(limit),
        cost_estimate=pl.CostEstimate(flops=size, bytes_accessed=2 * size, transcendentals=0),
        name=name,
    )(scalars, *arrays)


def core_sum_kernel(pos_ref, keep_ref, got_ref, own_ref, one_ref, three_ref, two_ref):
    y = pos_ref[0]
    for d, out_ref in ((0, own_ref), (1, one_ref), (3, three_ref), (2, two_ref)):
        here = pl.ds(((y - d + NY) % NY) * NXH, NXH)
        out_ref[...] = (keep_ref[here] + got_ref[here]).astype(out_ref.dtype)


def y_sum_kernel(pos_ref, own_ref, a_ref, b_ref, c_ref, keep_ref, same_ref, one_ref, two_ref, sum_ref):
    xh, x = pos_ref[1], pos_ref[2]
    sum_ref[...] = own_ref[...] + (
        a_ref[...].astype(F32) + b_ref[...].astype(F32) + c_ref[...].astype(F32)
    )

    def slab(out_ref, h, l):
        for k in range(NZ):
            out_ref[k * 8 : (k + 1) * 8, :] = sum_ref[
                h, pl.ds(pl.multiple_of((k * NX + l) * 8, 8), 8), :
            ]

    slab(keep_ref, xh, x)
    keep_ref[32:, :] = sum_ref[xh, 64:, :]
    slab(same_ref, 1 - xh, x)
    same_ref[32:, :] = sum_ref[1 - xh, 64:, :]
    slab(one_ref, xh, 1 - x)
    slab(two_ref, 1 - xh, 1 - x)


def x_sum_kernel(pos_ref, keep_ref, same_ref, a_ref, b_ref, own_ref, one_ref, three_ref, two_ref, out_ref, sum_ref):
    z, x = pos_ref[3], pos_ref[2]
    mine = keep_ref[...] + same_ref[...]
    sum_ref[x] = mine[:32]
    sum_ref[1 - x] = a_ref[...] + b_ref[...]
    out_ref[...] = mine[32:]
    for d, to_ref in ((0, own_ref), (1, one_ref), (3, three_ref), (2, two_ref)):
        here = pl.ds(pl.multiple_of(((z - d + NZ) % NZ) * 8, 8), 8)
        for l in range(NX):
            to_ref[l * 8 : (l + 1) * 8, :] = sum_ref[l, here, :]


def z_place_kernel(factor, pos_ref, own_ref, one_ref, three_ref, two_ref, out_ref, w_in_ref, w_out_ref):
    z = pos_ref[3]
    for d, ref in ((0, own_ref), (1, one_ref), (3, three_ref), (2, two_ref)):
        for l in range(NX):
            for k in range(4):
                at = pl.multiple_of((k * H + ((z + d) % NZ) * NX + l) * HD, HD)
                w_in_ref[:, pl.ds(at, HD)] = (
                    ref[l * 8 : (l + 1) * 8, k * HD : (k + 1) * HD] * factor
                )
    w_out_ref[:, : 4 * HD] = out_ref[:8] * factor
    w_out_ref[:, 4 * HD :] = out_ref[8:] * factor


def columns(ref):
    return jnp.concatenate([ref[h] for h in range(H)], axis=1)


def shard_out_kernel(gated_ref, grad_ref, w_in_ref, w_out_ref, hist_ref, layer_ref, acc_ref):
    term = dot_nt(columns(grad_ref), w_in_ref[...])

    @pl.when(pl.program_id(0) == 0)
    def _():
        hist = hist_ref[...].astype(F32)
        layer_ref[...] = (hist + dot(columns(gated_ref), w_out_ref[...])).astype(BF16)
        acc_ref[...] = term

    @pl.when(pl.program_id(0) > 0)
    def _():
        acc_ref[...] += term


def shard_grad_kernel(grad_ref, w_in_ref, hist_ref, cot_ref, half_ref, grad_hist_ref, acc_ref):
    term = dot_nt(columns(grad_ref), w_in_ref[...])

    @pl.when(pl.program_id(0) == 0)
    def _():
        acc_ref[...] = half_ref[...] + term

    @pl.when(pl.program_id(0) > 0)
    def _():
        normed, inverse = layer_norm(hist_ref[...].astype(F32))
        grad = norm_back(normed, inverse, acc_ref[...] + term)
        grad_hist_ref[...] = (cot_ref[...].astype(F32) + grad).astype(BF16)


def shard_out(back, w_in, w_out, hist):
    rows, width = hist.shape
    whole = lambda a: pl.BlockSpec(a.shape, lambda k: (0,) * a.ndim)
    return pl.pallas_call(
        shard_out_kernel,
        grid=(2,),
        in_specs=[
            pl.BlockSpec((H, rows, HD), lambda k: (0, 0, 4)),
            pl.BlockSpec((H, rows, HD), lambda k: (0, 0, k)),
            pl.BlockSpec((width, width), lambda k: (0, k)),
            whole(w_out),
            whole(hist),
        ],
        out_specs=[whole(hist)] * 2,
        out_shape=[jax.ShapeDtypeStruct(hist.shape, BF16), jax.ShapeDtypeStruct(hist.shape, F32)],
        compiler_params=params(LIMIT),
        cost_estimate=pl.CostEstimate(
            flops=6 * rows * width * width, bytes_accessed=8 << 20, transcendentals=0
        ),
        name="shard_out",
    )(back, back, w_in, w_out, hist)


def shard_grad(back, w_in, hist, cot, half):
    rows, width = hist.shape
    whole = lambda a: pl.BlockSpec(a.shape, lambda k: (0,) * a.ndim)
    return pl.pallas_call(
        shard_grad_kernel,
        grid=(2,),
        in_specs=[
            pl.BlockSpec((H, rows, HD), lambda k: (0, 0, 2 + k)),
            pl.BlockSpec((width, width), lambda k: (0, 2 + k)),
            whole(hist),
            whole(cot),
            whole(half),
        ],
        out_specs=whole(hist),
        out_shape=jax.ShapeDtypeStruct(hist.shape, BF16),
        scratch_shapes=[pltpu.VMEM((rows, width), F32)],
        compiler_params=params(LIMIT),
        cost_estimate=pl.CostEstimate(
            flops=4 * rows * width * width, bytes_accessed=8 << 20, transcendentals=0
        ),
        name="shard_grad",
    )(back, w_in, hist, cot, half)


def local(history, segment_ids, w_in, w_out, cotangent):
    hist = history[0]
    cot = cotangent[0]
    rows, width = hist.shape
    length = rows * NZ * NX
    s = lax.axis_index("seq")
    u = lax.axis_index("user")
    z, x = s // NX, s % NX
    y, xh, core = u // (NXH * NC), (u // NC) % NXH, u % NC

    users = NY * NXH * NC
    tie = lax.optimization_barrier
    w_head = jnp.concatenate(
        [lax.dynamic_slice(w_in, (0, i * width + s * HD), (width, HD)) for i in range(4)], axis=1
    )

    def place_of(key):
        return ((z + key[0]) % NZ) * NX + (x ^ key[1])

    def project(got, outs):
        at = jnp.stack([place_of(key) for key in got])
        return ln_proj(at, list(got.values()), w_head, outs)

    got = step_one(hist)
    outs = project({(0, 0): hist}, ())
    grad_gated_own = dot_nt(cot, w_out).astype(BF16).reshape(rows, H, HD).transpose(1, 0, 2)
    ids = segment_ids[0].astype(BF16).reshape(2, HD)
    ids = jnp.pad(ids, ((0, 14), (0, 0)))
    to_heads = jnp.concatenate(
        [
            grad_gated_own,
            jnp.broadcast_to(ids[None], (H, 16, HD)),
        ],
        axis=1,
    )
    at_head = lax.all_to_all(to_heads, "seq", 0, 0, tiled=True)
    cot_wide = jnp.broadcast_to(cot[None], (NZ * NX, rows, width))
    got, outs, cot_wide = tie((got, outs, cot_wide))
    more = step_two(got)
    outs = project(got, outs)
    more, outs, cot_wide = tie((more, outs, cot_wide))
    got.update(more)
    last = step_three(got)
    outs = project(more, outs)
    ids = at_head[:, rows : rows + 2].astype(jnp.int32)
    ids = jnp.concatenate([ids[:, 0], ids[::-1, 1]], axis=0).reshape(1, length)
    start = sum(jnp.where(ids > v, jnp.sum((ids == v).astype(jnp.int32)), 0) for v in range(3))
    last, outs, start, at_head, cot_wide = tie((last, outs, start, at_head, cot_wide))
    cot_all = lax.all_to_all(cot_wide, "seq", 0, 0, tiled=True).reshape(length, width)
    normed_t, act, slope = project(last, outs)
    att, gate_t, gg_t, stats = forward(act, at_head, start)
    pair = jnp.stack([stats, from_seq(stats, 0, 1)])
    others = [from_seq(pair, dz, 0) for dz in (1, 3, 2)]
    early, grad_out, grad_out_t = mix(pair, *others, att, gate_t, gg_t, slope)
    back = backward(act, grad_out, grad_out_t, start, early, slope)
    back, cot_all = tie((back, cot_all))
    back_tok = lax.all_to_all(back, "seq", 0, 0, tiled=True)

    at_core = core.reshape(1)
    keep, send = terms_in(at_core, normed_t, back)
    keep, send = terms_out(at_core, back, cot_all, keep, send)
    at = jnp.stack([y, xh, x, z])
    n = 4 * HD
    got = from_user(send, 0, 0, 1)
    own, *sends = small(
        core_sum_kernel,
        "core_sum",
        at,
        [keep, got],
        [((NXH, 80, n), F32)] + [((NXH, 80, n), BF16)] * 3,
        limit=LIMIT,
    )
    own, sends = tie((own, sends))
    sends = [from_user(a, d, 0, 0) for a, d in zip(sends, (1, 3, 2))]
    layer_out, half = shard_out(back_tok, w_in, w_out, hist)
    sends, layer_out, half = tie((sends, layer_out, half))
    keep, same, one, two = small(
        y_sum_kernel,
        "y_sum",
        at,
        [own, *sends],
        [((48, n), F32)] * 2 + [((32, n), F32)] * 2,
        [pltpu.VMEM((NXH, 80, n), F32)],
    )
    same = from_both(same, 1, 0)
    one = from_both(one, 0, 1)
    two = from_both(two, 1, 1)
    grad_history = shard_grad(back_tok, w_in, hist, cot, half)
    same, one, two, grad_history = tie((same, one, two, grad_history))
    own, *sends, own_out = small(
        x_sum_kernel,
        "x_sum",
        at,
        [keep, same, one, two],
        [((16, n), F32)] * 5,
        [pltpu.VMEM((NX, 32, n), F32)],
    )
    sends = [from_seq(a, d, 0) for a, d in zip(sends, (1, 3, 2))]
    factor = (length * users) ** (-0.5)
    grad_w_in, grad_w_out = small(
        functools.partial(z_place_kernel, factor),
        "z_place",
        at,
        [own, *sends, own_out],
        [((8, 4 * width), F32), ((8, width), F32)],
    )
    return layer_out[None], grad_history[None], grad_w_in, grad_w_out


def solution(mesh):
    in_specs = (P("user", "seq", None), P("user", "seq"), P(), P(), P("user", "seq", None))
    out_specs = (
        P("user", "seq", None),
        P("user", "seq", None),
        P(("seq", "user"), None),
        P(("seq", "user"), None),
    )
    return jax.shard_map(local, mesh=mesh, in_specs=in_specs, out_specs=out_specs, check_vma=False)
```

```python
import functools

import jax
import jax.numpy as jnp
from jax import lax
from jax.experimental import pallas as pl
from jax.experimental.pallas import tpu as pltpu
from jax.sharding import PartitionSpec as P

F32 = jnp.float32
BF16 = jnp.bfloat16
EPS = 1e-05
H = 8
HD = 128
NZ, NX = 4, 2
NY, NXH, NC = 4, 2, 2


def seq_perm(dz, dx):
    return [
        (((z + dz) % NZ) * NX + (x ^ dx), z * NX + x) for z in range(NZ) for x in range(NX)
    ]


def user_perm(dy, dh, dc):
    return [
        ((((y + dy) % NY) * NXH + (h ^ dh)) * NC + (c ^ dc), (y * NXH + h) * NC + c)
        for y in range(NY)
        for h in range(NXH)
        for c in range(NC)
    ]


def from_seq(a, dz, dx):
    return lax.ppermute(a, "seq", seq_perm(dz, dx))


def from_user(a, dy, dh, dc):
    return lax.ppermute(a, "user", user_perm(dy, dh, dc))


def from_both(a, dh, dx):
    pairs = []
    for s in range(NZ * NX):
        for u in range(NY * NXH * NC):
            pairs.append(((s ^ dx) * NY * NXH * NC + (u ^ (dh * NC)), s * NY * NXH * NC + u))
    return lax.ppermute(a, ("seq", "user"), pairs)


def layer_norm(entries):
    centre = jnp.mean(entries, axis=-1, keepdims=True)
    centred = entries - centre
    inverse = lax.rsqrt(jnp.mean(centred * centred, axis=-1, keepdims=True) + EPS)
    return centred * inverse, inverse


def norm_back(normed, inverse, upstream):
    first_term = jnp.mean(upstream, axis=-1, keepdims=True)
    second_term = jnp.mean(upstream * normed, axis=-1, keepdims=True)
    return inverse * (upstream - first_term - normed * second_term)


def dot(a, b):
    return jnp.dot(a, b, preferred_element_type=F32)


def dot_nt(a, b):
    return lax.dot_general(a, b, (((1,), (1,)), ((), ())), preferred_element_type=F32)


def dot_tn(a, b):
    return lax.dot_general(a, b, (((0,), (0,)), ((), ())), preferred_element_type=F32)


LIMIT = 56


def params(limit):
    return pltpu.CompilerParams(vmem_limit_bytes=limit << 20)


def ln_proj_kernel(count, at_ref, *refs):
    w_ref = refs[count]
    normed_ref, act_ref, slope_ref = refs[-3:]
    half = act_ref.shape[2]
    for k in range(count):

        @pl.when(pl.program_id(0) == k)
        def _():
            normed, _ = layer_norm(refs[k][...].astype(F32))
            normed_b = normed.astype(BF16)
            normed_ref[...] = normed_b.T
            projected = dot(normed_b, w_ref[...])
            tanh = jnp.tanh(0.5 * projected)
            sig = 0.5 + 0.5 * tanh
            silu = projected * sig
            act = silu.astype(BF16)
            slope = sig + silu * (1.0 - sig)
            for i in range(2):
                act_ref[i, 0] = act[i * half : (i + 1) * half]
                slope_ref[i, 0] = slope[i * half : (i + 1) * half]


def ln_proj(at, blocks, w_head, outs):
    rows, width = blocks[0].shape
    cols = w_head.shape[1]
    half, shards = rows // 2, NZ * NX
    by_half = pl.BlockSpec((2, 1, half, cols), lambda i, at_ref: (0, at_ref[i], 0, 0))
    in_specs = [pl.BlockSpec((rows, width), lambda i, at_ref: (0, 0))] * len(blocks)
    in_specs.append(pl.BlockSpec((width, cols), lambda i, at_ref: (0, 0)))
    aliases = {}
    if outs:
        in_specs += [pl.BlockSpec(memory_space=pl.ANY)] * 3
        aliases = {len(in_specs) + k - 2: k for k in range(3)}
    return pl.pallas_call(
        functools.partial(ln_proj_kernel, len(blocks)),
        grid_spec=pltpu.PrefetchScalarGridSpec(
            num_scalar_prefetch=1,
            grid=(len(blocks),),
            in_specs=in_specs,
            out_specs=(
                pl.BlockSpec((width, rows), lambda i, at_ref: (0, at_ref[i])),
                by_half,
                by_half,
            ),
        ),
        out_shape=(
            jax.ShapeDtypeStruct((width, rows * shards), BF16),
            jax.ShapeDtypeStruct((2, shards, half, cols), BF16),
            jax.ShapeDtypeStruct((2, shards, half, cols), F32),
        ),
        input_output_aliases=aliases,
        compiler_params=params(LIMIT),
        cost_estimate=pl.CostEstimate(
            flops=2 * rows * width * cols * len(blocks),
            bytes_accessed=3 * len(blocks) << 20,
            transcendentals=rows * cols * len(blocks),
        ),
        name="ln_proj",
    )(at, *blocks, w_head, *outs)


FQ, FK = 512, 512
BQ, BK = 256, 256
SCALE = HD ** (-0.5)


def tile_place(block):
    last = 2 * NZ * NX - 1
    return (block, 0) if block < NZ * NX else (last - block, HD)


def time_rows(ref, first, count, column, columns=1):
    parts = []
    for block in range(first // HD, (first + count) // HD):
        shard, row = tile_place(block)
        parts.append(ref[row // HD, shard, :, column * HD : (column + columns) * HD])
    return parts[0] if len(parts) == 1 else jnp.concatenate(parts, axis=0)


def tiles(length, rows, cols):
    key_row = lax.broadcasted_iota(jnp.int32, (cols, rows), 0)
    query_col = lax.broadcasted_iota(jnp.int32, (1, rows), 1)

    def seen(i, j, start):
        mask = key_row >= start - j
        if j + cols > i:
            mask = mask & (key_row <= query_col + (i - j))
        return mask

    return [(i, range(0, i + rows, cols)) for i in range(0, length, rows)], seen


def forward_kernel(act_ref, head_ref, att_ref, gate_ref, gg_ref, stats_ref, start_ref):
    length = att_ref.shape[1]
    rows = length // (NZ * NX)
    users = [head_ref[shard, rows:, :].astype(F32) for shard in range(NZ * NX)]
    places = [tile_place(block) for block in range(length // HD)]
    ids = jnp.concatenate([users[s][r // HD : r // HD + 1] for s, r in places], axis=1)
    first = jnp.zeros((1, length), F32)
    for v in range(3):
        count = jnp.sum(jnp.where(ids == v, 1.0, 0.0), axis=1, keepdims=True)
        first = first + jnp.where(ids > v, count, 0.0)
    start_ref[...] = first.astype(jnp.int32)
    values_t = [time_rows(act_ref, j, FK, 1).T for j in range(0, length, FK)]
    keys = [time_rows(act_ref, j, FK, 3) for j in range(0, length, FK)]
    queries_in, seen = tiles(length, FQ, FK)
    for i, keys_in in queries_in:
        at = slice(i, i + FQ)
        queries = time_rows(act_ref, i, FQ, 2)
        start = start_ref[:, at]
        total = None
        for j in keys_in:
            half = dot_nt(keys[j // FK], queries) * (0.5 * SCALE)
            weights = half + half * jnp.tanh(half)
            weights = jnp.where(seen(i, j, start), weights, 0.0).astype(BF16)
            term = dot(values_t[j // FK], weights)
            total = term if total is None else total + term
        att_ref[:, at] = total
        gate = time_rows(act_ref, i, FQ, 0).T
        parts = []
        for block in range(i // HD, (i + FQ) // HD):
            shard, row = tile_place(block)
            parts.append(head_ref[shard, row : row + HD, :])
        gg = jnp.concatenate(parts, axis=0).T
        gate_ref[:, at] = gate
        gg_ref[:, at] = gg
        grad_mixed = gg.astype(F32) * gate.astype(F32)
        mean = jnp.sum(total, axis=0, keepdims=True) * (1.0 / HD)
        centred = total - mean
        stats_ref[0:1, at] = mean
        stats_ref[1:2, at] = jnp.sum(centred * centred, axis=0, keepdims=True)
        stats_ref[2:3, at] = jnp.sum(grad_mixed, axis=0, keepdims=True)
        stats_ref[3:4, at] = jnp.sum(grad_mixed * centred, axis=0, keepdims=True)


def vmem():
    return pl.BlockSpec(memory_space=pltpu.VMEM)


def smem():
    return pl.BlockSpec(memory_space=pltpu.SMEM)


def forward(act, at_head):
    length = HD * 2 * NZ * NX
    return pl.pallas_call(
        forward_kernel,
        in_specs=[vmem()] * 2,
        out_specs=[vmem()] * 5,
        out_shape=(
            jax.ShapeDtypeStruct((HD, length), F32),
            jax.ShapeDtypeStruct((HD, length), BF16),
            jax.ShapeDtypeStruct((HD, length), BF16),
            jax.ShapeDtypeStruct((4, length), F32),
            jax.ShapeDtypeStruct((1, length), jnp.int32),
        ),
        compiler_params=params(LIMIT),
        cost_estimate=pl.CostEstimate(
            flops=8 * HD * length * length, bytes_accessed=6 << 20, transcendentals=length * length // 2
        ),
        name="attention_forward",
    )(act, at_head)


def mix_kernel(own_ref, one_ref, three_ref, two_ref, att_ref, gate_ref, gg_ref, slope_ref, early_ref, go_ref, got_ref):
    length = att_ref.shape[1]
    width = H * HD
    tile = 2 * HD
    heads = [ref[k] for ref in (own_ref, one_ref, three_ref, two_ref) for k in range(NX)]
    mean_all = sum(a[0:1] for a in heads) * (1.0 / H)
    apart = [a[0:1] - mean_all for a in heads]
    spread = sum(a[1:2] for a in heads) + HD * sum(d * d for d in apart)
    inverse_all = lax.rsqrt(spread * (1.0 / width) + EPS)
    first_all = sum(a[2:3] for a in heads) * (1.0 / width)
    second_all = inverse_all * sum(a[3:4] + d * a[2:3] for a, d in zip(heads, apart)) * (1.0 / width)
    for i in range(0, length, tile):
        at = slice(i, i + tile)
        gate = gate_ref[:, at].astype(F32)
        gg = gg_ref[:, at].astype(F32)
        inverse = inverse_all[:, at]
        mixed = (att_ref[:, at] - mean_all[:, at]) * inverse
        grad_att = inverse * (gg * gate - first_all[:, at] - mixed * second_all[:, at])
        got_ref[:, at] = grad_att.astype(BF16)
        go_ref[at, :] = grad_att.T.astype(BF16)
        gated = (mixed * gate).astype(BF16).T
        grad_u = ((gg * mixed).T * time_rows(slope_ref, i, tile, 0)).astype(BF16)
        for k in range(2):
            shard, row = tile_place(i // HD + k)
            early_ref[shard, row : row + HD, :HD] = gated[k * HD : (k + 1) * HD]
            early_ref[shard, row : row + HD, HD:] = grad_u[k * HD : (k + 1) * HD]


def mix(own, one, three, two, att, gate, gg, slope):
    length = att.shape[1]
    shards = NZ * NX
    whole = lambda shape: pl.BlockSpec(shape, lambda i: (0,) * len(shape))
    return pl.pallas_call(
        mix_kernel,
        grid=(1,),
        in_specs=[whole(own.shape)] * 4
        + [whole(att.shape)] * 3
        + [pl.BlockSpec(slope.shape[:3] + (HD,), lambda i: (0, 0, 0, 0))],
        out_specs=[whole((shards, length // shards, 2 * HD)), whole((length, HD)), whole((HD, length))],
        out_shape=(
            jax.ShapeDtypeStruct((shards, length // shards, 2 * HD), BF16),
            jax.ShapeDtypeStruct((length, HD), BF16),
            jax.ShapeDtypeStruct((HD, length), BF16),
        ),
        compiler_params=params(LIMIT),
        cost_estimate=pl.CostEstimate(flops=20 * HD * length, bytes_accessed=6 << 20, transcendentals=0),
        name="mix",
    )(own, one, three, two, att, gate, gg, slope)


def backward_kernel(act_ref, go_ref, got_ref, start_ref, early_ref, slope_hbm, back_ref, dk_ref, dv_ref, slope_ref, sem):
    length = go_ref.shape[0]
    copy = pltpu.make_async_copy(slope_hbm, slope_ref, sem)
    copy.start()
    back_ref[:, :, :HD] = early_ref[:, :, HD:]
    back_ref[:, :, 4 * HD :] = early_ref[:, :, :HD]
    keys = [time_rows(act_ref, j, BK, 3) for j in range(0, length, BK)]
    keys_t = [k.T for k in keys]
    values = [time_rows(act_ref, j, BK, 1) for j in range(0, length, BK)]
    queries_in, seen = tiles(length, BQ, BK)

    def put(first, column, value):
        value = (value * time_rows(slope_ref, first, value.shape[0], column)).astype(BF16)
        for k in range(value.shape[0] // HD):
            shard, row = tile_place(first // HD + k)
            back_ref[shard, row : row + HD, column * HD : (column + 1) * HD] = value[
                k * HD : (k + 1) * HD
            ]

    started = set()
    for i, keys_in in queries_in:
        at = slice(i, i + BQ)
        queries = time_rows(act_ref, i, BQ, 2)
        grad_out = go_ref[at, :]
        grad_out_t = got_ref[:, at]
        start = start_ref[:, at]
        total = None
        for j in keys_in:
            here = slice(j, j + BK)
            half = dot_nt(keys[j // BK], queries) * (0.5 * SCALE)
            tanh = jnp.tanh(half)
            weights = half + half * tanh
            sig = 0.5 + 0.5 * tanh
            slope = sig + weights * (1.0 - sig)
            mask = seen(i, j, start)
            ahead = dot(values[j // BK], grad_out_t)
            weights = jnp.where(mask, weights, 0.0).astype(BF16)
            slopes = jnp.where(mask, ahead * slope, 0.0).astype(BF16)
            dv = dot(weights, grad_out)
            dk = dot(slopes, queries)
            if j in started:
                dv_ref[here, :] += dv
                dk_ref[here, :] += dk
            else:
                dv_ref[here, :] = dv
                dk_ref[here, :] = dk
                started.add(j)
            term = dot(keys_t[j // BK], slopes)
            total = term if total is None else total + term
        if i == 0:
            copy.wait()
        put(i, 2, total.T * SCALE)
    for j in range(0, length, BK):
        put(j, 1, dv_ref[j : j + BK, :])
        put(j, 3, dk_ref[j : j + BK, :] * SCALE)


def backward(act, grad_out, grad_out_t, start, early, slope):
    length = start.shape[1]
    shards = NZ * NX
    return pl.pallas_call(
        backward_kernel,
        in_specs=[vmem()] * 5 + [pl.BlockSpec(memory_space=pl.ANY)],
        out_specs=vmem(),
        out_shape=jax.ShapeDtypeStruct((shards, length // shards, 5 * HD), BF16),
        scratch_shapes=[pltpu.VMEM((length, HD), F32)] * 2
        + [pltpu.VMEM(slope.shape, F32), pltpu.SemaphoreType.DMA],
        compiler_params=params(LIMIT),
        cost_estimate=pl.CostEstimate(
            flops=15 * HD * length * length, bytes_accessed=10 << 20, transcendentals=length * length // 2
        ),
        name="attention_backward",
    )(act, grad_out, grad_out_t, start, early, slope)


def terms_in_kernel(core_ref, normed_ref, grad_ref, keep_ref, send_ref, res_ref):
    shards, rows, cols = grad_ref.shape
    res_ref[...] = dot(normed_ref[...], grad_ref[...].reshape(shards * rows, cols))
    core = core_ref[0]
    for k in range(res_ref.shape[0] // HD):
        for pair in range(NY * NXH):
            mine = pl.multiple_of(k * HD + (pair * NC + core) * 8, 8)
            other = pl.multiple_of(k * HD + (pair * NC + 1 - core) * 8, 8)
            keep_ref[pair, k * 8 : (k + 1) * 8, :] = res_ref[pl.ds(mine, 8), :]
            send_ref[pair, k * 8 : (k + 1) * 8, :] = res_ref[pl.ds(other, 8), :]


def terms_in(core, normed_t, back):
    width, length = normed_t.shape
    shards, rows, _ = back.shape
    shape = jax.ShapeDtypeStruct((NY * NXH, 80, 4 * HD), F32)
    out_spec = pl.BlockSpec((NY * NXH, 16, 4 * HD), lambda g: (0, g, 0))
    return pl.pallas_call(
        terms_in_kernel,
        grid=(4,),
        in_specs=[
            smem(),
            pl.BlockSpec((width // 4, length), lambda g: (g, 0)),
            pl.BlockSpec((shards, rows, 4 * HD), lambda g: (0, 0, 0)),
        ],
        out_specs=[out_spec] * 2,
        out_shape=[shape] * 2,
        scratch_shapes=[pltpu.VMEM((width // 4, 4 * HD), F32)],
        compiler_params=params(LIMIT),
        cost_estimate=pl.CostEstimate(
            flops=2 * width * length * 4 * HD, bytes_accessed=9 << 20, transcendentals=0
        ),
        name="terms_in",
    )(core, normed_t, back)


def terms_out_kernel(core_ref, at_ref, gated_ref, *refs):
    keep_ref, send_ref, res_ref, gated_t_ref = refs[-4:]
    shards, rows, _ = gated_ref.shape

    @pl.when(pl.program_id(0) == 0)
    def _():
        for shard in range(shards):
            gated_t_ref[:, shard * rows : (shard + 1) * rows] = gated_ref[shard].T

    total = None
    for r in range(shards):
        here = pl.ds(pl.multiple_of(at_ref[r] * rows, rows), rows)
        term = dot(gated_t_ref[:, here], refs[r][...])
        total = term if total is None else total + term
    res_ref[...] = total
    core = core_ref[0]
    for pair in range(NY * NXH):
        for out_ref, who in ((keep_ref, core), (send_ref, 1 - core)):
            out_ref[pair] = res_ref[pl.ds(pl.multiple_of((pair * NC + who) * 8, 8), 8), :]


def terms_out(core, at, back, cots, keep, send):
    shards, rows, _ = back.shape
    width = cots[0].shape[1]
    length = shards * rows
    out_spec = pl.BlockSpec((NY * NXH, 8, 4 * HD), lambda g: (0, 8 + g, 0))
    return pl.pallas_call(
        terms_out_kernel,
        grid=(2,),
        in_specs=[smem(), smem(), pl.BlockSpec((shards, rows, HD), lambda g: (0, 0, 4))]
        + [pl.BlockSpec((rows, width // 2), lambda g: (0, g))] * shards
        + [pl.BlockSpec(memory_space=pl.ANY)] * 2,
        out_specs=[out_spec] * 2,
        out_shape=[jax.ShapeDtypeStruct(keep.shape, F32)] * 2,
        scratch_shapes=[pltpu.VMEM((HD, width // 2), F32), pltpu.VMEM((HD, length), BF16)],
        input_output_aliases={3 + shards: 0, 4 + shards: 1},
        compiler_params=params(LIMIT),
        cost_estimate=pl.CostEstimate(
            flops=2 * HD * width * length, bytes_accessed=6 << 20, transcendentals=0
        ),
        name="terms_out",
    )(core, at, back, *cots, keep, send)


def small(kernel, name, scalars, arrays, outs, scratch=(), limit=12):
    size = sum(a.size * a.dtype.itemsize for a in arrays)
    return pl.pallas_call(
        kernel,
        in_specs=[smem()] + [vmem()] * len(arrays),
        out_specs=[vmem()] * len(outs),
        out_shape=[jax.ShapeDtypeStruct(shape, dtype) for shape, dtype in outs],
        scratch_shapes=list(scratch),
        compiler_params=params(limit),
        cost_estimate=pl.CostEstimate(flops=size, bytes_accessed=2 * size, transcendentals=0),
        name=name,
    )(scalars, *arrays)


def core_sum_kernel(pos_ref, keep_ref, got_ref, own_ref, one_ref, three_ref, two_ref):
    y = pos_ref[0]
    for d, out_ref in ((0, own_ref), (1, one_ref), (3, three_ref), (2, two_ref)):
        here = pl.ds(((y - d + NY) % NY) * NXH, NXH)
        out_ref[...] = (keep_ref[here] + got_ref[here]).astype(out_ref.dtype)


def y_sum_kernel(pos_ref, own_ref, a_ref, b_ref, c_ref, keep_ref, same_ref, one_ref, two_ref, sum_ref):
    xh, x = pos_ref[1], pos_ref[2]
    sum_ref[...] = own_ref[...] + (
        a_ref[...].astype(F32) + b_ref[...].astype(F32) + c_ref[...].astype(F32)
    )

    def slab(out_ref, h, l):
        for k in range(NZ):
            out_ref[k * 8 : (k + 1) * 8, :] = sum_ref[
                h, pl.ds(pl.multiple_of((k * NX + l) * 8, 8), 8), :
            ]

    slab(keep_ref, xh, x)
    keep_ref[32:, :] = sum_ref[xh, 64:, :]
    slab(same_ref, 1 - xh, x)
    same_ref[32:, :] = sum_ref[1 - xh, 64:, :]
    slab(one_ref, xh, 1 - x)
    slab(two_ref, 1 - xh, 1 - x)


def x_sum_kernel(pos_ref, keep_ref, same_ref, a_ref, b_ref, own_ref, one_ref, three_ref, two_ref, out_ref, sum_ref):
    z, x = pos_ref[3], pos_ref[2]
    mine = keep_ref[...] + same_ref[...]
    sum_ref[x] = mine[:32]
    sum_ref[1 - x] = a_ref[...] + b_ref[...]
    out_ref[...] = mine[32:]
    for d, to_ref in ((0, own_ref), (1, one_ref), (3, three_ref), (2, two_ref)):
        here = pl.ds(pl.multiple_of(((z - d + NZ) % NZ) * 8, 8), 8)
        for l in range(NX):
            to_ref[l * 8 : (l + 1) * 8, :] = sum_ref[l, here, :]


def z_place_kernel(factor, pos_ref, own_ref, one_ref, three_ref, two_ref, out_ref, w_in_ref, w_out_ref):
    z = pos_ref[3]
    for d, ref in ((0, own_ref), (1, one_ref), (3, three_ref), (2, two_ref)):
        for l in range(NX):
            for k in range(4):
                at = pl.multiple_of((k * H + ((z + d) % NZ) * NX + l) * HD, HD)
                w_in_ref[:, pl.ds(at, HD)] = (
                    ref[l * 8 : (l + 1) * 8, k * HD : (k + 1) * HD] * factor
                )
    w_out_ref[:, : 4 * HD] = out_ref[:8] * factor
    w_out_ref[:, 4 * HD :] = out_ref[8:] * factor


def columns(ref):
    return jnp.concatenate([ref[h] for h in range(H)], axis=1)


def shard_out_kernel(gated_ref, grad_ref, w_in_ref, w_out_ref, hist_ref, layer_ref, acc_ref):
    term = dot_nt(columns(grad_ref), w_in_ref[...])

    @pl.when(pl.program_id(0) == 0)
    def _():
        hist = hist_ref[...].astype(F32)
        layer_ref[...] = (hist + dot(columns(gated_ref), w_out_ref[...])).astype(BF16)
        acc_ref[...] = term

    @pl.when(pl.program_id(0) > 0)
    def _():
        acc_ref[...] += term


def shard_grad_kernel(grad_ref, w_in_ref, hist_ref, cot_ref, half_ref, grad_hist_ref, acc_ref):
    term = dot_nt(columns(grad_ref), w_in_ref[...])

    @pl.when(pl.program_id(0) == 0)
    def _():
        acc_ref[...] = half_ref[...] + term

    @pl.when(pl.program_id(0) > 0)
    def _():
        normed, inverse = layer_norm(hist_ref[...].astype(F32))
        grad = norm_back(normed, inverse, acc_ref[...] + term)
        grad_hist_ref[...] = (cot_ref[...].astype(F32) + grad).astype(BF16)


def shard_out(back, w_in, w_out, hist):
    rows, width = hist.shape
    whole = lambda a: pl.BlockSpec(a.shape, lambda k: (0,) * a.ndim)
    return pl.pallas_call(
        shard_out_kernel,
        grid=(2,),
        in_specs=[
            pl.BlockSpec((H, rows, HD), lambda k: (0, 0, 4)),
            pl.BlockSpec((H, rows, HD), lambda k: (0, 0, k)),
            pl.BlockSpec((width, width), lambda k: (0, k)),
            whole(w_out),
            whole(hist),
        ],
        out_specs=[whole(hist)] * 2,
        out_shape=[jax.ShapeDtypeStruct(hist.shape, BF16), jax.ShapeDtypeStruct(hist.shape, F32)],
        compiler_params=params(32),
        cost_estimate=pl.CostEstimate(
            flops=6 * rows * width * width, bytes_accessed=8 << 20, transcendentals=0
        ),
        name="shard_out",
    )(back, back, w_in, w_out, hist)


def shard_grad(back, w_in, hist, cot, half):
    rows, width = hist.shape
    whole = lambda a: pl.BlockSpec(a.shape, lambda k: (0,) * a.ndim)
    return pl.pallas_call(
        shard_grad_kernel,
        grid=(2,),
        in_specs=[
            pl.BlockSpec((H, rows, HD), lambda k: (0, 0, 2 + k)),
            pl.BlockSpec((width, width), lambda k: (0, 2 + k)),
            whole(hist),
            whole(cot),
            whole(half),
        ],
        out_specs=whole(hist),
        out_shape=jax.ShapeDtypeStruct(hist.shape, BF16),
        scratch_shapes=[pltpu.VMEM((rows, width), F32)],
        compiler_params=params(32),
        cost_estimate=pl.CostEstimate(
            flops=4 * rows * width * width, bytes_accessed=8 << 20, transcendentals=0
        ),
        name="shard_grad",
    )(back, w_in, hist, cot, half)


def local(history, segment_ids, w_in, w_out, cotangent):
    hist = history[0]
    cot = cotangent[0]
    rows, width = hist.shape
    length = rows * NZ * NX
    s = lax.axis_index("seq")
    u = lax.axis_index("user")
    z, x = s // NX, s % NX
    y, xh, core = u // (NXH * NC), (u // NC) % NXH, u % NC

    users = NY * NXH * NC
    tie = lax.optimization_barrier
    w_head = jnp.concatenate(
        [lax.dynamic_slice(w_in, (0, i * width + s * HD), (width, HD)) for i in range(4)], axis=1
    )

    def place_of(key):
        return ((z + key[0]) % NZ) * NX + (x ^ key[1])

    def project(got, outs):
        at = jnp.stack([place_of(key) for key in got])
        return ln_proj(at, list(got.values()), w_head, outs)

    got = {
        (1, 0): from_seq(hist, 1, 0),
        (3, 0): from_seq(hist, 3, 0),
        (0, 1): from_seq(hist, 0, 1),
    }
    outs = project({(0, 0): hist}, ())
    grad_gated_own = dot_nt(cot, w_out).astype(BF16).reshape(rows, H, HD).transpose(1, 0, 2)
    ids = segment_ids[0].astype(BF16).reshape(2, HD)
    ids = jnp.pad(ids, ((0, 14), (0, 0)))
    to_heads = jnp.concatenate(
        [
            grad_gated_own,
            jnp.broadcast_to(ids[None], (H, 16, HD)),
        ],
        axis=1,
    )
    at_head = lax.all_to_all(to_heads, "seq", 0, 0, tiled=True)
    got, outs = tie((got, outs))
    more = {
        (2, 0): from_seq(got[1, 0], 1, 0),
        (3, 1): from_seq(got[0, 1], 3, 0),
        (1, 1): from_seq(got[1, 0], 0, 1),
    }
    outs = project(got, outs)
    more, outs, cot_next, at_head = tie((more, outs, cot, at_head))
    last = {(2, 1): from_seq(more[2, 0], 0, 1)}
    cots = {(1, 0): from_seq(cot_next, 1, 0), (3, 0): from_seq(cot_next, 3, 0)}
    outs = project(more, outs)
    last, cots, outs = tie((last, cots, outs))
    fresh = {(0, 1): from_seq(cot_next, 0, 1), (2, 0): from_seq(cots[1, 0], 1, 0)}
    normed_t, act, slope = project(last, outs)
    att, gate_t, gg_t, stats, start = forward(act, at_head)
    stats, fresh = tie((stats, fresh))
    cots.update(fresh)
    pair = jnp.stack([stats, from_seq(stats, 0, 1)])
    others = [from_seq(pair, dz, 0) for dz in (1, 3, 2)]
    early, grad_out, grad_out_t = mix(pair, *others, att, gate_t, gg_t, slope)
    early, grad_out, grad_out_t, cots = tie((early, grad_out, grad_out_t, cots))
    fresh = {
        (2, 1): from_seq(cots[2, 0], 0, 1),
        (1, 1): from_seq(cots[0, 1], 1, 0),
        (3, 1): from_seq(cots[0, 1], 3, 0),
    }
    back = backward(act, grad_out, grad_out_t, start, early, slope)
    back, fresh = tie((back, fresh))
    cots.update(fresh)
    cots[0, 0] = cot
    back_tok = lax.all_to_all(back, "seq", 0, 0, tiled=True)

    at_core = core.reshape(1)
    keep, send = terms_in(at_core, normed_t, back)
    places = jnp.stack([place_of(key) for key in cots])
    keep, send = terms_out(at_core, places, back, list(cots.values()), keep, send)
    at = jnp.stack([y, xh, x, z])
    n = 4 * HD
    got = from_user(send, 0, 0, 1)
    own, *sends = small(
        core_sum_kernel,
        "core_sum",
        at,
        [keep, got],
        [((NXH, 80, n), F32)] + [((NXH, 80, n), BF16)] * 3,
        limit=LIMIT,
    )
    own, sends = tie((own, sends))
    sends = [from_user(a, d, 0, 0) for a, d in zip(sends, (1, 3, 2))]
    layer_out, half = shard_out(back_tok, w_in, w_out, hist)
    sends, layer_out, half = tie((sends, layer_out, half))
    keep, same, one, two = small(
        y_sum_kernel,
        "y_sum",
        at,
        [own, *sends],
        [((48, n), F32)] * 2 + [((32, n), F32)] * 2,
        [pltpu.VMEM((NXH, 80, n), F32)],
    )
    same = from_both(same, 1, 0)
    one = from_both(one, 0, 1)
    two = from_both(two, 1, 1)
    grad_history = shard_grad(back_tok, w_in, hist, cot, half)
    same, one, two, grad_history = tie((same, one, two, grad_history))
    own, *sends, own_out = small(
        x_sum_kernel,
        "x_sum",
        at,
        [keep, same, one, two],
        [((16, n), F32)] * 5,
        [pltpu.VMEM((NX, 32, n), F32)],
    )
    sends = [from_seq(a, d, 0) for a, d in zip(sends, (1, 3, 2))]
    factor = (length * users) ** (-0.5)
    grad_w_in, grad_w_out = small(
        functools.partial(z_place_kernel, factor),
        "z_place",
        at,
        [own, *sends, own_out],
        [((8, 4 * width), F32), ((8, width), F32)],
    )
    return layer_out[None], grad_history[None], grad_w_in, grad_w_out


def solution(mesh):
    in_specs = (P("user", "seq", None), P("user", "seq"), P(), P(), P("user", "seq", None))
    out_specs = (
        P("user", "seq", None),
        P("user", "seq", None),
        P(("seq", "user"), None),
        P(("seq", "user"), None),
    )
    return jax.shard_map(local, mesh=mesh, in_specs=in_specs, out_specs=out_specs, check_vma=False)
```

```python
import functools

import jax
import jax.numpy as jnp
from jax import lax
from jax.experimental import pallas as pl
from jax.experimental.pallas import tpu as pltpu
from jax.sharding import PartitionSpec as P

F32 = jnp.float32
BF16 = jnp.bfloat16
EPS = 1e-05
H = 8
HD = 128
NZ, NX = 4, 2
NY, NXH, NC = 4, 2, 2


def seq_perm(dz, dx):
    return [
        (((z + dz) % NZ) * NX + (x ^ dx), z * NX + x) for z in range(NZ) for x in range(NX)
    ]


def user_perm(dy, dh, dc):
    return [
        ((((y + dy) % NY) * NXH + (h ^ dh)) * NC + (c ^ dc), (y * NXH + h) * NC + c)
        for y in range(NY)
        for h in range(NXH)
        for c in range(NC)
    ]


def from_seq(a, dz, dx):
    return lax.ppermute(a, "seq", seq_perm(dz, dx))


def from_user(a, dy, dh, dc):
    return lax.ppermute(a, "user", user_perm(dy, dh, dc))


def from_both(a, dh, dx):
    pairs = []
    for s in range(NZ * NX):
        for u in range(NY * NXH * NC):
            pairs.append(((s ^ dx) * NY * NXH * NC + (u ^ (dh * NC)), s * NY * NXH * NC + u))
    return lax.ppermute(a, ("seq", "user"), pairs)


def layer_norm(entries):
    centre = jnp.mean(entries, axis=-1, keepdims=True)
    centred = entries - centre
    inverse = lax.rsqrt(jnp.mean(centred * centred, axis=-1, keepdims=True) + EPS)
    return centred * inverse, inverse


def norm_back(normed, inverse, upstream):
    first_term = jnp.mean(upstream, axis=-1, keepdims=True)
    second_term = jnp.mean(upstream * normed, axis=-1, keepdims=True)
    return inverse * (upstream - first_term - normed * second_term)


def dot(a, b):
    return jnp.dot(a, b, preferred_element_type=F32)


def dot_nt(a, b):
    return lax.dot_general(a, b, (((1,), (1,)), ((), ())), preferred_element_type=F32)


def dot_tn(a, b):
    return lax.dot_general(a, b, (((0,), (0,)), ((), ())), preferred_element_type=F32)


LIMIT = 56


def params(limit):
    return pltpu.CompilerParams(vmem_limit_bytes=limit << 20)


def ln_proj_kernel(count, at_ref, *refs):
    w_ref = refs[count]
    normed_ref, act_ref, slope_ref = refs[-3:]
    half = act_ref.shape[2]
    for k in range(count):

        @pl.when(pl.program_id(0) == k)
        def _():
            normed, _ = layer_norm(refs[k][...].astype(F32))
            normed_b = normed.astype(BF16)
            normed_ref[...] = normed_b.T
            projected = dot(normed_b, w_ref[...])
            tanh = jnp.tanh(0.5 * projected)
            sig = 0.5 + 0.5 * tanh
            silu = projected * sig
            act = silu.astype(BF16)
            slope = sig + silu * (1.0 - sig)
            for i in range(2):
                act_ref[i, 0] = act[i * half : (i + 1) * half]
                slope_ref[i, 0] = slope[i * half : (i + 1) * half]


def ln_proj(at, blocks, w_head, outs):
    rows, width = blocks[0].shape
    cols = w_head.shape[1]
    half, shards = rows // 2, NZ * NX
    by_half = pl.BlockSpec((2, 1, half, cols), lambda i, at_ref: (0, at_ref[i], 0, 0))
    in_specs = [pl.BlockSpec((rows, width), lambda i, at_ref: (0, 0))] * len(blocks)
    in_specs.append(pl.BlockSpec((width, cols), lambda i, at_ref: (0, 0)))
    aliases = {}
    if outs:
        in_specs += [pl.BlockSpec(memory_space=pl.ANY)] * 3
        aliases = {len(in_specs) + k - 2: k for k in range(3)}
    return pl.pallas_call(
        functools.partial(ln_proj_kernel, len(blocks)),
        grid_spec=pltpu.PrefetchScalarGridSpec(
            num_scalar_prefetch=1,
            grid=(len(blocks),),
            in_specs=in_specs,
            out_specs=(
                pl.BlockSpec((width, rows), lambda i, at_ref: (0, at_ref[i])),
                by_half,
                by_half,
            ),
        ),
        out_shape=(
            jax.ShapeDtypeStruct((width, rows * shards), BF16),
            jax.ShapeDtypeStruct((2, shards, half, cols), BF16),
            jax.ShapeDtypeStruct((2, shards, half, cols), F32),
        ),
        input_output_aliases=aliases,
        compiler_params=params(LIMIT),
        cost_estimate=pl.CostEstimate(
            flops=2 * rows * width * cols * len(blocks),
            bytes_accessed=3 * len(blocks) << 20,
            transcendentals=rows * cols * len(blocks),
        ),
        name="ln_proj",
    )(at, *blocks, w_head, *outs)


FQ, FK = 512, 512
BQ, BK = 512, 256
SCALE = HD ** (-0.5)
UNSEEN = -1024.0


def tile_place(block):
    last = 2 * NZ * NX - 1
    return (block, 0) if block < NZ * NX else (last - block, HD)


def time_rows(ref, first, count, column, columns=1):
    parts = []
    for block in range(first // HD, (first + count) // HD):
        shard, row = tile_place(block)
        parts.append(ref[row // HD, shard, :, column * HD : (column + columns) * HD])
    return parts[0] if len(parts) == 1 else jnp.concatenate(parts, axis=0)


def tiles(length, rows, cols):
    key_row = lax.broadcasted_iota(jnp.int32, (cols, rows), 0)
    query_col = lax.broadcasted_iota(jnp.int32, (1, rows), 1)

    def seen(i, j, start):
        mask = key_row >= start - j
        if j + cols > i:
            mask = mask & (key_row <= query_col + (i - j))
        return mask

    return [(i, range(0, i + rows, cols)) for i in range(0, length, rows)], seen


def forward_kernel(act_ref, head_ref, att_ref, gate_ref, gg_ref, stats_ref, start_ref):
    length = att_ref.shape[1]
    rows = length // (NZ * NX)
    users = [head_ref[shard, rows:, :].astype(F32) for shard in range(NZ * NX)]
    places = [tile_place(block) for block in range(length // HD)]
    ids = jnp.concatenate([users[s][r // HD : r // HD + 1] for s, r in places], axis=1)
    first = jnp.zeros((1, length), F32)
    for v in range(3):
        count = jnp.sum(jnp.where(ids == v, 1.0, 0.0), axis=1, keepdims=True)
        first = first + jnp.where(ids > v, count, 0.0)
    start_ref[...] = first.astype(jnp.int32)
    values_t = [time_rows(act_ref, j, FK, 1).T for j in range(0, length, FK)]
    keys = [time_rows(act_ref, j, FK, 3) for j in range(0, length, FK)]
    queries_in, seen = tiles(length, FQ, FK)
    for i, keys_in in queries_in:
        at = slice(i, i + FQ)
        queries = time_rows(act_ref, i, FQ, 2)
        start = start_ref[:, at]
        total = None
        for j in keys_in:
            half = dot_nt(keys[j // FK], queries) * (0.5 * SCALE)
            half = jnp.where(seen(i, j, start), half, UNSEEN)
            weights = (half + half * jnp.tanh(half)).astype(BF16)
            term = dot(values_t[j // FK], weights)
            total = term if total is None else total + term
        att_ref[:, at] = total
        gate = time_rows(act_ref, i, FQ, 0).T
        parts = []
        for block in range(i // HD, (i + FQ) // HD):
            shard, row = tile_place(block)
            parts.append(head_ref[shard, row : row + HD, :])
        gg = jnp.concatenate(parts, axis=0).T
        gate_ref[:, at] = gate
        gg_ref[:, at] = gg
        grad_mixed = gg.astype(F32) * gate.astype(F32)
        mean = jnp.sum(total, axis=0, keepdims=True) * (1.0 / HD)
        centred = total - mean
        stats_ref[0:1, at] = mean
        stats_ref[1:2, at] = jnp.sum(centred * centred, axis=0, keepdims=True)
        stats_ref[2:3, at] = jnp.sum(grad_mixed, axis=0, keepdims=True)
        stats_ref[3:4, at] = jnp.sum(grad_mixed * centred, axis=0, keepdims=True)


def vmem():
    return pl.BlockSpec(memory_space=pltpu.VMEM)


def smem():
    return pl.BlockSpec(memory_space=pltpu.SMEM)


def forward(act, at_head):
    length = HD * 2 * NZ * NX
    return pl.pallas_call(
        forward_kernel,
        in_specs=[vmem()] * 2,
        out_specs=[vmem()] * 5,
        out_shape=(
            jax.ShapeDtypeStruct((HD, length), F32),
            jax.ShapeDtypeStruct((HD, length), BF16),
            jax.ShapeDtypeStruct((HD, length), BF16),
            jax.ShapeDtypeStruct((4, length), F32),
            jax.ShapeDtypeStruct((1, length), jnp.int32),
        ),
        compiler_params=params(LIMIT),
        cost_estimate=pl.CostEstimate(
            flops=8 * HD * length * length, bytes_accessed=6 << 20, transcendentals=length * length // 2
        ),
        name="attention_forward",
    )(act, at_head)


def mix_kernel(own_ref, one_ref, three_ref, two_ref, att_ref, gate_ref, gg_ref, slope_ref, early_ref, go_ref, got_ref):
    length = att_ref.shape[1]
    width = H * HD
    tile = 2 * HD
    heads = [ref[k] for ref in (own_ref, one_ref, three_ref, two_ref) for k in range(NX)]
    mean_all = sum(a[0:1] for a in heads) * (1.0 / H)
    apart = [a[0:1] - mean_all for a in heads]
    spread = sum(a[1:2] for a in heads) + HD * sum(d * d for d in apart)
    inverse_all = lax.rsqrt(spread * (1.0 / width) + EPS)
    first_all = sum(a[2:3] for a in heads) * (1.0 / width)
    second_all = inverse_all * sum(a[3:4] + d * a[2:3] for a, d in zip(heads, apart)) * (1.0 / width)
    for i in range(0, length, tile):
        at = slice(i, i + tile)
        gate = gate_ref[:, at].astype(F32)
        gg = gg_ref[:, at].astype(F32)
        inverse = inverse_all[:, at]
        mixed = (att_ref[:, at] - mean_all[:, at]) * inverse
        grad_att = inverse * (gg * gate - first_all[:, at] - mixed * second_all[:, at])
        got_ref[:, at] = grad_att.astype(BF16)
        go_ref[at, :] = grad_att.T.astype(BF16)
        gated = (mixed * gate).astype(BF16).T
        grad_u = ((gg * mixed).T * time_rows(slope_ref, i, tile, 0)).astype(BF16)
        for k in range(2):
            shard, row = tile_place(i // HD + k)
            early_ref[shard, row : row + HD, :HD] = gated[k * HD : (k + 1) * HD]
            early_ref[shard, row : row + HD, HD:] = grad_u[k * HD : (k + 1) * HD]


def mix(own, one, three, two, att, gate, gg, slope):
    length = att.shape[1]
    shards = NZ * NX
    whole = lambda shape: pl.BlockSpec(shape, lambda i: (0,) * len(shape))
    return pl.pallas_call(
        mix_kernel,
        grid=(1,),
        in_specs=[whole(own.shape)] * 4
        + [whole(att.shape)] * 3
        + [pl.BlockSpec(slope.shape[:3] + (HD,), lambda i: (0, 0, 0, 0))],
        out_specs=[whole((shards, length // shards, 2 * HD)), whole((length, HD)), whole((HD, length))],
        out_shape=(
            jax.ShapeDtypeStruct((shards, length // shards, 2 * HD), BF16),
            jax.ShapeDtypeStruct((length, HD), BF16),
            jax.ShapeDtypeStruct((HD, length), BF16),
        ),
        compiler_params=params(LIMIT),
        cost_estimate=pl.CostEstimate(flops=20 * HD * length, bytes_accessed=6 << 20, transcendentals=0),
        name="mix",
    )(own, one, three, two, att, gate, gg, slope)


def backward_kernel(act_ref, go_ref, got_ref, start_ref, early_ref, slope_hbm, back_ref, dk_ref, dv_ref, slope_ref, sem):
    length = go_ref.shape[0]
    copy = pltpu.make_async_copy(slope_hbm, slope_ref, sem)
    copy.start()
    back_ref[:, :, :HD] = early_ref[:, :, HD:]
    back_ref[:, :, 4 * HD :] = early_ref[:, :, :HD]
    keys = [time_rows(act_ref, j, BK, 3) for j in range(0, length, BK)]
    keys_t = [k.T for k in keys]
    values = [time_rows(act_ref, j, BK, 1) for j in range(0, length, BK)]
    queries_in, seen = tiles(length, BQ, BK)

    def put(first, column, value):
        value = (value * time_rows(slope_ref, first, value.shape[0], column)).astype(BF16)
        for k in range(value.shape[0] // HD):
            shard, row = tile_place(first // HD + k)
            back_ref[shard, row : row + HD, column * HD : (column + 1) * HD] = value[
                k * HD : (k + 1) * HD
            ]

    started = set()
    for i, keys_in in queries_in:
        at = slice(i, i + BQ)
        queries = time_rows(act_ref, i, BQ, 2)
        grad_out = go_ref[at, :]
        grad_out_t = got_ref[:, at]
        start = start_ref[:, at]
        total = None
        for j in keys_in:
            here = slice(j, j + BK)
            half = dot_nt(keys[j // BK], queries) * (0.5 * SCALE)
            half = jnp.where(seen(i, j, start), half, UNSEEN)
            tanh = jnp.tanh(half)
            weights = half + half * tanh
            sig = 0.5 + 0.5 * tanh
            slope = sig + weights * (1.0 - sig)
            ahead = dot(values[j // BK], grad_out_t)
            weights = weights.astype(BF16)
            slopes = (ahead * slope).astype(BF16)
            dv = dot(weights, grad_out)
            dk = dot(slopes, queries)
            if j in started:
                dv_ref[here, :] += dv
                dk_ref[here, :] += dk
            else:
                dv_ref[here, :] = dv
                dk_ref[here, :] = dk
                started.add(j)
            term = dot(keys_t[j // BK], slopes)
            total = term if total is None else total + term
        if i == 0:
            copy.wait()
        put(i, 2, total.T * SCALE)
    for j in range(0, length, BK):
        put(j, 1, dv_ref[j : j + BK, :])
        put(j, 3, dk_ref[j : j + BK, :] * SCALE)


def backward(act, grad_out, grad_out_t, start, early, slope):
    length = start.shape[1]
    shards = NZ * NX
    return pl.pallas_call(
        backward_kernel,
        in_specs=[vmem()] * 5 + [pl.BlockSpec(memory_space=pl.ANY)],
        out_specs=vmem(),
        out_shape=jax.ShapeDtypeStruct((shards, length // shards, 5 * HD), BF16),
        scratch_shapes=[pltpu.VMEM((length, HD), F32)] * 2
        + [pltpu.VMEM(slope.shape, F32), pltpu.SemaphoreType.DMA],
        compiler_params=params(LIMIT),
        cost_estimate=pl.CostEstimate(
            flops=15 * HD * length * length, bytes_accessed=10 << 20, transcendentals=length * length // 2
        ),
        name="attention_backward",
    )(act, grad_out, grad_out_t, start, early, slope)


def terms_in_kernel(core_ref, normed_ref, grad_ref, keep_ref, send_ref, res_ref):
    shards, rows, cols = grad_ref.shape
    res_ref[...] = dot(normed_ref[...], grad_ref[...].reshape(shards * rows, cols))
    core = core_ref[0]
    for k in range(res_ref.shape[0] // HD):
        for pair in range(NY * NXH):
            mine = pl.multiple_of(k * HD + (pair * NC + core) * 8, 8)
            other = pl.multiple_of(k * HD + (pair * NC + 1 - core) * 8, 8)
            keep_ref[pair, k * 8 : (k + 1) * 8, :] = res_ref[pl.ds(mine, 8), :]
            send_ref[pair, k * 8 : (k + 1) * 8, :] = res_ref[pl.ds(other, 8), :]


def terms_in(core, normed_t, back):
    width, length = normed_t.shape
    shards, rows, _ = back.shape
    shape = jax.ShapeDtypeStruct((NY * NXH, 64, 4 * HD), F32)
    out_spec = pl.BlockSpec((NY * NXH, 16, 4 * HD), lambda g: (0, g, 0))
    return pl.pallas_call(
        terms_in_kernel,
        grid=(4,),
        in_specs=[
            smem(),
            pl.BlockSpec((width // 4, length), lambda g: (g, 0)),
            pl.BlockSpec((shards, rows, 4 * HD), lambda g: (0, 0, 0)),
        ],
        out_specs=[out_spec] * 2,
        out_shape=[shape] * 2,
        scratch_shapes=[pltpu.VMEM((width // 4, 4 * HD), F32)],
        compiler_params=params(LIMIT),
        cost_estimate=pl.CostEstimate(
            flops=2 * width * length * 4 * HD, bytes_accessed=9 << 20, transcendentals=0
        ),
        name="terms_in",
    )(core, normed_t, back)


def terms_out_kernel(core_ref, at_ref, gated_ref, *refs):
    keep_ref, send_ref, res_ref, gated_t_ref = refs[-4:]
    shards, rows, _ = gated_ref.shape

    @pl.when(pl.program_id(0) == 0)
    def _():
        for shard in range(shards):
            gated_t_ref[:, shard * rows : (shard + 1) * rows] = gated_ref[shard].T

    total = None
    for r in range(shards):
        here = pl.ds(pl.multiple_of(at_ref[r] * rows, rows), rows)
        term = dot(gated_t_ref[:, here], refs[r][...])
        total = term if total is None else total + term
    res_ref[...] = total
    core = core_ref[0]
    for pair in range(NY * NXH):
        for out_ref, who in ((keep_ref, core), (send_ref, 1 - core)):
            out_ref[pair] = res_ref[pl.ds(pl.multiple_of((pair * NC + who) * 8, 8), 8), :]


def terms_out(core, at, back, cots):
    shards, rows, _ = back.shape
    width = cots[0].shape[1]
    length = shards * rows
    out_spec = pl.BlockSpec((NY * NXH, 8, 4 * HD), lambda g: (0, g, 0))
    return pl.pallas_call(
        terms_out_kernel,
        grid=(2,),
        in_specs=[smem(), smem(), pl.BlockSpec((shards, rows, HD), lambda g: (0, 0, 4))]
        + [pl.BlockSpec((rows, width // 2), lambda g: (0, g))] * shards,
        out_specs=[out_spec] * 2,
        out_shape=[jax.ShapeDtypeStruct((NY * NXH, 16, 4 * HD), F32)] * 2,
        scratch_shapes=[pltpu.VMEM((HD, width // 2), F32), pltpu.VMEM((HD, length), BF16)],
        compiler_params=params(LIMIT),
        cost_estimate=pl.CostEstimate(
            flops=2 * HD * width * length, bytes_accessed=6 << 20, transcendentals=0
        ),
        name="terms_out",
    )(core, at, back, *cots)


def small(kernel, name, scalars, arrays, outs, scratch=(), limit=12):
    size = sum(a.size * a.dtype.itemsize for a in arrays)
    return pl.pallas_call(
        kernel,
        in_specs=[smem()] + [vmem()] * len(arrays),
        out_specs=[vmem()] * len(outs),
        out_shape=[jax.ShapeDtypeStruct(shape, dtype) for shape, dtype in outs],
        scratch_shapes=list(scratch),
        compiler_params=params(limit),
        cost_estimate=pl.CostEstimate(flops=size, bytes_accessed=2 * size, transcendentals=0),
        name=name,
    )(scalars, *arrays)


def core_sum_kernel(pos_ref, keep_ref, got_ref, keep_out_ref, got_out_ref, own_ref, one_ref, three_ref, two_ref):
    y = pos_ref[0]
    for d, to_ref in ((0, own_ref), (1, one_ref), (3, three_ref), (2, two_ref)):
        here = pl.ds(((y - d + NY) % NY) * NXH, NXH)
        to_ref[:, :64, :] = (keep_ref[here] + got_ref[here]).astype(to_ref.dtype)
        to_ref[:, 64:, :] = (keep_out_ref[here] + got_out_ref[here]).astype(to_ref.dtype)


def y_sum_kernel(pos_ref, own_ref, a_ref, b_ref, c_ref, keep_ref, same_ref, one_ref, two_ref, sum_ref):
    xh, x = pos_ref[1], pos_ref[2]
    sum_ref[...] = own_ref[...] + (
        a_ref[...].astype(F32) + b_ref[...].astype(F32) + c_ref[...].astype(F32)
    )

    def slab(out_ref, h, l):
        for k in range(NZ):
            out_ref[k * 8 : (k + 1) * 8, :] = sum_ref[
                h, pl.ds(pl.multiple_of((k * NX + l) * 8, 8), 8), :
            ]

    slab(keep_ref, xh, x)
    keep_ref[32:, :] = sum_ref[xh, 64:, :]
    slab(same_ref, 1 - xh, x)
    same_ref[32:, :] = sum_ref[1 - xh, 64:, :]
    slab(one_ref, xh, 1 - x)
    slab(two_ref, 1 - xh, 1 - x)


def x_sum_kernel(pos_ref, keep_ref, same_ref, a_ref, b_ref, own_ref, one_ref, three_ref, two_ref, out_ref, sum_ref):
    z, x = pos_ref[3], pos_ref[2]
    mine = keep_ref[...] + same_ref[...]
    sum_ref[x] = mine[:32]
    sum_ref[1 - x] = a_ref[...] + b_ref[...]
    out_ref[...] = mine[32:]
    for d, to_ref in ((0, own_ref), (1, one_ref), (3, three_ref), (2, two_ref)):
        here = pl.ds(pl.multiple_of(((z - d + NZ) % NZ) * 8, 8), 8)
        for l in range(NX):
            to_ref[l * 8 : (l + 1) * 8, :] = sum_ref[l, here, :]


def z_place_kernel(factor, pos_ref, own_ref, one_ref, three_ref, two_ref, out_ref, w_in_ref, w_out_ref):
    z = pos_ref[3]
    for d, ref in ((0, own_ref), (1, one_ref), (3, three_ref), (2, two_ref)):
        for l in range(NX):
            for k in range(4):
                at = pl.multiple_of((k * H + ((z + d) % NZ) * NX + l) * HD, HD)
                w_in_ref[:, pl.ds(at, HD)] = (
                    ref[l * 8 : (l + 1) * 8, k * HD : (k + 1) * HD] * factor
                )
    w_out_ref[:, : 4 * HD] = out_ref[:8] * factor
    w_out_ref[:, 4 * HD :] = out_ref[8:] * factor


def columns(ref):
    return jnp.concatenate([ref[h] for h in range(H)], axis=1)


def shard_out_kernel(gated_ref, grad_ref, w_in_ref, w_out_ref, hist_ref, layer_ref, acc_ref):
    term = dot_nt(columns(grad_ref), w_in_ref[...])

    @pl.when(pl.program_id(0) == 0)
    def _():
        hist = hist_ref[...].astype(F32)
        layer_ref[...] = (hist + dot(columns(gated_ref), w_out_ref[...])).astype(BF16)
        acc_ref[...] = term

    @pl.when(pl.program_id(0) > 0)
    def _():
        acc_ref[...] += term


def shard_grad_kernel(grad_ref, w_in_ref, hist_ref, cot_ref, half_ref, grad_hist_ref, acc_ref):
    term = dot_nt(columns(grad_ref), w_in_ref[...])

    @pl.when(pl.program_id(0) == 0)
    def _():
        acc_ref[...] = half_ref[...] + term

    @pl.when(pl.program_id(0) > 0)
    def _():
        normed, inverse = layer_norm(hist_ref[...].astype(F32))
        grad = norm_back(normed, inverse, acc_ref[...] + term)
        grad_hist_ref[...] = (cot_ref[...].astype(F32) + grad).astype(BF16)


def shard_out(back, w_in, w_out, hist):
    rows, width = hist.shape
    whole = lambda a: pl.BlockSpec(a.shape, lambda k: (0,) * a.ndim)
    return pl.pallas_call(
        shard_out_kernel,
        grid=(2,),
        in_specs=[
            pl.BlockSpec((H, rows, HD), lambda k: (0, 0, 4)),
            pl.BlockSpec((H, rows, HD), lambda k: (0, 0, k)),
            pl.BlockSpec((width, width), lambda k: (0, k)),
            whole(w_out),
            whole(hist),
        ],
        out_specs=[whole(hist)] * 2,
        out_shape=[jax.ShapeDtypeStruct(hist.shape, BF16), jax.ShapeDtypeStruct(hist.shape, F32)],
        compiler_params=params(LIMIT),
        cost_estimate=pl.CostEstimate(
            flops=6 * rows * width * width, bytes_accessed=8 << 20, transcendentals=0
        ),
        name="shard_out",
    )(back, back, w_in, w_out, hist)


def shard_grad(back, w_in, hist, cot, half):
    rows, width = hist.shape
    whole = lambda a: pl.BlockSpec(a.shape, lambda k: (0,) * a.ndim)
    return pl.pallas_call(
        shard_grad_kernel,
        grid=(2,),
        in_specs=[
            pl.BlockSpec((H, rows, HD), lambda k: (0, 0, 2 + k)),
            pl.BlockSpec((width, width), lambda k: (0, 2 + k)),
            whole(hist),
            whole(cot),
            whole(half),
        ],
        out_specs=whole(hist),
        out_shape=jax.ShapeDtypeStruct(hist.shape, BF16),
        scratch_shapes=[pltpu.VMEM((rows, width), F32)],
        compiler_params=params(LIMIT),
        cost_estimate=pl.CostEstimate(
            flops=4 * rows * width * width, bytes_accessed=8 << 20, transcendentals=0
        ),
        name="shard_grad",
    )(back, w_in, hist, cot, half)


def local(history, segment_ids, w_in, w_out, cotangent):
    hist = history[0]
    cot = cotangent[0]
    rows, width = hist.shape
    length = rows * NZ * NX
    s = lax.axis_index("seq")
    u = lax.axis_index("user")
    z, x = s // NX, s % NX
    y, xh, core = u // (NXH * NC), (u // NC) % NXH, u % NC

    users = NY * NXH * NC
    tie = lax.optimization_barrier
    w_head = jnp.concatenate(
        [lax.dynamic_slice(w_in, (0, i * width + s * HD), (width, HD)) for i in range(4)], axis=1
    )

    def place_of(key):
        return ((z + key[0]) % NZ) * NX + (x ^ key[1])

    def project(got, outs):
        at = jnp.stack([place_of(key) for key in got])
        return ln_proj(at, list(got.values()), w_head, outs)

    got = {
        (1, 0): from_seq(hist, 1, 0),
        (3, 0): from_seq(hist, 3, 0),
        (0, 1): from_seq(hist, 0, 1),
    }
    outs = project({(0, 0): hist}, ())
    grad_gated_own = dot_nt(cot, w_out).astype(BF16).reshape(rows, H, HD).transpose(1, 0, 2)
    got, outs, grad_gated_own = tie((got, outs, grad_gated_own))
    ids = segment_ids[0].astype(BF16).reshape(2, HD)
    ids = jnp.pad(ids, ((0, 14), (0, 0)))
    to_heads = jnp.concatenate(
        [
            grad_gated_own,
            jnp.broadcast_to(ids[None], (H, 16, HD)),
        ],
        axis=1,
    )
    at_head = lax.all_to_all(to_heads, "seq", 0, 0, tiled=True)
    more = {
        (2, 0): from_seq(got[1, 0], 1, 0),
        (3, 1): from_seq(got[0, 1], 3, 0),
        (1, 1): from_seq(got[1, 0], 0, 1),
    }
    outs = project(got, outs)
    more, outs, cot_next = tie((more, outs, cot))
    last = {(2, 1): from_seq(more[2, 0], 0, 1)}
    cots = {(1, 0): from_seq(cot_next, 1, 0), (3, 0): from_seq(cot_next, 3, 0)}
    outs, at_head = tie((outs, at_head))
    outs = project(more, outs)
    last, cots, outs = tie((last, cots, outs))
    fresh = {(0, 1): from_seq(cot_next, 0, 1), (2, 0): from_seq(cots[1, 0], 1, 0)}
    normed_t, act, slope = project(last, outs)
    att, gate_t, gg_t, stats, start = forward(act, at_head)
    stats, fresh = tie((stats, fresh))
    cots.update(fresh)
    pair = jnp.stack([stats, from_seq(stats, 0, 1)])
    others = [from_seq(pair, dz, 0) for dz in (1, 3, 2)]
    early, grad_out, grad_out_t = mix(pair, *others, att, gate_t, gg_t, slope)
    early, grad_out, grad_out_t, cots = tie((early, grad_out, grad_out_t, cots))
    fresh = {
        (2, 1): from_seq(cots[2, 0], 0, 1),
        (1, 1): from_seq(cots[0, 1], 1, 0),
        (3, 1): from_seq(cots[0, 1], 3, 0),
    }
    back = backward(act, grad_out, grad_out_t, start, early, slope)
    back, fresh = tie((back, fresh))
    cots.update(fresh)
    cots[0, 0] = cot
    back_tok = lax.all_to_all(back, "seq", 0, 0, tiled=True)

    at_core = core.reshape(1)
    keep, send = terms_in(at_core, normed_t, back)
    places = jnp.stack([place_of(key) for key in cots])
    got = from_user(send, 0, 0, 1)
    keep_out, send_out = terms_out(at_core, places, back, list(cots.values()))
    got_out = from_user(send_out, 0, 0, 1)
    at = jnp.stack([y, xh, x, z])
    n = 4 * HD
    own, *sends = small(
        core_sum_kernel,
        "core_sum",
        at,
        [keep, got, keep_out, got_out],
        [((NXH, 80, n), F32)] + [((NXH, 80, n), BF16)] * 3,
        limit=LIMIT,
    )
    own, sends = tie((own, sends))
    sends = [from_user(a, d, 0, 0) for a, d in zip(sends, (1, 3, 2))]
    layer_out, half = shard_out(back_tok, w_in, w_out, hist)
    sends, layer_out, half = tie((sends, layer_out, half))
    keep, same, one, two = small(
        y_sum_kernel,
        "y_sum",
        at,
        [own, *sends],
        [((48, n), F32)] * 2 + [((32, n), F32)] * 2,
        [pltpu.VMEM((NXH, 80, n), F32)],
    )
    same = from_both(same, 1, 0)
    one = from_both(one, 0, 1)
    two = from_both(two, 1, 1)
    grad_history = shard_grad(back_tok, w_in, hist, cot, half)
    same, one, two, grad_history = tie((same, one, two, grad_history))
    own, *sends, own_out = small(
        x_sum_kernel,
        "x_sum",
        at,
        [keep, same, one, two],
        [((16, n), F32)] * 5,
        [pltpu.VMEM((NX, 32, n), F32)],
    )
    sends = [from_seq(a, d, 0) for a, d in zip(sends, (1, 3, 2))]
    factor = (length * users) ** (-0.5)
    grad_w_in, grad_w_out = small(
        functools.partial(z_place_kernel, factor),
        "z_place",
        at,
        [own, *sends, own_out],
        [((8, 4 * width), F32), ((8, width), F32)],
    )
    return layer_out[None], grad_history[None], grad_w_in, grad_w_out


def solution(mesh):
    in_specs = (P("user", "seq", None), P("user", "seq"), P(), P(), P("user", "seq", None))
    out_specs = (
        P("user", "seq", None),
        P("user", "seq", None),
        P(("seq", "user"), None),
        P(("seq", "user"), None),
    )
    return jax.shard_map(local, mesh=mesh, in_specs=in_specs, out_specs=out_specs, check_vma=False)
```

```python
import functools

import jax
import jax.numpy as jnp
from jax import lax
from jax.experimental import pallas as pl
from jax.experimental.pallas import tpu as pltpu
from jax.sharding import PartitionSpec as P

F32 = jnp.float32
BF16 = jnp.bfloat16
EPS = 1e-05
H = 8
HD = 128
NZ, NX = 4, 2
NY, NXH, NC = 4, 2, 2


def seq_perm(dz, dx):
    return [
        (((z + dz) % NZ) * NX + (x ^ dx), z * NX + x) for z in range(NZ) for x in range(NX)
    ]


def user_perm(dy, dh, dc):
    return [
        ((((y + dy) % NY) * NXH + (h ^ dh)) * NC + (c ^ dc), (y * NXH + h) * NC + c)
        for y in range(NY)
        for h in range(NXH)
        for c in range(NC)
    ]


def from_seq(a, dz, dx):
    return lax.ppermute(a, "seq", seq_perm(dz, dx))


def from_user(a, dy, dh, dc):
    return lax.ppermute(a, "user", user_perm(dy, dh, dc))


def from_both(a, dh, dx):
    pairs = []
    for s in range(NZ * NX):
        for u in range(NY * NXH * NC):
            pairs.append(((s ^ dx) * NY * NXH * NC + (u ^ (dh * NC)), s * NY * NXH * NC + u))
    return lax.ppermute(a, ("seq", "user"), pairs)


def layer_norm(entries):
    centre = jnp.mean(entries, axis=-1, keepdims=True)
    centred = entries - centre
    inverse = lax.rsqrt(jnp.mean(centred * centred, axis=-1, keepdims=True) + EPS)
    return centred * inverse, inverse


def norm_back(normed, inverse, upstream):
    first_term = jnp.mean(upstream, axis=-1, keepdims=True)
    second_term = jnp.mean(upstream * normed, axis=-1, keepdims=True)
    return inverse * (upstream - first_term - normed * second_term)


def dot(a, b):
    return jnp.dot(a, b, preferred_element_type=F32)


def dot_nt(a, b):
    return lax.dot_general(a, b, (((1,), (1,)), ((), ())), preferred_element_type=F32)


def dot_tn(a, b):
    return lax.dot_general(a, b, (((0,), (0,)), ((), ())), preferred_element_type=F32)


LIMIT = 56


def params(limit):
    return pltpu.CompilerParams(vmem_limit_bytes=limit << 20)


def ln_proj_kernel(count, at_ref, *refs):
    w_ref = refs[count]
    normed_ref, act_ref, slope_ref = refs[-3:]
    half = act_ref.shape[2]
    for k in range(count):

        @pl.when(pl.program_id(0) == k)
        def _():
            normed, _ = layer_norm(refs[k][...].astype(F32))
            normed_b = normed.astype(BF16)
            normed_ref[...] = normed_b.T
            projected = dot(normed_b, w_ref[...])
            tanh = jnp.tanh(0.5 * projected)
            sig = 0.5 + 0.5 * tanh
            silu = projected * sig
            act = silu.astype(BF16)
            slope = sig + silu * (1.0 - sig)
            for i in range(2):
                act_ref[i, 0] = act[i * half : (i + 1) * half]
                slope_ref[i, 0] = slope[i * half : (i + 1) * half]


def ln_proj(at, blocks, w_head, outs):
    rows, width = blocks[0].shape
    cols = w_head.shape[1]
    half, shards = rows // 2, NZ * NX
    by_half = pl.BlockSpec((2, 1, half, cols), lambda i, at_ref: (0, at_ref[i], 0, 0))
    in_specs = [pl.BlockSpec((rows, width), lambda i, at_ref: (0, 0))] * len(blocks)
    in_specs.append(pl.BlockSpec((width, cols), lambda i, at_ref: (0, 0)))
    aliases = {}
    if outs:
        in_specs += [pl.BlockSpec(memory_space=pl.ANY)] * 3
        aliases = {len(in_specs) + k - 2: k for k in range(3)}
    return pl.pallas_call(
        functools.partial(ln_proj_kernel, len(blocks)),
        grid_spec=pltpu.PrefetchScalarGridSpec(
            num_scalar_prefetch=1,
            grid=(len(blocks),),
            in_specs=in_specs,
            out_specs=(
                pl.BlockSpec((width, rows), lambda i, at_ref: (0, at_ref[i])),
                by_half,
                by_half,
            ),
        ),
        out_shape=(
            jax.ShapeDtypeStruct((width, rows * shards), BF16),
            jax.ShapeDtypeStruct((2, shards, half, cols), BF16),
            jax.ShapeDtypeStruct((2, shards, half, cols), F32),
        ),
        input_output_aliases=aliases,
        compiler_params=params(LIMIT),
        cost_estimate=pl.CostEstimate(
            flops=2 * rows * width * cols * len(blocks),
            bytes_accessed=3 * len(blocks) << 20,
            transcendentals=rows * cols * len(blocks),
        ),
        name="ln_proj",
    )(at, *blocks, w_head, *outs)


FQ, FK = 512, 512
BQ, BK = 512, 256
SCALE = HD ** (-0.5)
UNSEEN = -1024.0


def tile_place(block):
    last = 2 * NZ * NX - 1
    return (block, 0) if block < NZ * NX else (last - block, HD)


def time_rows(ref, first, count, column, columns=1):
    parts = []
    for block in range(first // HD, (first + count) // HD):
        shard, row = tile_place(block)
        parts.append(ref[row // HD, shard, :, column * HD : (column + columns) * HD])
    return parts[0] if len(parts) == 1 else jnp.concatenate(parts, axis=0)


def tiles(length, rows, cols):
    key_row = lax.broadcasted_iota(jnp.int32, (cols, rows), 0)
    query_col = lax.broadcasted_iota(jnp.int32, (1, rows), 1)

    def seen(i, j, start):
        mask = key_row >= start - j
        if j + cols > i:
            mask = mask & (key_row <= query_col + (i - j))
        return mask

    return [(i, range(0, i + rows, cols)) for i in range(0, length, rows)], seen


def forward_kernel(act_ref, head_ref, att_ref, gate_ref, gg_ref, stats_ref, start_ref):
    length = att_ref.shape[1]
    rows = length // (NZ * NX)
    users = [head_ref[shard, rows:, :].astype(F32) for shard in range(NZ * NX)]
    places = [tile_place(block) for block in range(length // HD)]
    ids = jnp.concatenate([users[s][r // HD : r // HD + 1] for s, r in places], axis=1)
    first = jnp.zeros((1, length), F32)
    for v in range(3):
        count = jnp.sum(jnp.where(ids == v, 1.0, 0.0), axis=1, keepdims=True)
        first = first + jnp.where(ids > v, count, 0.0)
    start_ref[...] = first.astype(jnp.int32)
    values_t = [time_rows(act_ref, j, FK, 1).T for j in range(0, length, FK)]
    keys = [time_rows(act_ref, j, FK, 3) for j in range(0, length, FK)]
    queries_in, seen = tiles(length, FQ, FK)
    for i, keys_in in queries_in:
        at = slice(i, i + FQ)
        queries = time_rows(act_ref, i, FQ, 2)
        start = start_ref[:, at]
        total = None
        for j in keys_in:
            half = dot_nt(keys[j // FK], queries) * (0.5 * SCALE)
            half = jnp.where(seen(i, j, start), half, UNSEEN)
            weights = (half + half * jnp.tanh(half)).astype(BF16)
            term = dot(values_t[j // FK], weights)
            total = term if total is None else total + term
        att_ref[:, at] = total
        gate = time_rows(act_ref, i, FQ, 0).T
        parts = []
        for block in range(i // HD, (i + FQ) // HD):
            shard, row = tile_place(block)
            parts.append(head_ref[shard, row : row + HD, :])
        gg = jnp.concatenate(parts, axis=0).T
        gate_ref[:, at] = gate
        gg_ref[:, at] = gg
        grad_mixed = gg.astype(F32) * gate.astype(F32)
        mean = jnp.sum(total, axis=0, keepdims=True) * (1.0 / HD)
        centred = total - mean
        stats_ref[0:1, at] = mean
        stats_ref[1:2, at] = jnp.sum(centred * centred, axis=0, keepdims=True)
        stats_ref[2:3, at] = jnp.sum(grad_mixed, axis=0, keepdims=True)
        stats_ref[3:4, at] = jnp.sum(grad_mixed * centred, axis=0, keepdims=True)


def vmem():
    return pl.BlockSpec(memory_space=pltpu.VMEM)


def smem():
    return pl.BlockSpec(memory_space=pltpu.SMEM)


def forward(act, at_head):
    length = HD * 2 * NZ * NX
    return pl.pallas_call(
        forward_kernel,
        in_specs=[vmem()] * 2,
        out_specs=[vmem()] * 5,
        out_shape=(
            jax.ShapeDtypeStruct((HD, length), F32),
            jax.ShapeDtypeStruct((HD, length), BF16),
            jax.ShapeDtypeStruct((HD, length), BF16),
            jax.ShapeDtypeStruct((4, length), F32),
            jax.ShapeDtypeStruct((1, length), jnp.int32),
        ),
        compiler_params=params(LIMIT),
        cost_estimate=pl.CostEstimate(
            flops=8 * HD * length * length, bytes_accessed=6 << 20, transcendentals=length * length // 2
        ),
        name="attention_forward",
    )(act, at_head)


def backward_kernel(own_ref, one_ref, three_ref, two_ref, act_ref, att_ref, gate_ref, gg_ref, start_ref, slope_hbm, back_ref, dk_ref, dv_ref, slope_ref, sem):
    length = att_ref.shape[1]
    width = H * HD
    copy = pltpu.make_async_copy(slope_hbm, slope_ref, sem)
    copy.start()
    heads = [ref[k] for ref in (own_ref, one_ref, three_ref, two_ref) for k in range(NX)]
    mean_all = sum(a[0:1] for a in heads) * (1.0 / H)
    apart = [a[0:1] - mean_all for a in heads]
    spread = sum(a[1:2] for a in heads) + HD * sum(d * d for d in apart)
    inverse_all = lax.rsqrt(spread * (1.0 / width) + EPS)
    first_all = sum(a[2:3] for a in heads) * (1.0 / width)
    second_all = inverse_all * sum(a[3:4] + d * a[2:3] for a, d in zip(heads, apart)) * (1.0 / width)

    keys = [time_rows(act_ref, j, BK, 3) for j in range(0, length, BK)]
    keys_t = [k.T for k in keys]
    values = [time_rows(act_ref, j, BK, 1) for j in range(0, length, BK)]
    queries_in, seen = tiles(length, BQ, BK)

    def put(first, column, value):
        value = value.astype(BF16)
        for k in range(value.shape[0] // HD):
            shard, row = tile_place(first // HD + k)
            back_ref[shard, row : row + HD, column * HD : (column + 1) * HD] = value[
                k * HD : (k + 1) * HD
            ]

    def put_grad(first, column, value):
        put(first, column, value * time_rows(slope_ref, first, value.shape[0], column))

    started = set()
    for i, keys_in in queries_in:
        at = slice(i, i + BQ)
        gate = gate_ref[:, at].astype(F32)
        gg = gg_ref[:, at].astype(F32)
        inverse = inverse_all[:, at]
        mixed = (att_ref[:, at] - mean_all[:, at]) * inverse
        grad_att = inverse * (gg * gate - first_all[:, at] - mixed * second_all[:, at])
        grad_out_t = grad_att.astype(BF16)
        grad_out = grad_out_t.T
        queries = time_rows(act_ref, i, BQ, 2)
        start = start_ref[:, at]
        total = None
        for j in keys_in:
            here = slice(j, j + BK)
            half = dot_nt(keys[j // BK], queries) * (0.5 * SCALE)
            half = jnp.where(seen(i, j, start), half, UNSEEN)
            tanh = jnp.tanh(half)
            weights = half + half * tanh
            sig = 0.5 + 0.5 * tanh
            slope = sig + weights * (1.0 - sig)
            ahead = dot(values[j // BK], grad_out_t)
            weights = weights.astype(BF16)
            slopes = (ahead * slope).astype(BF16)
            dv = dot(weights, grad_out)
            dk = dot(slopes, queries)
            if j in started:
                dv_ref[here, :] += dv
                dk_ref[here, :] += dk
            else:
                dv_ref[here, :] = dv
                dk_ref[here, :] = dk
                started.add(j)
            term = dot(keys_t[j // BK], slopes)
            total = term if total is None else total + term
        if i == 0:
            copy.wait()
        put(i, 4, (mixed * gate).astype(BF16).T)
        put_grad(i, 0, (gg * mixed).T)
        put_grad(i, 2, total.T * SCALE)
    for j in range(0, length, BK):
        put_grad(j, 1, dv_ref[j : j + BK, :])
        put_grad(j, 3, dk_ref[j : j + BK, :] * SCALE)


def backward(stats, act, att, gate, gg, start, slope):
    length = start.shape[1]
    shards = NZ * NX
    return pl.pallas_call(
        backward_kernel,
        in_specs=[vmem()] * 9 + [pl.BlockSpec(memory_space=pl.ANY)],
        out_specs=vmem(),
        out_shape=jax.ShapeDtypeStruct((shards, length // shards, 5 * HD), BF16),
        scratch_shapes=[pltpu.VMEM((length, HD), F32)] * 2
        + [pltpu.VMEM(slope.shape, F32), pltpu.SemaphoreType.DMA],
        compiler_params=params(LIMIT),
        cost_estimate=pl.CostEstimate(
            flops=15 * HD * length * length, bytes_accessed=10 << 20, transcendentals=length * length // 2
        ),
        name="attention_backward",
    )(*stats, act, att, gate, gg, start, slope)


def terms_in_kernel(core_ref, normed_ref, grad_ref, keep_ref, send_ref, res_ref):
    shards, rows, cols = grad_ref.shape
    res_ref[...] = dot(normed_ref[...], grad_ref[...].reshape(shards * rows, cols))
    core = core_ref[0]
    for k in range(res_ref.shape[0] // HD):
        for pair in range(NY * NXH):
            mine = pl.multiple_of(k * HD + (pair * NC + core) * 8, 8)
            other = pl.multiple_of(k * HD + (pair * NC + 1 - core) * 8, 8)
            keep_ref[pair, k * 8 : (k + 1) * 8, :] = res_ref[pl.ds(mine, 8), :]
            send_ref[pair, k * 8 : (k + 1) * 8, :] = res_ref[pl.ds(other, 8), :]


def terms_in(core, normed_t, back):
    width, length = normed_t.shape
    shards, rows, _ = back.shape
    shape = jax.ShapeDtypeStruct((NY * NXH, 64, 4 * HD), F32)
    out_spec = pl.BlockSpec((NY * NXH, 16, 4 * HD), lambda g: (0, g, 0))
    return pl.pallas_call(
        terms_in_kernel,
        grid=(4,),
        in_specs=[
            smem(),
            pl.BlockSpec((width // 4, length), lambda g: (g, 0)),
            pl.BlockSpec((shards, rows, 4 * HD), lambda g: (0, 0, 0)),
        ],
        out_specs=[out_spec] * 2,
        out_shape=[shape] * 2,
        scratch_shapes=[pltpu.VMEM((width // 4, 4 * HD), F32)],
        compiler_params=params(LIMIT),
        cost_estimate=pl.CostEstimate(
            flops=2 * width * length * 4 * HD, bytes_accessed=9 << 20, transcendentals=0
        ),
        name="terms_in",
    )(core, normed_t, back)


def terms_out_kernel(core_ref, at_ref, gated_ref, *refs):
    keep_ref, send_ref, res_ref, gated_t_ref = refs[-4:]
    shards, rows, _ = gated_ref.shape

    @pl.when(pl.program_id(0) == 0)
    def _():
        for shard in range(shards):
            gated_t_ref[:, shard * rows : (shard + 1) * rows] = gated_ref[shard].T

    total = None
    for r in range(shards):
        here = pl.ds(pl.multiple_of(at_ref[r] * rows, rows), rows)
        term = dot(gated_t_ref[:, here], refs[r][...])
        total = term if total is None else total + term
    res_ref[...] = total
    core = core_ref[0]
    for pair in range(NY * NXH):
        for out_ref, who in ((keep_ref, core), (send_ref, 1 - core)):
            out_ref[pair] = res_ref[pl.ds(pl.multiple_of((pair * NC + who) * 8, 8), 8), :]


def terms_out(core, at, back, cots):
    shards, rows, _ = back.shape
    width = cots[0].shape[1]
    length = shards * rows
    out_spec = pl.BlockSpec((NY * NXH, 8, 4 * HD), lambda g: (0, g, 0))
    return pl.pallas_call(
        terms_out_kernel,
        grid=(2,),
        in_specs=[smem(), smem(), pl.BlockSpec((shards, rows, HD), lambda g: (0, 0, 4))]
        + [pl.BlockSpec((rows, width // 2), lambda g: (0, g))] * shards,
        out_specs=[out_spec] * 2,
        out_shape=[jax.ShapeDtypeStruct((NY * NXH, 16, 4 * HD), F32)] * 2,
        scratch_shapes=[pltpu.VMEM((HD, width // 2), F32), pltpu.VMEM((HD, length), BF16)],
        compiler_params=params(LIMIT),
        cost_estimate=pl.CostEstimate(
            flops=2 * HD * width * length, bytes_accessed=6 << 20, transcendentals=0
        ),
        name="terms_out",
    )(core, at, back, *cots)


def small(kernel, name, scalars, arrays, outs, scratch=(), limit=12):
    size = sum(a.size * a.dtype.itemsize for a in arrays)
    return pl.pallas_call(
        kernel,
        in_specs=[smem()] + [vmem()] * len(arrays),
        out_specs=[vmem()] * len(outs),
        out_shape=[jax.ShapeDtypeStruct(shape, dtype) for shape, dtype in outs],
        scratch_shapes=list(scratch),
        compiler_params=params(limit),
        cost_estimate=pl.CostEstimate(flops=size, bytes_accessed=2 * size, transcendentals=0),
        name=name,
    )(scalars, *arrays)


def core_sum_kernel(pos_ref, keep_ref, got_ref, keep_out_ref, got_out_ref, own_ref, one_ref, three_ref, two_ref):
    y = pos_ref[0]
    for d, to_ref in ((0, own_ref), (1, one_ref), (3, three_ref), (2, two_ref)):
        here = pl.ds(((y - d + NY) % NY) * NXH, NXH)
        to_ref[:, :64, :] = (keep_ref[here] + got_ref[here]).astype(to_ref.dtype)
        to_ref[:, 64:, :] = (keep_out_ref[here] + got_out_ref[here]).astype(to_ref.dtype)


def y_sum_kernel(pos_ref, own_ref, a_ref, b_ref, c_ref, keep_ref, same_ref, one_ref, two_ref, sum_ref):
    xh, x = pos_ref[1], pos_ref[2]
    sum_ref[...] = own_ref[...] + (
        a_ref[...].astype(F32) + b_ref[...].astype(F32) + c_ref[...].astype(F32)
    )

    def slab(out_ref, h, l):
        for k in range(NZ):
            out_ref[k * 8 : (k + 1) * 8, :] = sum_ref[
                h, pl.ds(pl.multiple_of((k * NX + l) * 8, 8), 8), :
            ]

    slab(keep_ref, xh, x)
    keep_ref[32:, :] = sum_ref[xh, 64:, :]
    slab(same_ref, 1 - xh, x)
    same_ref[32:, :] = sum_ref[1 - xh, 64:, :]
    slab(one_ref, xh, 1 - x)
    slab(two_ref, 1 - xh, 1 - x)


def x_sum_kernel(pos_ref, keep_ref, same_ref, a_ref, b_ref, own_ref, one_ref, three_ref, two_ref, out_ref, sum_ref):
    z, x = pos_ref[3], pos_ref[2]
    mine = keep_ref[...] + same_ref[...]
    sum_ref[x] = mine[:32]
    sum_ref[1 - x] = a_ref[...] + b_ref[...]
    out_ref[...] = mine[32:]
    for d, to_ref in ((0, own_ref), (1, one_ref), (3, three_ref), (2, two_ref)):
        here = pl.ds(pl.multiple_of(((z - d + NZ) % NZ) * 8, 8), 8)
        for l in range(NX):
            to_ref[l * 8 : (l + 1) * 8, :] = sum_ref[l, here, :]


def z_place_kernel(factor, pos_ref, own_ref, one_ref, three_ref, two_ref, out_ref, w_in_ref, w_out_ref):
    z = pos_ref[3]
    for d, ref in ((0, own_ref), (1, one_ref), (3, three_ref), (2, two_ref)):
        for l in range(NX):
            for k in range(4):
                at = pl.multiple_of((k * H + ((z + d) % NZ) * NX + l) * HD, HD)
                w_in_ref[:, pl.ds(at, HD)] = (
                    ref[l * 8 : (l + 1) * 8, k * HD : (k + 1) * HD] * factor
                )
    w_out_ref[:, : 4 * HD] = out_ref[:8] * factor
    w_out_ref[:, 4 * HD :] = out_ref[8:] * factor


def columns(ref):
    return jnp.concatenate([ref[h] for h in range(H)], axis=1)


def shard_out_kernel(gated_ref, grad_ref, w_in_ref, w_out_ref, hist_ref, layer_ref, acc_ref):
    term = dot_nt(columns(grad_ref), w_in_ref[...])

    @pl.when(pl.program_id(0) == 0)
    def _():
        hist = hist_ref[...].astype(F32)
        layer_ref[...] = (hist + dot(columns(gated_ref), w_out_ref[...])).astype(BF16)
        acc_ref[...] = term

    @pl.when(pl.program_id(0) > 0)
    def _():
        acc_ref[...] += term


def shard_grad_kernel(grad_ref, w_in_ref, hist_ref, cot_ref, half_ref, grad_hist_ref, acc_ref):
    term = dot_nt(columns(grad_ref), w_in_ref[...])

    @pl.when(pl.program_id(0) == 0)
    def _():
        acc_ref[...] = half_ref[...] + term

    @pl.when(pl.program_id(0) > 0)
    def _():
        normed, inverse = layer_norm(hist_ref[...].astype(F32))
        grad = norm_back(normed, inverse, acc_ref[...] + term)
        grad_hist_ref[...] = (cot_ref[...].astype(F32) + grad).astype(BF16)


def shard_out(back, w_in, w_out, hist):
    rows, width = hist.shape
    whole = lambda a: pl.BlockSpec(a.shape, lambda k: (0,) * a.ndim)
    return pl.pallas_call(
        shard_out_kernel,
        grid=(2,),
        in_specs=[
            pl.BlockSpec((H, rows, HD), lambda k: (0, 0, 4)),
            pl.BlockSpec((H, rows, HD), lambda k: (0, 0, k)),
            pl.BlockSpec((width, width), lambda k: (0, k)),
            whole(w_out),
            whole(hist),
        ],
        out_specs=[whole(hist)] * 2,
        out_shape=[jax.ShapeDtypeStruct(hist.shape, BF16), jax.ShapeDtypeStruct(hist.shape, F32)],
        compiler_params=params(LIMIT),
        cost_estimate=pl.CostEstimate(
            flops=6 * rows * width * width, bytes_accessed=8 << 20, transcendentals=0
        ),
        name="shard_out",
    )(back, back, w_in, w_out, hist)


def shard_grad(back, w_in, hist, cot, half):
    rows, width = hist.shape
    whole = lambda a: pl.BlockSpec(a.shape, lambda k: (0,) * a.ndim)
    return pl.pallas_call(
        shard_grad_kernel,
        grid=(2,),
        in_specs=[
            pl.BlockSpec((H, rows, HD), lambda k: (0, 0, 2 + k)),
            pl.BlockSpec((width, width), lambda k: (0, 2 + k)),
            whole(hist),
            whole(cot),
            whole(half),
        ],
        out_specs=whole(hist),
        out_shape=jax.ShapeDtypeStruct(hist.shape, BF16),
        scratch_shapes=[pltpu.VMEM((rows, width), F32)],
        compiler_params=params(LIMIT),
        cost_estimate=pl.CostEstimate(
            flops=4 * rows * width * width, bytes_accessed=8 << 20, transcendentals=0
        ),
        name="shard_grad",
    )(back, w_in, hist, cot, half)


def local(history, segment_ids, w_in, w_out, cotangent):
    hist = history[0]
    cot = cotangent[0]
    rows, width = hist.shape
    length = rows * NZ * NX
    s = lax.axis_index("seq")
    u = lax.axis_index("user")
    z, x = s // NX, s % NX
    y, xh, core = u // (NXH * NC), (u // NC) % NXH, u % NC

    users = NY * NXH * NC
    tie = lax.optimization_barrier
    w_head = jnp.concatenate(
        [lax.dynamic_slice(w_in, (0, i * width + s * HD), (width, HD)) for i in range(4)], axis=1
    )

    def place_of(key):
        return ((z + key[0]) % NZ) * NX + (x ^ key[1])

    at_core = core.reshape(1)
    at = jnp.stack([y, xh, x, z])
    orders = (
        ((0, 0),),
        ((0, 1), (1, 0), (3, 0)),
        ((1, 1), (2, 0), (3, 1)),
        ((2, 1),),
        ((1, 0), (3, 0), (0, 1), (2, 0), (2, 1), (1, 1), (3, 1), (0, 0)),
    )
    places = {keys: jnp.stack([place_of(key) for key in keys]) for keys in orders}

    def project(got, outs):
        keys = tuple(sorted(got))
        return ln_proj(places[keys], [got[key] for key in keys], w_head, outs)

    got = {
        (1, 0): from_seq(hist, 1, 0),
        (3, 0): from_seq(hist, 3, 0),
        (0, 1): from_seq(hist, 0, 1),
    }
    outs = project({(0, 0): hist}, ())
    grad_gated_own = dot_nt(cot, w_out).astype(BF16).reshape(rows, H, HD).transpose(1, 0, 2)
    got, outs, grad_gated_own, waiting, at_core, at = tie(
        (got, outs, grad_gated_own, tuple(places.values()), at_core, at)
    )
    places = dict(zip(orders, waiting))
    ids = segment_ids[0].astype(BF16).reshape(2, HD)
    ids = jnp.pad(ids, ((0, 14), (0, 0)))
    to_heads = jnp.concatenate(
        [
            grad_gated_own,
            jnp.broadcast_to(ids[None], (H, 16, HD)),
        ],
        axis=1,
    )
    at_head = lax.all_to_all(to_heads, "seq", 0, 0, tiled=True)
    more = {
        (2, 0): from_seq(got[1, 0], 1, 0),
        (3, 1): from_seq(got[0, 1], 3, 0),
        (1, 1): from_seq(got[1, 0], 0, 1),
    }
    outs = project(got, outs)
    more, outs, cot_next = tie((more, outs, cot))
    last = {(2, 1): from_seq(more[2, 0], 0, 1)}
    cots = {(1, 0): from_seq(cot_next, 1, 0), (3, 0): from_seq(cot_next, 3, 0)}
    outs, at_head = tie((outs, at_head))
    outs = project(more, outs)
    last, cots, outs = tie((last, cots, outs))
    fresh = {(0, 1): from_seq(cot_next, 0, 1), (2, 0): from_seq(cots[1, 0], 1, 0)}
    normed_t, act, slope = project(last, outs)
    att, gate_t, gg_t, stats, start = forward(act, at_head)
    stats, fresh = tie((stats, fresh))
    cots.update(fresh)
    pair = jnp.stack([stats, from_seq(stats, 0, 1)])
    others = [from_seq(pair, dz, 0) for dz in (1, 3, 2)]
    pair, others, cots = tie((pair, others, cots))
    fresh = {
        (2, 1): from_seq(cots[2, 0], 0, 1),
        (1, 1): from_seq(cots[0, 1], 1, 0),
        (3, 1): from_seq(cots[0, 1], 3, 0),
    }
    back = backward([pair, *others], act, att, gate_t, gg_t, start, slope)
    back, fresh = tie((back, fresh))
    cots.update(fresh)
    cots[0, 0] = cot
    back_tok = lax.all_to_all(back, "seq", 0, 0, tiled=True)

    keep, send = terms_in(at_core, normed_t, back)
    got = from_user(send, 0, 0, 1)
    keep_out, send_out = terms_out(at_core, places[orders[4]], back, [cots[key] for key in orders[4]])
    got_out = from_user(send_out, 0, 0, 1)
    n = 4 * HD
    own, *sends = small(
        core_sum_kernel,
        "core_sum",
        at,
        [keep, got, keep_out, got_out],
        [((NXH, 80, n), F32)] + [((NXH, 80, n), BF16)] * 3,
        limit=LIMIT,
    )
    own, sends = tie((own, sends))
    sends = [from_user(a, d, 0, 0) for a, d in zip(sends, (1, 3, 2))]
    layer_out, half = shard_out(back_tok, w_in, w_out, hist)
    sends, layer_out, half = tie((sends, layer_out, half))
    keep, same, one, two = small(
        y_sum_kernel,
        "y_sum",
        at,
        [own, *sends],
        [((48, n), F32)] * 2 + [((32, n), F32)] * 2,
        [pltpu.VMEM((NXH, 80, n), F32)],
    )
    same = from_both(same, 1, 0)
    one = from_both(one, 0, 1)
    two = from_both(two, 1, 1)
    grad_history = shard_grad(back_tok, w_in, hist, cot, half)
    same, one, two, grad_history = tie((same, one, two, grad_history))
    own, *sends, own_out = small(
        x_sum_kernel,
        "x_sum",
        at,
        [keep, same, one, two],
        [((16, n), F32)] * 5,
        [pltpu.VMEM((NX, 32, n), F32)],
    )
    sends = [from_seq(a, d, 0) for a, d in zip(sends, (1, 3, 2))]
    factor = (length * users) ** (-0.5)
    grad_w_in, grad_w_out = small(
        functools.partial(z_place_kernel, factor),
        "z_place",
        at,
        [own, *sends, own_out],
        [((8, 4 * width), F32), ((8, width), F32)],
    )
    return layer_out[None], grad_history[None], grad_w_in, grad_w_out


def solution(mesh):
    in_specs = (P("user", "seq", None), P("user", "seq"), P(), P(), P("user", "seq", None))
    out_specs = (
        P("user", "seq", None),
        P("user", "seq", None),
        P(("seq", "user"), None),
        P(("seq", "user"), None),
    )
    return jax.shard_map(local, mesh=mesh, in_specs=in_specs, out_specs=out_specs, check_vma=False)
```

```python
import functools

import jax
import jax.numpy as jnp
from jax import lax
from jax.experimental import pallas as pl
from jax.experimental.pallas import tpu as pltpu
from jax.sharding import PartitionSpec as P

F32 = jnp.float32
BF16 = jnp.bfloat16
EPS = 1e-05
H = 8
HD = 128
NZ, NX = 4, 2
NY, NXH, NC = 4, 2, 2


def seq_perm(dz, dx):
    return [
        (((z + dz) % NZ) * NX + (x ^ dx), z * NX + x) for z in range(NZ) for x in range(NX)
    ]


def user_perm(dy, dh, dc):
    return [
        ((((y + dy) % NY) * NXH + (h ^ dh)) * NC + (c ^ dc), (y * NXH + h) * NC + c)
        for y in range(NY)
        for h in range(NXH)
        for c in range(NC)
    ]


def from_seq(a, dz, dx):
    return lax.ppermute(a, "seq", seq_perm(dz, dx))


def from_user(a, dy, dh, dc):
    return lax.ppermute(a, "user", user_perm(dy, dh, dc))


def from_both(a, dh, dx):
    pairs = []
    for s in range(NZ * NX):
        for u in range(NY * NXH * NC):
            pairs.append(((s ^ dx) * NY * NXH * NC + (u ^ (dh * NC)), s * NY * NXH * NC + u))
    return lax.ppermute(a, ("seq", "user"), pairs)


def layer_norm(entries):
    centre = jnp.mean(entries, axis=-1, keepdims=True)
    centred = entries - centre
    inverse = lax.rsqrt(jnp.mean(centred * centred, axis=-1, keepdims=True) + EPS)
    return centred * inverse, inverse


def norm_back(normed, inverse, upstream):
    first_term = jnp.mean(upstream, axis=-1, keepdims=True)
    second_term = jnp.mean(upstream * normed, axis=-1, keepdims=True)
    return inverse * (upstream - first_term - normed * second_term)


def dot(a, b):
    return jnp.dot(a, b, preferred_element_type=F32)


def dot_nt(a, b):
    return lax.dot_general(a, b, (((1,), (1,)), ((), ())), preferred_element_type=F32)


def dot_tn(a, b):
    return lax.dot_general(a, b, (((0,), (0,)), ((), ())), preferred_element_type=F32)


LIMIT = 56


def params(limit):
    return pltpu.CompilerParams(vmem_limit_bytes=limit << 20)


def ln_proj_kernel(count, at_ref, *refs):
    w_ref = refs[count]
    normed_ref, act_ref, slope_ref = refs[-3:]
    half = act_ref.shape[2]
    for k in range(count):

        @pl.when(pl.program_id(0) == k)
        def _():
            normed, _ = layer_norm(refs[k][...].astype(F32))
            normed_b = normed.astype(BF16)
            normed_ref[...] = normed_b.T
            projected = dot(normed_b, w_ref[...])
            tanh = jnp.tanh(0.5 * projected)
            sig = 0.5 + 0.5 * tanh
            silu = projected * sig
            act = silu.astype(BF16)
            slope = sig + silu * (1.0 - sig)
            for i in range(2):
                act_ref[i, 0] = act[i * half : (i + 1) * half]
                slope_ref[i, 0] = slope[i * half : (i + 1) * half]


def ln_proj(at, blocks, w_head, outs):
    rows, width = blocks[0].shape
    cols = w_head.shape[1]
    half, shards = rows // 2, NZ * NX
    by_half = pl.BlockSpec((2, 1, half, cols), lambda i, at_ref: (0, at_ref[i], 0, 0))
    in_specs = [pl.BlockSpec((rows, width), lambda i, at_ref: (0, 0))] * len(blocks)
    in_specs.append(pl.BlockSpec((width, cols), lambda i, at_ref: (0, 0)))
    aliases = {}
    if outs:
        in_specs += [pl.BlockSpec(memory_space=pl.ANY)] * 3
        aliases = {len(in_specs) + k - 2: k for k in range(3)}
    return pl.pallas_call(
        functools.partial(ln_proj_kernel, len(blocks)),
        grid_spec=pltpu.PrefetchScalarGridSpec(
            num_scalar_prefetch=1,
            grid=(len(blocks),),
            in_specs=in_specs,
            out_specs=(
                pl.BlockSpec((width, rows), lambda i, at_ref: (0, at_ref[i])),
                by_half,
                by_half,
            ),
        ),
        out_shape=(
            jax.ShapeDtypeStruct((width, rows * shards), BF16),
            jax.ShapeDtypeStruct((2, shards, half, cols), BF16),
            jax.ShapeDtypeStruct((2, shards, half, cols), F32),
        ),
        input_output_aliases=aliases,
        compiler_params=params(LIMIT),
        cost_estimate=pl.CostEstimate(
            flops=2 * rows * width * cols * len(blocks),
            bytes_accessed=3 * len(blocks) << 20,
            transcendentals=rows * cols * len(blocks),
        ),
        name="ln_proj",
    )(at, *blocks, w_head, *outs)


FQ, FK = 512, 512
BQ, BK = 512, 256
SCALE = HD ** (-0.5)
UNSEEN = -1024.0


def tile_place(block):
    last = 2 * NZ * NX - 1
    return (block, 0) if block < NZ * NX else (last - block, HD)


def time_rows(ref, first, count, column, columns=1):
    parts = []
    for block in range(first // HD, (first + count) // HD):
        shard, row = tile_place(block)
        parts.append(ref[row // HD, shard, :, column * HD : (column + columns) * HD])
    return parts[0] if len(parts) == 1 else jnp.concatenate(parts, axis=0)


def tiles(length, rows, cols):
    key_row = lax.broadcasted_iota(jnp.int32, (cols, rows), 0)
    query_col = lax.broadcasted_iota(jnp.int32, (1, rows), 1)

    def seen(i, j, start):
        mask = key_row >= start - j
        if j + cols > i:
            mask = mask & (key_row <= query_col + (i - j))
        return mask

    return [(i, range(0, i + rows, cols)) for i in range(0, length, rows)], seen


def forward_kernel(act_ref, head_ref, att_ref, gate_ref, gg_ref, stats_ref, start_ref):
    length = att_ref.shape[1]
    rows = length // (NZ * NX)
    users = [head_ref[shard, rows:, :].astype(F32) for shard in range(NZ * NX)]
    places = [tile_place(block) for block in range(length // HD)]
    ids = jnp.concatenate([users[s][r // HD : r // HD + 1] for s, r in places], axis=1)
    first = jnp.zeros((1, length), F32)
    for v in range(3):
        count = jnp.sum(jnp.where(ids == v, 1.0, 0.0), axis=1, keepdims=True)
        first = first + jnp.where(ids > v, count, 0.0)
    start_ref[...] = first.astype(jnp.int32)
    values_t = [time_rows(act_ref, j, FK, 1).T for j in range(0, length, FK)]
    keys = [time_rows(act_ref, j, FK, 3) for j in range(0, length, FK)]
    queries_in, seen = tiles(length, FQ, FK)
    for i, keys_in in queries_in:
        at = slice(i, i + FQ)
        queries = time_rows(act_ref, i, FQ, 2)
        start = start_ref[:, at]
        total = None
        for j in keys_in:
            half = dot_nt(keys[j // FK], queries) * (0.5 * SCALE)
            half = jnp.where(seen(i, j, start), half, UNSEEN)
            weights = (half + half * jnp.tanh(half)).astype(BF16)
            term = dot(values_t[j // FK], weights)
            total = term if total is None else total + term
        att_ref[:, at] = total
        gate = time_rows(act_ref, i, FQ, 0).T
        parts = []
        for block in range(i // HD, (i + FQ) // HD):
            shard, row = tile_place(block)
            parts.append(head_ref[shard, row : row + HD, :])
        gg = jnp.concatenate(parts, axis=0).T
        gate_ref[:, at] = gate
        gg_ref[:, at] = gg
        grad_mixed = gg.astype(F32) * gate.astype(F32)
        mean = jnp.sum(total, axis=0, keepdims=True) * (1.0 / HD)
        centred = total - mean
        stats_ref[0:1, at] = mean
        stats_ref[1:2, at] = jnp.sum(centred * centred, axis=0, keepdims=True)
        stats_ref[2:3, at] = jnp.sum(grad_mixed, axis=0, keepdims=True)
        stats_ref[3:4, at] = jnp.sum(grad_mixed * centred, axis=0, keepdims=True)


def vmem():
    return pl.BlockSpec(memory_space=pltpu.VMEM)


def smem():
    return pl.BlockSpec(memory_space=pltpu.SMEM)


def forward(act, at_head):
    length = HD * 2 * NZ * NX
    return pl.pallas_call(
        forward_kernel,
        in_specs=[vmem()] * 2,
        out_specs=[vmem()] * 5,
        out_shape=(
            jax.ShapeDtypeStruct((HD, length), F32),
            jax.ShapeDtypeStruct((HD, length), BF16),
            jax.ShapeDtypeStruct((HD, length), BF16),
            jax.ShapeDtypeStruct((4, length), F32),
            jax.ShapeDtypeStruct((1, length), jnp.int32),
        ),
        compiler_params=params(LIMIT),
        cost_estimate=pl.CostEstimate(
            flops=8 * HD * length * length, bytes_accessed=6 << 20, transcendentals=length * length // 2
        ),
        name="attention_forward",
    )(act, at_head)


def backward_kernel(own_ref, one_ref, three_ref, two_ref, act_ref, att_ref, gate_ref, gg_ref, start_ref, slope_hbm, back_ref, dk_ref, dv_ref, slope_ref, sem):
    length = att_ref.shape[1]
    width = H * HD
    copy = pltpu.make_async_copy(slope_hbm, slope_ref, sem)
    copy.start()
    heads = [ref[k] for ref in (own_ref, one_ref, three_ref, two_ref) for k in range(NX)]
    mean_all = sum(a[0:1] for a in heads) * (1.0 / H)
    apart = [a[0:1] - mean_all for a in heads]
    spread = sum(a[1:2] for a in heads) + HD * sum(d * d for d in apart)
    inverse_all = lax.rsqrt(spread * (1.0 / width) + EPS)
    first_all = sum(a[2:3] for a in heads) * (1.0 / width)
    second_all = inverse_all * sum(a[3:4] + d * a[2:3] for a, d in zip(heads, apart)) * (1.0 / width)

    keys = [time_rows(act_ref, j, BK, 3) for j in range(0, length, BK)]
    keys_t = [k.T for k in keys]
    values = [time_rows(act_ref, j, BK, 1) for j in range(0, length, BK)]
    queries_in, seen = tiles(length, BQ, BK)

    def put(first, column, value):
        value = value.astype(BF16)
        for k in range(value.shape[0] // HD):
            shard, row = tile_place(first // HD + k)
            back_ref[shard, row : row + HD, column * HD : (column + 1) * HD] = value[
                k * HD : (k + 1) * HD
            ]

    def put_grad(first, column, value):
        put(first, column, value * time_rows(slope_ref, first, value.shape[0], column))

    started = set()
    for i, keys_in in queries_in:
        at = slice(i, i + BQ)
        gate = gate_ref[:, at].astype(F32)
        gg = gg_ref[:, at].astype(F32)
        inverse = inverse_all[:, at]
        mixed = (att_ref[:, at] - mean_all[:, at]) * inverse
        grad_att = inverse * (gg * gate - first_all[:, at] - mixed * second_all[:, at])
        grad_out_t = grad_att.astype(BF16)
        grad_out = grad_out_t.T
        queries = time_rows(act_ref, i, BQ, 2)
        start = start_ref[:, at]
        total = None
        for j in keys_in:
            here = slice(j, j + BK)
            half = dot_nt(keys[j // BK], queries) * (0.5 * SCALE)
            half = jnp.where(seen(i, j, start), half, UNSEEN)
            tanh = jnp.tanh(half)
            weights = half + half * tanh
            sig = 0.5 + 0.5 * tanh
            slope = sig + weights * (1.0 - sig)
            ahead = dot(values[j // BK], grad_out_t)
            weights = weights.astype(BF16)
            slopes = (ahead * slope).astype(BF16)
            dv = dot(weights, grad_out)
            dk = dot(slopes, queries)
            if j in started:
                dv_ref[here, :] += dv
                dk_ref[here, :] += dk
            else:
                dv_ref[here, :] = dv
                dk_ref[here, :] = dk
                started.add(j)
            term = dot(keys_t[j // BK], slopes)
            total = term if total is None else total + term
        if i == 0:
            copy.wait()
        put(i, 4, (mixed * gate).astype(BF16).T)
        put_grad(i, 0, (gg * mixed).T)
        put_grad(i, 2, total.T * SCALE)
    for j in range(0, length, BK):
        put_grad(j, 1, dv_ref[j : j + BK, :])
        put_grad(j, 3, dk_ref[j : j + BK, :] * SCALE)


def backward(stats, act, att, gate, gg, start, slope):
    length = start.shape[1]
    shards = NZ * NX
    return pl.pallas_call(
        backward_kernel,
        in_specs=[vmem()] * 9 + [pl.BlockSpec(memory_space=pl.ANY)],
        out_specs=vmem(),
        out_shape=jax.ShapeDtypeStruct((shards, length // shards, 5 * HD), BF16),
        scratch_shapes=[pltpu.VMEM((length, HD), F32)] * 2
        + [pltpu.VMEM(slope.shape, F32), pltpu.SemaphoreType.DMA],
        compiler_params=params(LIMIT),
        cost_estimate=pl.CostEstimate(
            flops=15 * HD * length * length, bytes_accessed=10 << 20, transcendentals=length * length // 2
        ),
        name="attention_backward",
    )(*stats, act, att, gate, gg, start, slope)


def terms_in_kernel(core_ref, normed_ref, grad_ref, keep_ref, send_ref, res_ref):
    shards, rows, cols = grad_ref.shape
    res_ref[...] = dot(normed_ref[...], grad_ref[...].reshape(shards * rows, cols))
    core = core_ref[0]
    for k in range(res_ref.shape[0] // HD):
        for pair in range(NY * NXH):
            mine = pl.multiple_of(k * HD + (pair * NC + core) * 8, 8)
            other = pl.multiple_of(k * HD + (pair * NC + 1 - core) * 8, 8)
            keep_ref[pair, k * 8 : (k + 1) * 8, :] = res_ref[pl.ds(mine, 8), :]
            send_ref[pair, k * 8 : (k + 1) * 8, :] = res_ref[pl.ds(other, 8), :]


def terms_in(core, normed_t, back):
    width, length = normed_t.shape
    shards, rows, _ = back.shape
    shape = jax.ShapeDtypeStruct((NY * NXH, 64, 4 * HD), F32)
    out_spec = pl.BlockSpec((NY * NXH, 16, 4 * HD), lambda g: (0, g, 0))
    return pl.pallas_call(
        terms_in_kernel,
        grid=(4,),
        in_specs=[
            smem(),
            pl.BlockSpec((width // 4, length), lambda g: (g, 0)),
            pl.BlockSpec((shards, rows, 4 * HD), lambda g: (0, 0, 0)),
        ],
        out_specs=[out_spec] * 2,
        out_shape=[shape] * 2,
        scratch_shapes=[pltpu.VMEM((width // 4, 4 * HD), F32)],
        compiler_params=params(LIMIT),
        cost_estimate=pl.CostEstimate(
            flops=2 * width * length * 4 * HD, bytes_accessed=9 << 20, transcendentals=0
        ),
        name="terms_in",
    )(core, normed_t, back)


def terms_out_kernel(core_ref, at_ref, gated_ref, *refs):
    keep_ref, send_ref, res_ref, gated_t_ref = refs[-4:]
    shards, rows, _ = gated_ref.shape

    @pl.when(pl.program_id(0) == 0)
    def _():
        for shard in range(shards):
            gated_t_ref[:, shard * rows : (shard + 1) * rows] = gated_ref[shard].T

    total = None
    for r in range(shards):
        here = pl.ds(pl.multiple_of(at_ref[r] * rows, rows), rows)
        term = dot(gated_t_ref[:, here], refs[r][...])
        total = term if total is None else total + term
    res_ref[...] = total
    core = core_ref[0]
    for pair in range(NY * NXH):
        for out_ref, who in ((keep_ref, core), (send_ref, 1 - core)):
            out_ref[pair] = res_ref[pl.ds(pl.multiple_of((pair * NC + who) * 8, 8), 8), :]


def terms_out(core, at, back, cots):
    shards, rows, _ = back.shape
    width = cots[0].shape[1]
    length = shards * rows
    out_spec = pl.BlockSpec((NY * NXH, 8, 4 * HD), lambda g: (0, g, 0))
    return pl.pallas_call(
        terms_out_kernel,
        grid=(2,),
        in_specs=[smem(), smem(), pl.BlockSpec((shards, rows, HD), lambda g: (0, 0, 4))]
        + [pl.BlockSpec((rows, width // 2), lambda g: (0, g))] * shards,
        out_specs=[out_spec] * 2,
        out_shape=[jax.ShapeDtypeStruct((NY * NXH, 16, 4 * HD), F32)] * 2,
        scratch_shapes=[pltpu.VMEM((HD, width // 2), F32), pltpu.VMEM((HD, length), BF16)],
        compiler_params=params(LIMIT),
        cost_estimate=pl.CostEstimate(
            flops=2 * HD * width * length, bytes_accessed=6 << 20, transcendentals=0
        ),
        name="terms_out",
    )(core, at, back, *cots)


def small(kernel, name, scalars, arrays, outs, scratch=(), limit=12):
    size = sum(a.size * a.dtype.itemsize for a in arrays)
    return pl.pallas_call(
        kernel,
        in_specs=[smem()] + [vmem()] * len(arrays),
        out_specs=[vmem()] * len(outs),
        out_shape=[jax.ShapeDtypeStruct(shape, dtype) for shape, dtype in outs],
        scratch_shapes=list(scratch),
        compiler_params=params(limit),
        cost_estimate=pl.CostEstimate(flops=size, bytes_accessed=2 * size, transcendentals=0),
        name=name,
    )(scalars, *arrays)


def core_sum_kernel(pos_ref, keep_ref, got_ref, keep_out_ref, got_out_ref, own_ref, one_ref, three_ref, two_ref):
    y = pos_ref[0]
    for d, to_ref in ((0, own_ref), (1, one_ref), (3, three_ref), (2, two_ref)):
        here = pl.ds(((y - d + NY) % NY) * NXH, NXH)
        to_ref[:, :64, :] = (keep_ref[here] + got_ref[here]).astype(to_ref.dtype)
        to_ref[:, 64:, :] = (keep_out_ref[here] + got_out_ref[here]).astype(to_ref.dtype)


def y_sum_kernel(pos_ref, own_ref, a_ref, b_ref, c_ref, keep_ref, same_ref, one_ref, two_ref, sum_ref):
    xh, x = pos_ref[1], pos_ref[2]
    sum_ref[...] = own_ref[...] + (
        a_ref[...].astype(F32) + b_ref[...].astype(F32) + c_ref[...].astype(F32)
    )

    def slab(out_ref, h, l):
        for k in range(NZ):
            out_ref[k * 8 : (k + 1) * 8, :] = sum_ref[
                h, pl.ds(pl.multiple_of((k * NX + l) * 8, 8), 8), :
            ]

    slab(keep_ref, xh, x)
    keep_ref[32:, :] = sum_ref[xh, 64:, :]
    slab(same_ref, 1 - xh, x)
    same_ref[32:, :] = sum_ref[1 - xh, 64:, :]
    slab(one_ref, xh, 1 - x)
    slab(two_ref, 1 - xh, 1 - x)


def x_sum_kernel(pos_ref, keep_ref, same_ref, a_ref, b_ref, own_ref, one_ref, three_ref, two_ref, out_ref, sum_ref):
    z, x = pos_ref[3], pos_ref[2]
    mine = keep_ref[...] + same_ref[...]
    sum_ref[x] = mine[:32]
    sum_ref[1 - x] = a_ref[...] + b_ref[...]
    out_ref[...] = mine[32:]
    for d, to_ref in ((0, own_ref), (1, one_ref), (3, three_ref), (2, two_ref)):
        here = pl.ds(pl.multiple_of(((z - d + NZ) % NZ) * 8, 8), 8)
        for l in range(NX):
            to_ref[l * 8 : (l + 1) * 8, :] = sum_ref[l, here, :]


def z_place_kernel(factor, pos_ref, own_ref, one_ref, three_ref, two_ref, out_ref, w_in_ref, w_out_ref):
    z = pos_ref[3]
    for d, ref in ((0, own_ref), (1, one_ref), (3, three_ref), (2, two_ref)):
        for l in range(NX):
            for k in range(4):
                at = pl.multiple_of((k * H + ((z + d) % NZ) * NX + l) * HD, HD)
                w_in_ref[:, pl.ds(at, HD)] = (
                    ref[l * 8 : (l + 1) * 8, k * HD : (k + 1) * HD] * factor
                )
    w_out_ref[:, : 4 * HD] = out_ref[:8] * factor
    w_out_ref[:, 4 * HD :] = out_ref[8:] * factor


def columns(ref):
    return jnp.concatenate([ref[h] for h in range(H)], axis=1)


def shard_out_kernel(gated_ref, grad_ref, w_in_ref, w_out_ref, hist_ref, layer_ref, sum_ref):
    hist = hist_ref[...].astype(F32)
    layer_ref[...] = (hist + dot(columns(gated_ref), w_out_ref[...])).astype(BF16)
    sum_ref[...] = dot_nt(columns(grad_ref), w_in_ref[...])


def shard_more_kernel(grad_ref, w_in_ref, before_ref, sum_ref):
    term = dot_nt(columns(grad_ref), w_in_ref[...])

    @pl.when(pl.program_id(0) == 0)
    def _():
        sum_ref[...] = before_ref[...] + term

    @pl.when(pl.program_id(0) > 0)
    def _():
        sum_ref[...] += term


def shard_grad_kernel(grad_ref, w_in_ref, hist_ref, cot_ref, before_ref, grad_hist_ref):
    grad_normed = before_ref[...] + dot_nt(columns(grad_ref), w_in_ref[...])
    normed, inverse = layer_norm(hist_ref[...].astype(F32))
    grad = norm_back(normed, inverse, grad_normed)
    grad_hist_ref[...] = (cot_ref[...].astype(F32) + grad).astype(BF16)


def whole(a):
    return pl.BlockSpec(a.shape, lambda k: (0,) * a.ndim)


def shard_part(kernel, name, back, w_in, first, count, before, after, outs):
    rows, width = back.shape[1], w_in.shape[0]
    return pl.pallas_call(
        kernel,
        grid=(count,),
        in_specs=[pl.BlockSpec((H, rows, HD), lambda k: (0, 0, 4))] * before
        + [
            pl.BlockSpec((H, rows, HD), lambda k: (0, 0, first + k)),
            pl.BlockSpec((width, width), lambda k: (0, first + k)),
        ]
        + [whole(a) for a in after],
        out_specs=[pl.BlockSpec((rows, width), lambda k: (0, 0))] * len(outs),
        out_shape=[jax.ShapeDtypeStruct((rows, width), dtype) for dtype in outs],
        compiler_params=params(LIMIT),
        cost_estimate=pl.CostEstimate(
            flops=2 * (count + before) * rows * width * width, bytes_accessed=8 << 20, transcendentals=0
        ),
        name=name,
    )(*[back] * (before + 1), w_in, *after)


def local(history, segment_ids, w_in, w_out, cotangent):
    hist = history[0]
    cot = cotangent[0]
    rows, width = hist.shape
    length = rows * NZ * NX
    s = lax.axis_index("seq")
    u = lax.axis_index("user")
    z, x = s // NX, s % NX
    y, xh, core = u // (NXH * NC), (u // NC) % NXH, u % NC

    users = NY * NXH * NC
    tie = lax.optimization_barrier
    w_head = jnp.concatenate(
        [lax.dynamic_slice(w_in, (0, i * width + s * HD), (width, HD)) for i in range(4)], axis=1
    )

    def place_of(key):
        return ((z + key[0]) % NZ) * NX + (x ^ key[1])

    at_core = core.reshape(1)
    at = jnp.stack([y, xh, x, z])
    orders = (
        ((0, 0),),
        ((0, 1), (1, 0), (3, 0)),
        ((1, 1), (2, 0), (3, 1)),
        ((2, 1),),
        ((1, 0), (3, 0), (0, 1), (2, 0), (2, 1), (1, 1), (3, 1), (0, 0)),
    )
    places = {keys: jnp.stack([place_of(key) for key in keys]) for keys in orders}

    def project(got, outs):
        keys = tuple(sorted(got))
        return ln_proj(places[keys], [got[key] for key in keys], w_head, outs)

    got = {
        (1, 0): from_seq(hist, 1, 0),
        (3, 0): from_seq(hist, 3, 0),
        (0, 1): from_seq(hist, 0, 1),
    }
    outs = project({(0, 0): hist}, ())
    grad_gated_own = dot_nt(cot, w_out).astype(BF16).reshape(rows, H, HD).transpose(1, 0, 2)
    outs, grad_gated_own, waiting, at_core, at = tie(
        (outs, grad_gated_own, tuple(places.values()), at_core, at)
    )
    places = dict(zip(orders, waiting))
    ids = segment_ids[0].astype(BF16).reshape(2, HD)
    ids = jnp.pad(ids, ((0, 14), (0, 0)))
    to_heads = jnp.concatenate(
        [
            grad_gated_own,
            jnp.broadcast_to(ids[None], (H, 16, HD)),
        ],
        axis=1,
    )
    at_head = lax.all_to_all(to_heads, "seq", 0, 0, tiled=True)
    more = {
        (2, 0): from_seq(got[1, 0], 1, 0),
        (3, 1): from_seq(got[0, 1], 3, 0),
        (1, 1): from_seq(got[1, 0], 0, 1),
    }
    outs = project(got, outs)
    more, outs, cot_next = tie((more, outs, cot))
    last = {(2, 1): from_seq(more[2, 0], 0, 1)}
    cots = {(1, 0): from_seq(cot_next, 1, 0), (3, 0): from_seq(cot_next, 3, 0)}
    outs, at_head = tie((outs, at_head))
    outs = project(more, outs)
    last, cots, outs = tie((last, cots, outs))
    fresh = {(0, 1): from_seq(cot_next, 0, 1), (2, 0): from_seq(cots[1, 0], 1, 0)}
    normed_t, act, slope = project(last, outs)
    att, gate_t, gg_t, stats, start = forward(act, at_head)
    stats, fresh = tie((stats, fresh))
    cots.update(fresh)
    pair = jnp.stack([stats, from_seq(stats, 0, 1)])
    others = [from_seq(pair, dz, 0) for dz in (1, 3, 2)]
    pair, others, cots = tie((pair, others, cots))
    fresh = {
        (2, 1): from_seq(cots[2, 0], 0, 1),
        (1, 1): from_seq(cots[0, 1], 1, 0),
        (3, 1): from_seq(cots[0, 1], 3, 0),
    }
    back = backward([pair, *others], act, att, gate_t, gg_t, start, slope)
    back, fresh = tie((back, fresh))
    cots.update(fresh)
    cots[0, 0] = cot
    back_tok = lax.all_to_all(back, "seq", 0, 0, tiled=True)

    keep, send = terms_in(at_core, normed_t, back)
    got = from_user(send, 0, 0, 1)
    keep_out, send_out = terms_out(at_core, places[orders[4]], back, [cots[key] for key in orders[4]])
    got_out = from_user(send_out, 0, 0, 1)
    n = 4 * HD
    own, *sends = small(
        core_sum_kernel,
        "core_sum",
        at,
        [keep, got, keep_out, got_out],
        [((NXH, 80, n), F32)] + [((NXH, 80, n), BF16)] * 3,
        limit=LIMIT,
    )
    own, sends = tie((own, sends))
    sends = [from_user(a, d, 0, 0) for a, d in zip(sends, (1, 3, 2))]
    layer_out, partial = shard_part(
        shard_out_kernel, "shard_out", back_tok, w_in, 0, 1, 1, [w_out, hist], [BF16, F32]
    )
    sends, layer_out, partial = tie((sends, layer_out, partial))
    keep, same, one, two = small(
        y_sum_kernel,
        "y_sum",
        at,
        [own, *sends],
        [((48, n), F32)] * 2 + [((32, n), F32)] * 2,
        [pltpu.VMEM((NXH, 80, n), F32)],
    )
    same = from_both(same, 1, 0)
    one = from_both(one, 0, 1)
    two = from_both(two, 1, 1)
    (partial,) = shard_part(shard_more_kernel, "shard_more", back_tok, w_in, 1, 2, 0, [partial], [F32])
    same, one, two, partial = tie((same, one, two, partial))
    own, *sends, own_out = small(
        x_sum_kernel,
        "x_sum",
        at,
        [keep, same, one, two],
        [((16, n), F32)] * 5,
        [pltpu.VMEM((NX, 32, n), F32)],
    )
    sends = [from_seq(a, d, 0) for a, d in zip(sends, (1, 3, 2))]
    (grad_history,) = shard_part(
        shard_grad_kernel, "shard_grad", back_tok, w_in, 3, 1, 0, [hist, cot, partial], [BF16]
    )
    sends, grad_history = tie((sends, grad_history))
    factor = (length * users) ** (-0.5)
    grad_w_in, grad_w_out = small(
        functools.partial(z_place_kernel, factor),
        "z_place",
        at,
        [own, *sends, own_out],
        [((8, 4 * width), F32), ((8, width), F32)],
    )
    return layer_out[None], grad_history[None], grad_w_in, grad_w_out


def solution(mesh):
    in_specs = (P("user", "seq", None), P("user", "seq"), P(), P(), P("user", "seq", None))
    out_specs = (
        P("user", "seq", None),
        P("user", "seq", None),
        P(("seq", "user"), None),
        P(("seq", "user"), None),
    )
    return jax.shard_map(local, mesh=mesh, in_specs=in_specs, out_specs=out_specs, check_vma=False)
```

```python
import functools

import jax
import jax.numpy as jnp
from jax import lax
from jax.experimental import pallas as pl
from jax.experimental.pallas import tpu as pltpu
from jax.sharding import PartitionSpec as P

F32 = jnp.float32
BF16 = jnp.bfloat16
EPS = 1e-05
H = 8
HD = 128
NZ, NX = 4, 2
NY, NXH, NC = 4, 2, 2


def seq_perm(dz, dx):
    return [
        (((z + dz) % NZ) * NX + (x ^ dx), z * NX + x) for z in range(NZ) for x in range(NX)
    ]


def user_perm(dy, dh, dc):
    return [
        ((((y + dy) % NY) * NXH + (h ^ dh)) * NC + (c ^ dc), (y * NXH + h) * NC + c)
        for y in range(NY)
        for h in range(NXH)
        for c in range(NC)
    ]


def from_seq(a, dz, dx):
    return lax.ppermute(a, "seq", seq_perm(dz, dx))


def from_user(a, dy, dh, dc):
    return lax.ppermute(a, "user", user_perm(dy, dh, dc))


def from_both(a, dh, dx):
    pairs = []
    for s in range(NZ * NX):
        for u in range(NY * NXH * NC):
            pairs.append(((s ^ dx) * NY * NXH * NC + (u ^ (dh * NC)), s * NY * NXH * NC + u))
    return lax.ppermute(a, ("seq", "user"), pairs)


def layer_norm(entries):
    centre = jnp.mean(entries, axis=-1, keepdims=True)
    centred = entries - centre
    inverse = lax.rsqrt(jnp.mean(centred * centred, axis=-1, keepdims=True) + EPS)
    return centred * inverse, inverse


def norm_back(normed, inverse, upstream):
    first_term = jnp.mean(upstream, axis=-1, keepdims=True)
    second_term = jnp.mean(upstream * normed, axis=-1, keepdims=True)
    return inverse * (upstream - first_term - normed * second_term)


def dot(a, b):
    return jnp.dot(a, b, preferred_element_type=F32)


def dot_nt(a, b):
    return lax.dot_general(a, b, (((1,), (1,)), ((), ())), preferred_element_type=F32)


def dot_tn(a, b):
    return lax.dot_general(a, b, (((0,), (0,)), ((), ())), preferred_element_type=F32)


LIMIT = 56


def params(limit):
    return pltpu.CompilerParams(vmem_limit_bytes=limit << 20)


def ln_proj_kernel(count, at_ref, *refs):
    w_ref = refs[count]
    normed_ref, act_ref, slope_ref = refs[-3:]
    half = act_ref.shape[2]
    for k in range(count):

        @pl.when(pl.program_id(0) == k)
        def _():
            normed, _ = layer_norm(refs[k][...].astype(F32))
            normed_b = normed.astype(BF16)
            normed_ref[...] = normed_b.T
            projected = dot(normed_b, w_ref[...])
            tanh = jnp.tanh(0.5 * projected)
            sig = 0.5 + 0.5 * tanh
            silu = projected * sig
            act = silu.astype(BF16)
            slope = sig + silu * (1.0 - sig)
            for i in range(2):
                act_ref[i, 0] = act[i * half : (i + 1) * half]
                slope_ref[i, 0] = slope[i * half : (i + 1) * half]


def ln_proj(at, blocks, w_head, outs):
    rows, width = blocks[0].shape
    cols = w_head.shape[1]
    half, shards = rows // 2, NZ * NX
    by_half = pl.BlockSpec((2, 1, half, cols), lambda i, at_ref: (0, at_ref[i], 0, 0))
    in_specs = [pl.BlockSpec((rows, width), lambda i, at_ref: (0, 0))] * len(blocks)
    in_specs.append(pl.BlockSpec((width, cols), lambda i, at_ref: (0, 0)))
    aliases = {}
    if outs:
        in_specs += [pl.BlockSpec(memory_space=pl.ANY)] * 3
        aliases = {len(in_specs) + k - 2: k for k in range(3)}
    return pl.pallas_call(
        functools.partial(ln_proj_kernel, len(blocks)),
        grid_spec=pltpu.PrefetchScalarGridSpec(
            num_scalar_prefetch=1,
            grid=(len(blocks),),
            in_specs=in_specs,
            out_specs=(
                pl.BlockSpec((width, rows), lambda i, at_ref: (0, at_ref[i])),
                by_half,
                by_half,
            ),
        ),
        out_shape=(
            jax.ShapeDtypeStruct((width, rows * shards), BF16),
            jax.ShapeDtypeStruct((2, shards, half, cols), BF16),
            jax.ShapeDtypeStruct((2, shards, half, cols), F32),
        ),
        input_output_aliases=aliases,
        compiler_params=params(LIMIT),
        cost_estimate=pl.CostEstimate(
            flops=2 * rows * width * cols * len(blocks),
            bytes_accessed=3 * len(blocks) << 20,
            transcendentals=rows * cols * len(blocks),
        ),
        name="ln_proj",
    )(at, *blocks, w_head, *outs)


FQ, FK = 512, 512
BQ, BK = 512, 256
SCALE = HD ** (-0.5)
UNSEEN = -1024.0


def tile_place(block):
    last = 2 * NZ * NX - 1
    return (block, 0) if block < NZ * NX else (last - block, HD)


def time_rows(ref, first, count, column, columns=1):
    parts = []
    for block in range(first // HD, (first + count) // HD):
        shard, row = tile_place(block)
        parts.append(ref[row // HD, shard, :, column * HD : (column + columns) * HD])
    return parts[0] if len(parts) == 1 else jnp.concatenate(parts, axis=0)


def tiles(length, rows, cols):
    key_row = lax.broadcasted_iota(jnp.int32, (cols, rows), 0)
    query_col = lax.broadcasted_iota(jnp.int32, (1, rows), 1)

    def seen(i, j, start):
        mask = key_row >= start - j
        if j + cols > i:
            mask = mask & (key_row <= query_col + (i - j))
        return mask

    return [(i, range(0, i + rows, cols)) for i in range(0, length, rows)], seen


def forward_kernel(act_ref, head_ref, att_ref, gate_ref, gg_ref, stats_ref, start_ref):
    length = att_ref.shape[1]
    rows = length // (NZ * NX)
    users = [head_ref[shard, rows:, :].astype(F32) for shard in range(NZ * NX)]
    places = [tile_place(block) for block in range(length // HD)]
    ids = jnp.concatenate([users[s][r // HD : r // HD + 1] for s, r in places], axis=1)
    first = jnp.zeros((1, length), F32)
    for v in range(3):
        count = jnp.sum(jnp.where(ids == v, 1.0, 0.0), axis=1, keepdims=True)
        first = first + jnp.where(ids > v, count, 0.0)
    start_ref[...] = first.astype(jnp.int32)
    values_t = [time_rows(act_ref, j, FK, 1).T for j in range(0, length, FK)]
    keys = [time_rows(act_ref, j, FK, 3) for j in range(0, length, FK)]
    queries_in, seen = tiles(length, FQ, FK)
    for i, keys_in in queries_in:
        at = slice(i, i + FQ)
        queries = time_rows(act_ref, i, FQ, 2)
        start = start_ref[:, at]
        total = None
        for j in keys_in:
            half = dot_nt(keys[j // FK], queries) * (0.5 * SCALE)
            half = jnp.where(seen(i, j, start), half, UNSEEN)
            weights = (half + half * jnp.tanh(half)).astype(BF16)
            term = dot(values_t[j // FK], weights)
            total = term if total is None else total + term
        att_ref[:, at] = total
        gate = time_rows(act_ref, i, FQ, 0).T
        parts = []
        for block in range(i // HD, (i + FQ) // HD):
            shard, row = tile_place(block)
            parts.append(head_ref[shard, row : row + HD, :])
        gg = jnp.concatenate(parts, axis=0).T
        gate_ref[:, at] = gate
        gg_ref[:, at] = gg
        grad_mixed = gg.astype(F32) * gate.astype(F32)
        mean = jnp.sum(total, axis=0, keepdims=True) * (1.0 / HD)
        centred = total - mean
        stats_ref[0:1, at] = mean
        stats_ref[1:2, at] = jnp.sum(centred * centred, axis=0, keepdims=True)
        stats_ref[2:3, at] = jnp.sum(grad_mixed, axis=0, keepdims=True)
        stats_ref[3:4, at] = jnp.sum(grad_mixed * centred, axis=0, keepdims=True)


def vmem():
    return pl.BlockSpec(memory_space=pltpu.VMEM)


def smem():
    return pl.BlockSpec(memory_space=pltpu.SMEM)


def forward(act, at_head):
    length = HD * 2 * NZ * NX
    return pl.pallas_call(
        forward_kernel,
        in_specs=[vmem()] * 2,
        out_specs=[vmem()] * 5,
        out_shape=(
            jax.ShapeDtypeStruct((HD, length), F32),
            jax.ShapeDtypeStruct((HD, length), BF16),
            jax.ShapeDtypeStruct((HD, length), BF16),
            jax.ShapeDtypeStruct((4, length), F32),
            jax.ShapeDtypeStruct((1, length), jnp.int32),
        ),
        compiler_params=params(LIMIT),
        cost_estimate=pl.CostEstimate(
            flops=8 * HD * length * length, bytes_accessed=6 << 20, transcendentals=length * length // 2
        ),
        name="attention_forward",
    )(act, at_head)


def backward_kernel(*refs):
    act_ref, att_ref, gate_ref, gg_ref, start_ref, slope_hbm, back_ref = refs[H : H + 7]
    dk_ref, dv_ref, slope_ref, sem = refs[H + 7 :]
    length = att_ref.shape[1]
    width = H * HD
    copy = pltpu.make_async_copy(slope_hbm, slope_ref, sem)
    copy.start()
    heads = [ref[...] for ref in refs[:H]]
    mean_all = sum(a[0:1] for a in heads) * (1.0 / H)
    apart = [a[0:1] - mean_all for a in heads]
    spread = sum(a[1:2] for a in heads) + HD * sum(d * d for d in apart)
    inverse_all = lax.rsqrt(spread * (1.0 / width) + EPS)
    first_all = sum(a[2:3] for a in heads) * (1.0 / width)
    second_all = inverse_all * sum(a[3:4] + d * a[2:3] for a, d in zip(heads, apart)) * (1.0 / width)

    keys = [time_rows(act_ref, j, BK, 3) for j in range(0, length, BK)]
    keys_t = [k.T for k in keys]
    values = [time_rows(act_ref, j, BK, 1) for j in range(0, length, BK)]
    queries_in, seen = tiles(length, BQ, BK)

    def put(first, column, value):
        value = value.astype(BF16)
        for k in range(value.shape[0] // HD):
            shard, row = tile_place(first // HD + k)
            back_ref[shard, row : row + HD, column * HD : (column + 1) * HD] = value[
                k * HD : (k + 1) * HD
            ]

    def put_grad(first, column, value):
        put(first, column, value * time_rows(slope_ref, first, value.shape[0], column))

    started = set()
    for i, keys_in in queries_in:
        at = slice(i, i + BQ)
        gate = gate_ref[:, at].astype(F32)
        gg = gg_ref[:, at].astype(F32)
        inverse = inverse_all[:, at]
        mixed = (att_ref[:, at] - mean_all[:, at]) * inverse
        grad_att = inverse * (gg * gate - first_all[:, at] - mixed * second_all[:, at])
        grad_out_t = grad_att.astype(BF16)
        grad_out = grad_out_t.T
        queries = time_rows(act_ref, i, BQ, 2)
        start = start_ref[:, at]
        total = None
        for j in keys_in:
            here = slice(j, j + BK)
            half = dot_nt(keys[j // BK], queries) * (0.5 * SCALE)
            half = jnp.where(seen(i, j, start), half, UNSEEN)
            tanh = jnp.tanh(half)
            weights = half + half * tanh
            sig = 0.5 + 0.5 * tanh
            slope = sig + weights * (1.0 - sig)
            ahead = dot(values[j // BK], grad_out_t)
            weights = weights.astype(BF16)
            slopes = (ahead * slope).astype(BF16)
            dv = dot(weights, grad_out)
            dk = dot(slopes, queries)
            if j in started:
                dv_ref[here, :] += dv
                dk_ref[here, :] += dk
            else:
                dv_ref[here, :] = dv
                dk_ref[here, :] = dk
                started.add(j)
            term = dot(keys_t[j // BK], slopes)
            total = term if total is None else total + term
        if i == 0:
            copy.wait()
        put(i, 4, (mixed * gate).astype(BF16).T)
        put_grad(i, 0, (gg * mixed).T)
        put_grad(i, 2, total.T * SCALE)
    for j in range(0, length, BK):
        put_grad(j, 1, dv_ref[j : j + BK, :])
        put_grad(j, 3, dk_ref[j : j + BK, :] * SCALE)


def backward(stats, act, att, gate, gg, start, slope):
    length = start.shape[1]
    shards = NZ * NX
    return pl.pallas_call(
        backward_kernel,
        in_specs=[vmem()] * (H + 5) + [pl.BlockSpec(memory_space=pl.ANY)],
        out_specs=vmem(),
        out_shape=jax.ShapeDtypeStruct((shards, length // shards, 5 * HD), BF16),
        scratch_shapes=[pltpu.VMEM((length, HD), F32)] * 2
        + [pltpu.VMEM(slope.shape, F32), pltpu.SemaphoreType.DMA],
        compiler_params=params(LIMIT),
        cost_estimate=pl.CostEstimate(
            flops=15 * HD * length * length, bytes_accessed=10 << 20, transcendentals=length * length // 2
        ),
        name="attention_backward",
    )(*stats, act, att, gate, gg, start, slope)


def terms_in_kernel(core_ref, normed_ref, grad_ref, keep_ref, send_ref, res_ref):
    shards, rows, cols = grad_ref.shape
    res_ref[...] = dot(normed_ref[...], grad_ref[...].reshape(shards * rows, cols))
    core = core_ref[0]
    for k in range(res_ref.shape[0] // HD):
        for pair in range(NY * NXH):
            mine = pl.multiple_of(k * HD + (pair * NC + core) * 8, 8)
            other = pl.multiple_of(k * HD + (pair * NC + 1 - core) * 8, 8)
            keep_ref[pair, k * 8 : (k + 1) * 8, :] = res_ref[pl.ds(mine, 8), :]
            send_ref[pair, k * 8 : (k + 1) * 8, :] = res_ref[pl.ds(other, 8), :]


def terms_in(core, normed_t, back):
    width, length = normed_t.shape
    shards, rows, _ = back.shape
    shape = jax.ShapeDtypeStruct((NY * NXH, 64, 4 * HD), F32)
    out_spec = pl.BlockSpec((NY * NXH, 32, 4 * HD), lambda g: (0, g, 0))
    return pl.pallas_call(
        terms_in_kernel,
        grid=(2,),
        in_specs=[
            smem(),
            pl.BlockSpec((width // 2, length), lambda g: (g, 0)),
            pl.BlockSpec((shards, rows, 4 * HD), lambda g: (0, 0, 0)),
        ],
        out_specs=[out_spec] * 2,
        out_shape=[shape] * 2,
        scratch_shapes=[pltpu.VMEM((width // 2, 4 * HD), F32)],
        compiler_params=params(LIMIT),
        cost_estimate=pl.CostEstimate(
            flops=2 * width * length * 4 * HD, bytes_accessed=9 << 20, transcendentals=0
        ),
        name="terms_in",
    )(core, normed_t, back)


def terms_out_kernel(core_ref, at_ref, gated_ref, *refs):
    keep_ref, send_ref, res_ref, gated_t_ref = refs[-4:]
    shards, rows, _ = gated_ref.shape

    @pl.when(pl.program_id(0) == 0)
    def _():
        for shard in range(shards):
            gated_t_ref[:, shard * rows : (shard + 1) * rows] = gated_ref[shard].T

    total = None
    for r in range(shards):
        here = pl.ds(pl.multiple_of(at_ref[r] * rows, rows), rows)
        term = dot(gated_t_ref[:, here], refs[r][...])
        total = term if total is None else total + term
    res_ref[...] = total
    core = core_ref[0]
    for pair in range(NY * NXH):
        for out_ref, who in ((keep_ref, core), (send_ref, 1 - core)):
            out_ref[pair] = res_ref[pl.ds(pl.multiple_of((pair * NC + who) * 8, 8), 8), :]


def terms_out(core, at, back, cots):
    shards, rows, _ = back.shape
    width = cots[0].shape[1]
    length = shards * rows
    out_spec = pl.BlockSpec((NY * NXH, 8, 4 * HD), lambda g: (0, g, 0))
    return pl.pallas_call(
        terms_out_kernel,
        grid=(2,),
        in_specs=[smem(), smem(), pl.BlockSpec((shards, rows, HD), lambda g: (0, 0, 4))]
        + [pl.BlockSpec((rows, width // 2), lambda g: (0, g))] * shards,
        out_specs=[out_spec] * 2,
        out_shape=[jax.ShapeDtypeStruct((NY * NXH, 16, 4 * HD), F32)] * 2,
        scratch_shapes=[pltpu.VMEM((HD, width // 2), F32), pltpu.VMEM((HD, length), BF16)],
        compiler_params=params(LIMIT),
        cost_estimate=pl.CostEstimate(
            flops=2 * HD * width * length, bytes_accessed=6 << 20, transcendentals=0
        ),
        name="terms_out",
    )(core, at, back, *cots)


def small(kernel, name, scalars, arrays, outs, scratch=(), limit=12):
    size = sum(a.size * a.dtype.itemsize for a in arrays)
    return pl.pallas_call(
        kernel,
        in_specs=[smem()] + [vmem()] * len(arrays),
        out_specs=[vmem()] * len(outs),
        out_shape=[jax.ShapeDtypeStruct(shape, dtype) for shape, dtype in outs],
        scratch_shapes=list(scratch),
        compiler_params=params(limit),
        cost_estimate=pl.CostEstimate(flops=size, bytes_accessed=2 * size, transcendentals=0),
        name=name,
    )(scalars, *arrays)


def core_sum_kernel(pos_ref, keep_ref, got_ref, keep_out_ref, got_out_ref, own_ref, one_ref, three_ref, two_ref):
    y = pos_ref[0]
    for d, to_ref in ((0, own_ref), (1, one_ref), (3, three_ref), (2, two_ref)):
        here = pl.ds(((y - d + NY) % NY) * NXH, NXH)
        to_ref[:, :64, :] = (keep_ref[here] + got_ref[here]).astype(to_ref.dtype)
        to_ref[:, 64:, :] = (keep_out_ref[here] + got_out_ref[here]).astype(to_ref.dtype)


def y_sum_kernel(pos_ref, own_ref, a_ref, b_ref, c_ref, keep_ref, same_ref, one_ref, two_ref, sum_ref):
    xh, x = pos_ref[1], pos_ref[2]
    sum_ref[...] = own_ref[...] + (
        a_ref[...].astype(F32) + b_ref[...].astype(F32) + c_ref[...].astype(F32)
    )

    def slab(out_ref, h, l):
        for k in range(NZ):
            out_ref[k * 8 : (k + 1) * 8, :] = sum_ref[
                h, pl.ds(pl.multiple_of((k * NX + l) * 8, 8), 8), :
            ]

    slab(keep_ref, xh, x)
    keep_ref[32:, :] = sum_ref[xh, 64:, :]
    slab(same_ref, 1 - xh, x)
    same_ref[32:, :] = sum_ref[1 - xh, 64:, :]
    slab(one_ref, xh, 1 - x)
    slab(two_ref, 1 - xh, 1 - x)


def x_sum_kernel(pos_ref, keep_ref, same_ref, a_ref, b_ref, own_ref, one_ref, three_ref, two_ref, out_ref, sum_ref):
    z, x = pos_ref[3], pos_ref[2]
    mine = keep_ref[...] + same_ref[...]
    sum_ref[x] = mine[:32]
    sum_ref[1 - x] = a_ref[...] + b_ref[...]
    out_ref[...] = mine[32:]
    for d, to_ref in ((0, own_ref), (1, one_ref), (3, three_ref), (2, two_ref)):
        here = pl.ds(pl.multiple_of(((z - d + NZ) % NZ) * 8, 8), 8)
        for l in range(NX):
            to_ref[l * 8 : (l + 1) * 8, :] = sum_ref[l, here, :]


def z_place_kernel(factor, pos_ref, own_ref, one_ref, three_ref, two_ref, out_ref, w_in_ref, w_out_ref):
    z = pos_ref[3]
    for d, ref in ((0, own_ref), (1, one_ref), (3, three_ref), (2, two_ref)):
        for l in range(NX):
            for k in range(4):
                at = pl.multiple_of((k * H + ((z + d) % NZ) * NX + l) * HD, HD)
                w_in_ref[:, pl.ds(at, HD)] = (
                    ref[l * 8 : (l + 1) * 8, k * HD : (k + 1) * HD] * factor
                )
    w_out_ref[:, : 4 * HD] = out_ref[:8] * factor
    w_out_ref[:, 4 * HD :] = out_ref[8:] * factor


def columns(ref):
    return jnp.concatenate([ref[h] for h in range(H)], axis=1)


def shard_out_kernel(gated_ref, grad_ref, w_in_ref, w_out_ref, hist_ref, layer_ref, acc_ref):
    term = dot_nt(columns(grad_ref), w_in_ref[...])

    @pl.when(pl.program_id(0) == 0)
    def _():
        hist = hist_ref[...].astype(F32)
        layer_ref[...] = (hist + dot(columns(gated_ref), w_out_ref[...])).astype(BF16)
        acc_ref[...] = term

    @pl.when(pl.program_id(0) > 0)
    def _():
        acc_ref[...] += term


def shard_grad_kernel(grad_ref, w_in_ref, hist_ref, cot_ref, half_ref, grad_hist_ref, acc_ref):
    term = dot_nt(columns(grad_ref), w_in_ref[...])

    @pl.when(pl.program_id(0) == 0)
    def _():
        acc_ref[...] = half_ref[...] + term

    @pl.when(pl.program_id(0) > 0)
    def _():
        normed, inverse = layer_norm(hist_ref[...].astype(F32))
        grad = norm_back(normed, inverse, acc_ref[...] + term)
        grad_hist_ref[...] = (cot_ref[...].astype(F32) + grad).astype(BF16)


def shard_out(back, w_in, w_out, hist):
    rows, width = hist.shape
    whole = lambda a: pl.BlockSpec(a.shape, lambda k: (0,) * a.ndim)
    return pl.pallas_call(
        shard_out_kernel,
        grid=(2,),
        in_specs=[
            pl.BlockSpec((H, rows, HD), lambda k: (0, 0, 4)),
            pl.BlockSpec((H, rows, HD), lambda k: (0, 0, k)),
            pl.BlockSpec((width, width), lambda k: (0, k)),
            whole(w_out),
            whole(hist),
        ],
        out_specs=[whole(hist)] * 2,
        out_shape=[jax.ShapeDtypeStruct(hist.shape, BF16), jax.ShapeDtypeStruct(hist.shape, F32)],
        compiler_params=params(LIMIT),
        cost_estimate=pl.CostEstimate(
            flops=6 * rows * width * width, bytes_accessed=8 << 20, transcendentals=0
        ),
        name="shard_out",
    )(back, back, w_in, w_out, hist)


def shard_grad(back, w_in, hist, cot, half):
    rows, width = hist.shape
    whole = lambda a: pl.BlockSpec(a.shape, lambda k: (0,) * a.ndim)
    return pl.pallas_call(
        shard_grad_kernel,
        grid=(2,),
        in_specs=[
            pl.BlockSpec((H, rows, HD), lambda k: (0, 0, 2 + k)),
            pl.BlockSpec((width, width), lambda k: (0, 2 + k)),
            whole(hist),
            whole(cot),
            whole(half),
        ],
        out_specs=whole(hist),
        out_shape=jax.ShapeDtypeStruct(hist.shape, BF16),
        scratch_shapes=[pltpu.VMEM((rows, width), F32)],
        compiler_params=params(LIMIT),
        cost_estimate=pl.CostEstimate(
            flops=4 * rows * width * width, bytes_accessed=8 << 20, transcendentals=0
        ),
        name="shard_grad",
    )(back, w_in, hist, cot, half)


def local(history, segment_ids, w_in, w_out, cotangent):
    hist = history[0]
    cot = cotangent[0]
    rows, width = hist.shape
    length = rows * NZ * NX
    s = lax.axis_index("seq")
    u = lax.axis_index("user")
    z, x = s // NX, s % NX
    y, xh, core = u // (NXH * NC), (u // NC) % NXH, u % NC

    users = NY * NXH * NC
    tie = lax.optimization_barrier
    w_head = jnp.concatenate(
        [lax.dynamic_slice(w_in, (0, i * width + s * HD), (width, HD)) for i in range(4)], axis=1
    )

    def place_of(key):
        return ((z + key[0]) % NZ) * NX + (x ^ key[1])

    at_core = core.reshape(1)
    at = jnp.stack([y, xh, x, z])
    orders = (
        ((0, 0),),
        ((0, 1), (1, 0), (3, 0)),
        ((1, 1), (2, 0), (3, 1)),
        ((2, 1),),
        ((1, 0), (3, 0), (0, 1), (2, 0), (2, 1), (1, 1), (3, 1), (0, 0)),
    )
    places = {keys: jnp.stack([place_of(key) for key in keys]) for keys in orders}

    def project(got, outs):
        keys = tuple(sorted(got))
        return ln_proj(places[keys], [got[key] for key in keys], w_head, outs)

    got = {
        (1, 0): from_seq(hist, 1, 0),
        (3, 0): from_seq(hist, 3, 0),
        (0, 1): from_seq(hist, 0, 1),
    }
    outs = project({(0, 0): hist}, ())
    grad_gated_own = dot_nt(cot, w_out).astype(BF16).reshape(rows, H, HD).transpose(1, 0, 2)
    got, outs, grad_gated_own, waiting, at_core, at = tie(
        (got, outs, grad_gated_own, tuple(places.values()), at_core, at)
    )
    places = dict(zip(orders, waiting))
    ids = segment_ids[0].astype(BF16).reshape(2, HD)
    ids = jnp.pad(ids, ((0, 14), (0, 0)))
    to_heads = jnp.concatenate(
        [
            grad_gated_own,
            jnp.broadcast_to(ids[None], (H, 16, HD)),
        ],
        axis=1,
    )
    at_head = lax.all_to_all(to_heads, "seq", 0, 0, tiled=True)
    more = {
        (2, 0): from_seq(got[1, 0], 1, 0),
        (3, 1): from_seq(got[0, 1], 3, 0),
        (1, 1): from_seq(got[1, 0], 0, 1),
    }
    outs = project(got, outs)
    more, outs, cot_next = tie((more, outs, cot))
    last = {(2, 1): from_seq(more[2, 0], 0, 1)}
    cots = {(1, 0): from_seq(cot_next, 1, 0), (3, 0): from_seq(cot_next, 3, 0)}
    outs, at_head = tie((outs, at_head))
    outs = project(more, outs)
    last, cots, outs = tie((last, cots, outs))
    fresh = {(0, 1): from_seq(cot_next, 0, 1), (2, 0): from_seq(cots[1, 0], 1, 0)}
    normed_t, act, slope = project(last, outs)
    att, gate_t, gg_t, stats, start = forward(act, at_head)
    stats, fresh = tie((stats, fresh))
    cots.update(fresh)
    others = [from_seq(stats, dz, dx) for dz, dx in ((2, 1), (1, 1), (3, 1), (2, 0), (1, 0), (3, 0), (0, 1))]
    stats, others, cots = tie((stats, others, cots))
    fresh = {
        (2, 1): from_seq(cots[2, 0], 0, 1),
        (1, 1): from_seq(cots[0, 1], 1, 0),
        (3, 1): from_seq(cots[0, 1], 3, 0),
    }
    back = backward([stats, *others], act, att, gate_t, gg_t, start, slope)
    back, fresh = tie((back, fresh))
    cots.update(fresh)
    cots[0, 0] = cot
    back_tok = lax.all_to_all(back, "seq", 0, 0, tiled=True)

    keep, send = terms_in(at_core, normed_t, back)
    got = from_user(send, 0, 0, 1)
    keep_out, send_out = terms_out(at_core, places[orders[4]], back, [cots[key] for key in orders[4]])
    got_out = from_user(send_out, 0, 0, 1)
    n = 4 * HD
    own, *sends = small(
        core_sum_kernel,
        "core_sum",
        at,
        [keep, got, keep_out, got_out],
        [((NXH, 80, n), F32)] + [((NXH, 80, n), BF16)] * 3,
        limit=LIMIT,
    )
    own, sends = tie((own, sends))
    sends = [from_user(a, d, 0, 0) for a, d in zip(sends, (1, 3, 2))]
    layer_out, half = shard_out(back_tok, w_in, w_out, hist)
    sends, layer_out, half = tie((sends, layer_out, half))
    keep, same, one, two = small(
        y_sum_kernel,
        "y_sum",
        at,
        [own, *sends],
        [((48, n), F32)] * 2 + [((32, n), F32)] * 2,
        [pltpu.VMEM((NXH, 80, n), F32)],
    )
    same = from_both(same, 1, 0)
    one = from_both(one, 0, 1)
    two = from_both(two, 1, 1)
    grad_history = shard_grad(back_tok, w_in, hist, cot, half)
    same, one, two, grad_history = tie((same, one, two, grad_history))
    own, *sends, own_out = small(
        x_sum_kernel,
        "x_sum",
        at,
        [keep, same, one, two],
        [((16, n), F32)] * 5,
        [pltpu.VMEM((NX, 32, n), F32)],
    )
    sends = [from_seq(a, d, 0) for a, d in zip(sends, (1, 3, 2))]
    factor = (length * users) ** (-0.5)
    grad_w_in, grad_w_out = small(
        functools.partial(z_place_kernel, factor),
        "z_place",
        at,
        [own, *sends, own_out],
        [((8, 4 * width), F32), ((8, width), F32)],
    )
    return layer_out[None], grad_history[None], grad_w_in, grad_w_out


def solution(mesh):
    in_specs = (P("user", "seq", None), P("user", "seq"), P(), P(), P("user", "seq", None))
    out_specs = (
        P("user", "seq", None),
        P("user", "seq", None),
        P(("seq", "user"), None),
        P(("seq", "user"), None),
    )
    return jax.shard_map(local, mesh=mesh, in_specs=in_specs, out_specs=out_specs, check_vma=False)
```

```python
import functools

import jax
import jax.numpy as jnp
from jax import lax
from jax.experimental import pallas as pl
from jax.experimental.pallas import tpu as pltpu
from jax.sharding import PartitionSpec as P

F32 = jnp.float32
BF16 = jnp.bfloat16
EPS = 1e-05
H = 8
HD = 128
NZ, NX = 4, 2
NY, NXH, NC = 4, 2, 2


def seq_perm(dz, dx):
    return [
        (((z + dz) % NZ) * NX + (x ^ dx), z * NX + x) for z in range(NZ) for x in range(NX)
    ]


def user_perm(dy, dh, dc):
    return [
        ((((y + dy) % NY) * NXH + (h ^ dh)) * NC + (c ^ dc), (y * NXH + h) * NC + c)
        for y in range(NY)
        for h in range(NXH)
        for c in range(NC)
    ]


def from_seq(a, dz, dx):
    return lax.ppermute(a, "seq", seq_perm(dz, dx))


def from_user(a, dy, dh, dc):
    return lax.ppermute(a, "user", user_perm(dy, dh, dc))


def from_both(a, dh, dx):
    pairs = []
    for s in range(NZ * NX):
        for u in range(NY * NXH * NC):
            pairs.append(((s ^ dx) * NY * NXH * NC + (u ^ (dh * NC)), s * NY * NXH * NC + u))
    return lax.ppermute(a, ("seq", "user"), pairs)


def layer_norm(entries):
    centre = jnp.mean(entries, axis=-1, keepdims=True)
    centred = entries - centre
    inverse = lax.rsqrt(jnp.mean(centred * centred, axis=-1, keepdims=True) + EPS)
    return centred * inverse, inverse


def norm_back(normed, inverse, upstream):
    first_term = jnp.mean(upstream, axis=-1, keepdims=True)
    second_term = jnp.mean(upstream * normed, axis=-1, keepdims=True)
    return inverse * (upstream - first_term - normed * second_term)


def dot(a, b):
    return jnp.dot(a, b, preferred_element_type=F32)


def dot_nt(a, b):
    return lax.dot_general(a, b, (((1,), (1,)), ((), ())), preferred_element_type=F32)


def dot_tn(a, b):
    return lax.dot_general(a, b, (((0,), (0,)), ((), ())), preferred_element_type=F32)


LIMIT = 56


def params(limit):
    return pltpu.CompilerParams(vmem_limit_bytes=limit << 20)


def ln_proj_kernel(count, at_ref, *refs):
    w_ref = refs[count]
    normed_ref, act_ref, slope_ref = refs[-3:]
    half = act_ref.shape[2]
    for k in range(count):

        @pl.when(pl.program_id(0) == k)
        def _():
            normed, _ = layer_norm(refs[k][...].astype(F32))
            normed_b = normed.astype(BF16)
            normed_ref[...] = normed_b.T
            projected = dot(normed_b, w_ref[...])
            tanh = jnp.tanh(0.5 * projected)
            sig = 0.5 + 0.5 * tanh
            silu = projected * sig
            act = silu.astype(BF16)
            slope = sig + silu * (1.0 - sig)
            for i in range(2):
                act_ref[i, 0] = act[i * half : (i + 1) * half]
                slope_ref[i, 0] = slope[i * half : (i + 1) * half]


def ln_proj(at, blocks, w_head, outs):
    rows, width = blocks[0].shape
    cols = w_head.shape[1]
    half, shards = rows // 2, NZ * NX
    by_half = pl.BlockSpec((2, 1, half, cols), lambda i, at_ref: (0, at_ref[i], 0, 0))
    in_specs = [pl.BlockSpec((rows, width), lambda i, at_ref: (0, 0))] * len(blocks)
    in_specs.append(pl.BlockSpec((width, cols), lambda i, at_ref: (0, 0)))
    aliases = {}
    if outs:
        in_specs += [pl.BlockSpec(memory_space=pl.ANY)] * 3
        aliases = {len(in_specs) + k - 2: k for k in range(3)}
    return pl.pallas_call(
        functools.partial(ln_proj_kernel, len(blocks)),
        grid_spec=pltpu.PrefetchScalarGridSpec(
            num_scalar_prefetch=1,
            grid=(len(blocks),),
            in_specs=in_specs,
            out_specs=(
                pl.BlockSpec((width, rows), lambda i, at_ref: (0, at_ref[i])),
                by_half,
                by_half,
            ),
        ),
        out_shape=(
            jax.ShapeDtypeStruct((width, rows * shards), BF16),
            jax.ShapeDtypeStruct((2, shards, half, cols), BF16),
            jax.ShapeDtypeStruct((2, shards, half, cols), F32),
        ),
        input_output_aliases=aliases,
        compiler_params=params(LIMIT),
        cost_estimate=pl.CostEstimate(
            flops=2 * rows * width * cols * len(blocks),
            bytes_accessed=3 * len(blocks) << 20,
            transcendentals=rows * cols * len(blocks),
        ),
        name="ln_proj",
    )(at, *blocks, w_head, *outs)


FQ, FK = 512, 512
BQ, BK = 512, 256
SCALE = HD ** (-0.5)
UNSEEN = -1024.0


def tile_place(block):
    last = 2 * NZ * NX - 1
    return (block, 0) if block < NZ * NX else (last - block, HD)


def time_rows(ref, first, count, column, columns=1):
    parts = []
    for block in range(first // HD, (first + count) // HD):
        shard, row = tile_place(block)
        parts.append(ref[row // HD, shard, :, column * HD : (column + columns) * HD])
    return parts[0] if len(parts) == 1 else jnp.concatenate(parts, axis=0)


def tiles(length, rows, cols):
    key_row = lax.broadcasted_iota(jnp.int32, (cols, rows), 0)
    query_col = lax.broadcasted_iota(jnp.int32, (1, rows), 1)

    def seen(i, j, start):
        mask = key_row >= start - j
        if j + cols > i:
            mask = mask & (key_row <= query_col + (i - j))
        return mask

    return [(i, range(0, i + rows, cols)) for i in range(0, length, rows)], seen


def forward_kernel(act_ref, head_ref, att_ref, gate_ref, gg_ref, stats_ref, start_ref):
    length = att_ref.shape[1]
    rows = length // (NZ * NX)
    users = [head_ref[shard, rows:, :].astype(F32) for shard in range(NZ * NX)]
    places = [tile_place(block) for block in range(length // HD)]
    ids = jnp.concatenate([users[s][r // HD : r // HD + 1] for s, r in places], axis=1)
    first = jnp.zeros((1, length), F32)
    for v in range(3):
        count = jnp.sum(jnp.where(ids == v, 1.0, 0.0), axis=1, keepdims=True)
        first = first + jnp.where(ids > v, count, 0.0)
    start_ref[...] = first.astype(jnp.int32)
    values_t = [time_rows(act_ref, j, FK, 1).T for j in range(0, length, FK)]
    keys = [time_rows(act_ref, j, FK, 3) for j in range(0, length, FK)]
    queries_in, seen = tiles(length, FQ, FK)
    for i, keys_in in queries_in:
        at = slice(i, i + FQ)
        queries = time_rows(act_ref, i, FQ, 2)
        start = start_ref[:, at]
        total = None
        for j in keys_in:
            half = dot_nt(keys[j // FK], queries) * (0.5 * SCALE)
            half = jnp.where(seen(i, j, start), half, UNSEEN)
            weights = (half + half * jnp.tanh(half)).astype(BF16)
            term = dot(values_t[j // FK], weights)
            total = term if total is None else total + term
        att_ref[:, at] = total
        gate = time_rows(act_ref, i, FQ, 0).T
        parts = []
        for block in range(i // HD, (i + FQ) // HD):
            shard, row = tile_place(block)
            parts.append(head_ref[shard, row : row + HD, :])
        gg = jnp.concatenate(parts, axis=0).T
        gate_ref[:, at] = gate
        gg_ref[:, at] = gg
        grad_mixed = gg.astype(F32) * gate.astype(F32)
        mean = jnp.sum(total, axis=0, keepdims=True) * (1.0 / HD)
        centred = total - mean
        stats_ref[0:1, at] = mean
        stats_ref[1:2, at] = jnp.sum(centred * centred, axis=0, keepdims=True)
        stats_ref[2:3, at] = jnp.sum(grad_mixed, axis=0, keepdims=True)
        stats_ref[3:4, at] = jnp.sum(grad_mixed * centred, axis=0, keepdims=True)


def vmem():
    return pl.BlockSpec(memory_space=pltpu.VMEM)


def smem():
    return pl.BlockSpec(memory_space=pltpu.SMEM)


def forward(act, at_head):
    length = HD * 2 * NZ * NX
    return pl.pallas_call(
        forward_kernel,
        in_specs=[vmem()] * 2,
        out_specs=[vmem()] * 5,
        out_shape=(
            jax.ShapeDtypeStruct((HD, length), F32),
            jax.ShapeDtypeStruct((HD, length), BF16),
            jax.ShapeDtypeStruct((HD, length), BF16),
            jax.ShapeDtypeStruct((4, length), F32),
            jax.ShapeDtypeStruct((1, length), jnp.int32),
        ),
        compiler_params=params(LIMIT),
        cost_estimate=pl.CostEstimate(
            flops=8 * HD * length * length, bytes_accessed=6 << 20, transcendentals=length * length // 2
        ),
        name="attention_forward",
    )(act, at_head)


def backward_kernel(own_ref, one_ref, three_ref, two_ref, act_ref, att_ref, gate_ref, gg_ref, start_ref, slope_hbm, back_ref, dk_ref, dv_ref, slope_ref, sem):
    length = att_ref.shape[1]
    width = H * HD
    copy = pltpu.make_async_copy(slope_hbm, slope_ref, sem)
    copy.start()
    heads = [ref[k] for ref in (own_ref, one_ref, three_ref, two_ref) for k in range(NX)]
    mean_all = sum(a[0:1] for a in heads) * (1.0 / H)
    apart = [a[0:1] - mean_all for a in heads]
    spread = sum(a[1:2] for a in heads) + HD * sum(d * d for d in apart)
    inverse_all = lax.rsqrt(spread * (1.0 / width) + EPS)
    first_all = sum(a[2:3] for a in heads) * (1.0 / width)
    second_all = inverse_all * sum(a[3:4] + d * a[2:3] for a, d in zip(heads, apart)) * (1.0 / width)

    keys = [time_rows(act_ref, j, BK, 3) for j in range(0, length, BK)]
    keys_t = [k.T for k in keys]
    values = [time_rows(act_ref, j, BK, 1) for j in range(0, length, BK)]
    queries_in, seen = tiles(length, BQ, BK)

    def put(first, column, value):
        value = value.astype(BF16)
        for k in range(value.shape[0] // HD):
            shard, row = tile_place(first // HD + k)
            back_ref[shard, row : row + HD, column * HD : (column + 1) * HD] = value[
                k * HD : (k + 1) * HD
            ]

    def put_grad(first, column, value):
        put(first, column, value * time_rows(slope_ref, first, value.shape[0], column))

    started = set()
    for i, keys_in in queries_in:
        at = slice(i, i + BQ)
        gate = gate_ref[:, at].astype(F32)
        gg = gg_ref[:, at].astype(F32)
        inverse = inverse_all[:, at]
        mixed = (att_ref[:, at] - mean_all[:, at]) * inverse
        grad_att = inverse * (gg * gate - first_all[:, at] - mixed * second_all[:, at])
        grad_out_t = grad_att.astype(BF16)
        grad_out = grad_out_t.T
        queries = time_rows(act_ref, i, BQ, 2)
        start = start_ref[:, at]
        total = None
        for j in keys_in:
            here = slice(j, j + BK)
            half = dot_nt(keys[j // BK], queries) * (0.5 * SCALE)
            half = jnp.where(seen(i, j, start), half, UNSEEN)
            tanh = jnp.tanh(half)
            weights = half + half * tanh
            sig = 0.5 + 0.5 * tanh
            slope = sig + weights * (1.0 - sig)
            ahead = dot(values[j // BK], grad_out_t)
            weights = weights.astype(BF16)
            slopes = (ahead * slope).astype(BF16)
            dv = dot(weights, grad_out)
            dk = dot(slopes, queries)
            if j in started:
                dv_ref[here, :] += dv
                dk_ref[here, :] += dk
            else:
                dv_ref[here, :] = dv
                dk_ref[here, :] = dk
                started.add(j)
            term = dot(keys_t[j // BK], slopes)
            total = term if total is None else total + term
        if i == 0:
            copy.wait()
        put(i, 4, (mixed * gate).astype(BF16).T)
        put_grad(i, 0, (gg * mixed).T)
        put_grad(i, 2, total.T * SCALE)
    for j in range(0, length, BK):
        put_grad(j, 1, dv_ref[j : j + BK, :])
        put_grad(j, 3, dk_ref[j : j + BK, :] * SCALE)


def backward(stats, act, att, gate, gg, start, slope):
    length = start.shape[1]
    shards = NZ * NX
    return pl.pallas_call(
        backward_kernel,
        in_specs=[vmem()] * 9 + [pl.BlockSpec(memory_space=pl.ANY)],
        out_specs=vmem(),
        out_shape=jax.ShapeDtypeStruct((shards, length // shards, 5 * HD), BF16),
        scratch_shapes=[pltpu.VMEM((length, HD), F32)] * 2
        + [pltpu.VMEM(slope.shape, F32), pltpu.SemaphoreType.DMA],
        compiler_params=params(LIMIT),
        cost_estimate=pl.CostEstimate(
            flops=15 * HD * length * length, bytes_accessed=10 << 20, transcendentals=length * length // 2
        ),
        name="attention_backward",
    )(*stats, act, att, gate, gg, start, slope)


def terms_in_kernel(core_ref, normed_ref, grad_ref, keep_ref, send_ref, res_ref):
    shards, rows, cols = grad_ref.shape
    res_ref[...] = dot(normed_ref[...], grad_ref[...].reshape(shards * rows, cols))
    core = core_ref[0]
    for k in range(res_ref.shape[0] // HD):
        for pair in range(NY * NXH):
            mine = pl.multiple_of(k * HD + (pair * NC + core) * 8, 8)
            other = pl.multiple_of(k * HD + (pair * NC + 1 - core) * 8, 8)
            keep_ref[pair, k * 8 : (k + 1) * 8, :] = res_ref[pl.ds(mine, 8), :]
            send_ref[pair, k * 8 : (k + 1) * 8, :] = res_ref[pl.ds(other, 8), :]


def terms_in(core, normed_t, back):
    width, length = normed_t.shape
    shards, rows, _ = back.shape
    shape = jax.ShapeDtypeStruct((NY * NXH, 64, 4 * HD), F32)
    out_spec = pl.BlockSpec((NY * NXH, 32, 4 * HD), lambda g: (0, g, 0))
    return pl.pallas_call(
        terms_in_kernel,
        grid=(2,),
        in_specs=[
            smem(),
            pl.BlockSpec((width // 2, length), lambda g: (g, 0)),
            pl.BlockSpec((shards, rows, 4 * HD), lambda g: (0, 0, 0)),
        ],
        out_specs=[out_spec] * 2,
        out_shape=[shape] * 2,
        scratch_shapes=[pltpu.VMEM((width // 2, 4 * HD), F32)],
        compiler_params=params(LIMIT),
        cost_estimate=pl.CostEstimate(
            flops=2 * width * length * 4 * HD, bytes_accessed=9 << 20, transcendentals=0
        ),
        name="terms_in",
    )(core, normed_t, back)


def terms_out_kernel(core_ref, at_ref, gated_ref, *refs):
    keep_ref, send_ref, res_ref, gated_t_ref = refs[-4:]
    shards, rows, _ = gated_ref.shape

    @pl.when(pl.program_id(0) == 0)
    def _():
        for shard in range(shards):
            gated_t_ref[:, shard * rows : (shard + 1) * rows] = gated_ref[shard].T

    total = None
    for r in range(shards):
        here = pl.ds(pl.multiple_of(at_ref[r] * rows, rows), rows)
        term = dot(gated_t_ref[:, here], refs[r][...])
        total = term if total is None else total + term
    res_ref[...] = total
    core = core_ref[0]
    for pair in range(NY * NXH):
        for out_ref, who in ((keep_ref, core), (send_ref, 1 - core)):
            out_ref[pair] = res_ref[pl.ds(pl.multiple_of((pair * NC + who) * 8, 8), 8), :]


def terms_out(core, at, back, cots):
    shards, rows, _ = back.shape
    width = cots[0].shape[1]
    length = shards * rows
    out_spec = pl.BlockSpec((NY * NXH, 8, 4 * HD), lambda g: (0, g, 0))
    return pl.pallas_call(
        terms_out_kernel,
        grid=(2,),
        in_specs=[smem(), smem(), pl.BlockSpec((shards, rows, HD), lambda g: (0, 0, 4))]
        + [pl.BlockSpec((rows, width // 2), lambda g: (0, g))] * shards,
        out_specs=[out_spec] * 2,
        out_shape=[jax.ShapeDtypeStruct((NY * NXH, 16, 4 * HD), F32)] * 2,
        scratch_shapes=[pltpu.VMEM((HD, width // 2), F32), pltpu.VMEM((HD, length), BF16)],
        compiler_params=params(LIMIT),
        cost_estimate=pl.CostEstimate(
            flops=2 * HD * width * length, bytes_accessed=6 << 20, transcendentals=0
        ),
        name="terms_out",
    )(core, at, back, *cots)


def small(kernel, name, scalars, arrays, outs, scratch=(), limit=12):
    size = sum(a.size * a.dtype.itemsize for a in arrays)
    return pl.pallas_call(
        kernel,
        in_specs=[smem()] + [vmem()] * len(arrays),
        out_specs=[vmem()] * len(outs),
        out_shape=[jax.ShapeDtypeStruct(shape, dtype) for shape, dtype in outs],
        scratch_shapes=list(scratch),
        compiler_params=params(limit),
        cost_estimate=pl.CostEstimate(flops=size, bytes_accessed=2 * size, transcendentals=0),
        name=name,
    )(scalars, *arrays)


def core_sum_kernel(pos_ref, keep_ref, got_ref, keep_out_ref, got_out_ref, own_ref, one_ref, three_ref, two_ref):
    y = pos_ref[0]
    for d, to_ref in ((0, own_ref), (1, one_ref), (3, three_ref), (2, two_ref)):
        here = pl.ds(((y - d + NY) % NY) * NXH, NXH)
        to_ref[:, :64, :] = (keep_ref[here] + got_ref[here]).astype(to_ref.dtype)
        to_ref[:, 64:, :] = (keep_out_ref[here] + got_out_ref[here]).astype(to_ref.dtype)


def y_sum_kernel(pos_ref, own_ref, a_ref, b_ref, c_ref, keep_ref, same_ref, one_ref, two_ref, sum_ref):
    xh, x = pos_ref[1], pos_ref[2]
    sum_ref[...] = own_ref[...] + (
        a_ref[...].astype(F32) + b_ref[...].astype(F32) + c_ref[...].astype(F32)
    )

    def slab(out_ref, h, l):
        for k in range(NZ):
            out_ref[k * 8 : (k + 1) * 8, :] = sum_ref[
                h, pl.ds(pl.multiple_of((k * NX + l) * 8, 8), 8), :
            ]

    slab(keep_ref, xh, x)
    keep_ref[32:, :] = sum_ref[xh, 64:, :]
    slab(same_ref, 1 - xh, x)
    same_ref[32:, :] = sum_ref[1 - xh, 64:, :]
    slab(one_ref, xh, 1 - x)
    slab(two_ref, 1 - xh, 1 - x)


def x_sum_kernel(pos_ref, keep_ref, same_ref, a_ref, b_ref, own_ref, one_ref, three_ref, two_ref, out_ref, sum_ref):
    z, x = pos_ref[3], pos_ref[2]
    mine = keep_ref[...] + same_ref[...]
    sum_ref[x] = mine[:32]
    sum_ref[1 - x] = a_ref[...] + b_ref[...]
    out_ref[...] = mine[32:]
    for d, to_ref in ((0, own_ref), (1, one_ref), (3, three_ref), (2, two_ref)):
        here = pl.ds(pl.multiple_of(((z - d + NZ) % NZ) * 8, 8), 8)
        for l in range(NX):
            to_ref[l * 8 : (l + 1) * 8, :] = sum_ref[l, here, :]


def z_place_kernel(factor, pos_ref, own_ref, one_ref, three_ref, two_ref, out_ref, w_in_ref, w_out_ref):
    z = pos_ref[3]
    for d, ref in ((0, own_ref), (1, one_ref), (3, three_ref), (2, two_ref)):
        for l in range(NX):
            for k in range(4):
                at = pl.multiple_of((k * H + ((z + d) % NZ) * NX + l) * HD, HD)
                w_in_ref[:, pl.ds(at, HD)] = (
                    ref[l * 8 : (l + 1) * 8, k * HD : (k + 1) * HD] * factor
                )
    w_out_ref[:, : 4 * HD] = out_ref[:8] * factor
    w_out_ref[:, 4 * HD :] = out_ref[8:] * factor


def columns(ref):
    return jnp.concatenate([ref[h] for h in range(H)], axis=1)


def shard_out_kernel(gated_ref, grad_ref, w_in_ref, w_out_ref, hist_ref, layer_ref, acc_ref):
    term = dot_nt(columns(grad_ref), w_in_ref[...])

    @pl.when(pl.program_id(0) == 0)
    def _():
        hist = hist_ref[...].astype(F32)
        layer_ref[...] = (hist + dot(columns(gated_ref), w_out_ref[...])).astype(BF16)
        acc_ref[...] = term

    @pl.when(pl.program_id(0) > 0)
    def _():
        acc_ref[...] += term


def shard_grad_kernel(grad_ref, w_in_ref, hist_ref, cot_ref, half_ref, grad_hist_ref, acc_ref):
    term = dot_nt(columns(grad_ref), w_in_ref[...])

    @pl.when(pl.program_id(0) == 0)
    def _():
        acc_ref[...] = half_ref[...] + term

    @pl.when(pl.program_id(0) > 0)
    def _():
        normed, inverse = layer_norm(hist_ref[...].astype(F32))
        grad = norm_back(normed, inverse, acc_ref[...] + term)
        grad_hist_ref[...] = (cot_ref[...].astype(F32) + grad).astype(BF16)


def shard_out(back, w_in, w_out, hist):
    rows, width = hist.shape
    whole = lambda a: pl.BlockSpec(a.shape, lambda k: (0,) * a.ndim)
    return pl.pallas_call(
        shard_out_kernel,
        grid=(2,),
        in_specs=[
            pl.BlockSpec((H, rows, HD), lambda k: (0, 0, 4)),
            pl.BlockSpec((H, rows, HD), lambda k: (0, 0, k)),
            pl.BlockSpec((width, width), lambda k: (0, k)),
            whole(w_out),
            whole(hist),
        ],
        out_specs=[whole(hist)] * 2,
        out_shape=[jax.ShapeDtypeStruct(hist.shape, BF16), jax.ShapeDtypeStruct(hist.shape, F32)],
        compiler_params=params(LIMIT),
        cost_estimate=pl.CostEstimate(
            flops=6 * rows * width * width, bytes_accessed=8 << 20, transcendentals=0
        ),
        name="shard_out",
    )(back, back, w_in, w_out, hist)


def shard_grad(back, w_in, hist, cot, half):
    rows, width = hist.shape
    whole = lambda a: pl.BlockSpec(a.shape, lambda k: (0,) * a.ndim)
    return pl.pallas_call(
        shard_grad_kernel,
        grid=(2,),
        in_specs=[
            pl.BlockSpec((H, rows, HD), lambda k: (0, 0, 2 + k)),
            pl.BlockSpec((width, width), lambda k: (0, 2 + k)),
            whole(hist),
            whole(cot),
            whole(half),
        ],
        out_specs=whole(hist),
        out_shape=jax.ShapeDtypeStruct(hist.shape, BF16),
        scratch_shapes=[pltpu.VMEM((rows, width), F32)],
        compiler_params=params(LIMIT),
        cost_estimate=pl.CostEstimate(
            flops=4 * rows * width * width, bytes_accessed=8 << 20, transcendentals=0
        ),
        name="shard_grad",
    )(back, w_in, hist, cot, half)


def local(history, segment_ids, w_in, w_out, cotangent):
    hist = history[0]
    cot = cotangent[0]
    rows, width = hist.shape
    length = rows * NZ * NX
    s = lax.axis_index("seq")
    u = lax.axis_index("user")
    z, x = s // NX, s % NX
    y, xh, core = u // (NXH * NC), (u // NC) % NXH, u % NC

    users = NY * NXH * NC
    tie = lax.optimization_barrier
    w_head = jnp.concatenate(
        [lax.dynamic_slice(w_in, (0, i * width + s * HD), (width, HD)) for i in range(4)], axis=1
    )

    def place_of(key):
        return ((z + key[0]) % NZ) * NX + (x ^ key[1])

    at_core = core.reshape(1)
    at = jnp.stack([y, xh, x, z])
    orders = (
        ((0, 0),),
        ((0, 1), (1, 0), (3, 0)),
        ((1, 1), (2, 0), (3, 1)),
        ((2, 1),),
        ((1, 0), (3, 0), (0, 1), (2, 0), (2, 1), (1, 1), (3, 1), (0, 0)),
    )
    places = {keys: jnp.stack([place_of(key) for key in keys]) for keys in orders}

    def project(got, outs):
        keys = tuple(sorted(got))
        return ln_proj(places[keys], [got[key] for key in keys], w_head, outs)

    got = {
        (1, 0): from_seq(hist, 1, 0),
        (3, 0): from_seq(hist, 3, 0),
        (0, 1): from_seq(hist, 0, 1),
    }
    outs = project({(0, 0): hist}, ())
    grad_gated_own = dot_nt(cot, w_out).astype(BF16).reshape(rows, H, HD).transpose(1, 0, 2)
    got, outs, grad_gated_own, waiting, at_core, at = tie(
        (got, outs, grad_gated_own, tuple(places.values()), at_core, at)
    )
    places = dict(zip(orders, waiting))
    ids = segment_ids[0].astype(BF16).reshape(2, HD)
    ids = jnp.pad(ids, ((0, 14), (0, 0)))
    to_heads = jnp.concatenate(
        [
            grad_gated_own,
            jnp.broadcast_to(ids[None], (H, 16, HD)),
        ],
        axis=1,
    )
    at_head = lax.all_to_all(to_heads, "seq", 0, 0, tiled=True)
    more = {
        (2, 0): from_seq(got[1, 0], 1, 0),
        (3, 1): from_seq(got[0, 1], 3, 0),
        (1, 1): from_seq(got[1, 0], 0, 1),
    }
    outs = project(got, outs)
    more, outs, cot_next = tie((more, outs, cot))
    last = {(2, 1): from_seq(more[2, 0], 0, 1)}
    cots = {(1, 0): from_seq(cot_next, 1, 0), (3, 0): from_seq(cot_next, 3, 0)}
    outs, at_head = tie((outs, at_head))
    outs = project(more, outs)
    last, cots, outs = tie((last, cots, outs))
    fresh = {(0, 1): from_seq(cot_next, 0, 1), (2, 0): from_seq(cots[1, 0], 1, 0)}
    normed_t, act, slope = project(last, outs)
    att, gate_t, gg_t, stats, start = forward(act, at_head)
    stats, fresh = tie((stats, fresh))
    cots.update(fresh)
    pair = jnp.stack([stats, from_seq(stats, 0, 1)])
    others = [from_seq(pair, dz, 0) for dz in (1, 3, 2)]
    pair, others, cots = tie((pair, others, cots))
    fresh = {
        (2, 1): from_seq(cots[2, 0], 0, 1),
        (1, 1): from_seq(cots[0, 1], 1, 0),
        (3, 1): from_seq(cots[0, 1], 3, 0),
    }
    back = backward([pair, *others], act, att, gate_t, gg_t, start, slope)
    back, fresh = tie((back, fresh))
    cots.update(fresh)
    cots[0, 0] = cot
    back_tok = lax.all_to_all(back, "seq", 0, 0, tiled=True)

    keep, send = terms_in(at_core, normed_t, back)
    got = from_user(send, 0, 0, 1)
    keep_out, send_out = terms_out(at_core, places[orders[4]], back, [cots[key] for key in orders[4]])
    got_out = from_user(send_out, 0, 0, 1)
    n = 4 * HD
    own, *sends = small(
        core_sum_kernel,
        "core_sum",
        at,
        [keep, got, keep_out, got_out],
        [((NXH, 80, n), F32)] + [((NXH, 80, n), BF16)] * 3,
        limit=32,
    )
    own, sends = tie((own, sends))
    sends = [from_user(a, d, 0, 0) for a, d in zip(sends, (1, 3, 2))]
    layer_out, half = shard_out(back_tok, w_in, w_out, hist)
    sends, layer_out, half = tie((sends, layer_out, half))
    keep, same, one, two = small(
        y_sum_kernel,
        "y_sum",
        at,
        [own, *sends],
        [((48, n), F32)] * 2 + [((32, n), F32)] * 2,
        [pltpu.VMEM((NXH, 80, n), F32)],
    )
    same = from_both(same, 1, 0)
    one = from_both(one, 0, 1)
    two = from_both(two, 1, 1)
    grad_history = shard_grad(back_tok, w_in, hist, cot, half)
    same, one, two, grad_history = tie((same, one, two, grad_history))
    own, *sends, own_out = small(
        x_sum_kernel,
        "x_sum",
        at,
        [keep, same, one, two],
        [((16, n), F32)] * 5,
        [pltpu.VMEM((NX, 32, n), F32)],
    )
    sends = [from_seq(a, d, 0) for a, d in zip(sends, (1, 3, 2))]
    factor = (length * users) ** (-0.5)
    grad_w_in, grad_w_out = small(
        functools.partial(z_place_kernel, factor),
        "z_place",
        at,
        [own, *sends, own_out],
        [((8, 4 * width), F32), ((8, width), F32)],
    )
    return layer_out[None], grad_history[None], grad_w_in, grad_w_out


def solution(mesh):
    in_specs = (P("user", "seq", None), P("user", "seq"), P(), P(), P("user", "seq", None))
    out_specs = (
        P("user", "seq", None),
        P("user", "seq", None),
        P(("seq", "user"), None),
        P(("seq", "user"), None),
    )
    return jax.shard_map(local, mesh=mesh, in_specs=in_specs, out_specs=out_specs, check_vma=False)
```
